256 devices in a mesh: tile: 64 (over z, y, core), group: 4 (over x).
Axes of the slice: x: 4, y: 4, z: 8, core: 2. Of those that a mesh axis runs over, the one named last changes fastest.
Arguments:
- features: bfloat16 [64, 8, 96, 16, 128], P('tile', 'group'), may hold values from -6 to 6
- tile_list: int32 [64], replicated, may hold values from 0 to 63, as said below
- neighbours: int32 [64, 8], replicated, may hold values from -1 to 63, as said below
- clip_frames: int32 [16], replicated, may hold values from 1 to 8, as said below
- gain_one: float32 [96], replicated, may hold values from 0.1 to 1.9
- weight_one: bfloat16 [3, 3, 3, 96, 96], replicated, may hold values from -0.125 to 0.125
- bias_one: float32 [96], replicated, may hold values from -3 to 3
- gain_two: float32 [96], replicated, may hold values from 0.1 to 1.9
- weight_two: bfloat16 [3, 3, 3, 96, 96], replicated, may hold values from -0.125 to 0.125
- bias_two: float32 [96], replicated, may hold values from -3 to 3
Outputs:
- decoded: bfloat16 [64, 8, 96, 16, 128], P('tile', 'group')
The draws below stay inside these ranges and needn't reach their ends.
Inputs may be any that keep to these rules, and one draw needn't show every extreme that they name: `tile_list`: each tile number appears once. Tiles of clip k are numbers k * 4 to (k + 1) * 4 - 1, laid on a 2 x 2 grid in an order drawn from the seed; the table lists each tile's grid neighbours within its clip and -1 past the clip's border. `clip_frames`: some clip has all 8 frames.
All inputs are finite; a program needn't handle non-finite values.
Results may differ from the reference program's by a relative error of at most 0.0034.
Values may be sent and summed in bfloat16 or wider, within the bound.
No kernel may reach another device: no remote copies, remote signals or barrier semaphores. Data moves between devices by JAX's collectives and lax.ppermute only.
A program may use at most 64 MiB of HBM per device.

```python
import jax
import jax.numpy as jnp
from jax import lax

C = 96
H = 16
W = 128
GH = 2
GW = 2
TPC = 4
NT = 64
NCLIP = 16
NF = 8


OFFSETS = ((-1, -1), (-1, 0), (-1, 1), (0, -1), (0, 1), (1, -1), (1, 0), (1, 1))


def draw_tile_list(key, part):
    key = jax.random.fold_in(key, 12)
    return jax.random.permutation(key, NT).astype(jnp.int32)


def draw_neighbours(key, part):
    key = jax.random.fold_in(key, 11)
    subkeys = jax.random.split(key, NCLIP)
    ordering = jax.vmap(lambda sub: jax.random.permutation(sub, TPC))(subkeys).astype(jnp.int32)
    layout = (ordering + (jnp.arange(NCLIP, dtype=jnp.int32) * TPC)[:, None]).reshape(NCLIP, GH, GW)
    framed = jnp.pad(layout, ((0, 0), (1, 1), (1, 1)), constant_values=-1)
    columns = []
    for shift_r, shift_q in OFFSETS:
        columns.append(framed[:, 1 + shift_r:1 + shift_r + GH, 1 + shift_q:1 + shift_q + GW].reshape(-1))
    values = jnp.stack(columns, axis=-1)
    lookup = jnp.zeros((NT, 8), jnp.int32).at[layout.reshape(-1)].set(values)
    return lookup


def draw_clip_frames(key, part):
    key = jax.random.fold_in(key, 13)
    first_key, second_key = jax.random.split(key)
    lengths_drawn = jax.random.randint(first_key, (NCLIP,), 1, NF + 1)
    longest = jax.random.randint(second_key, (), 0, NCLIP)
    return jnp.where(jnp.arange(NCLIP) == longest, NF, lengths_drawn).astype(jnp.int32)


def level_of(own_key, shape, pieces, low, high):
    factor_of, own = 1.0, jax.random.fold_in(own_key, 6)
    for position, parts in pieces:
        heights = jnp.exp(jax.random.uniform(jax.random.fold_in(own, position), (parts,), jnp.float32, low / len(pieces), high / len(pieces)))
        factor_of = factor_of * jnp.repeat(heights, shape[position] // parts).reshape([-1 if axis == position else 1 for axis in range(len(shape))])
    return factor_of


def normal_values(stream_key, extent, deviation, reach, pieces=(), kind=jnp.bfloat16):
    loudness = level_of(stream_key, extent, pieces, -0.22, 0.18) if pieces else 1.0
    values = jax.random.normal(stream_key, extent, jnp.float32) * deviation * loudness
    return jnp.minimum(jnp.maximum(values, -reach), reach).astype(kind)


def setup_inputs(seed: int = 0) -> dict:
    key_list = jax.random.split(jax.random.key(seed), 11)
    features = normal_values(key_list[0], (NT, NF, C, H, W), 1.0, 6.0, ((0, 64), (1, 4)))
    tile_list = draw_tile_list(jax.random.fold_in(key_list[10], 71), 0)
    neighbours = draw_neighbours(jax.random.fold_in(key_list[10], 71), 0)
    clip_frames = draw_clip_frames(jax.random.fold_in(key_list[10], 71), 0)
    gain_one = jnp.clip(1.0 + 0.18 * jax.random.normal(key_list[4], (C,), jnp.float32), 0.1, 1.9)
    weight_one = normal_values(key_list[5], (3, 3, 3, C, C), (27 * C) ** -0.5, 0.125)
    bias_one = normal_values(key_list[6], (C,), 0.5, 3.0, (), jnp.float32)
    gain_two = jnp.clip(1.0 + 0.18 * jax.random.normal(key_list[7], (C,), jnp.float32), 0.1, 1.9)
    weight_two = normal_values(key_list[8], (3, 3, 3, C, C), (27 * C) ** -0.5, 0.125)
    bias_two = normal_values(key_list[9], (C,), 0.5, 3.0, (), jnp.float32)
    return {"features": features, "tile_list": tile_list, "neighbours": neighbours, "clip_frames": clip_frames, "gain_one": gain_one, "weight_one": weight_one, "bias_one": bias_one, "gain_two": gain_two, "weight_two": weight_two, "bias_two": bias_two}


OFFSETS = ((-1, -1), (-1, 0), (-1, 1), (0, -1), (0, 1), (1, -1), (1, 0), (1, 1))

def rms_silu(values, gain_vec):
    inverse = lax.rsqrt(lax.optimization_barrier(jnp.mean(values * values, axis=-3, keepdims=True)) + 1e-06)
    return jax.nn.silu(values * inverse * gain_vec[:, None, None])

def layer(active, sources, weight, bias):
    zeros_tile = jnp.zeros((1,) + active.shape[1:], active.dtype)
    extended = jnp.concatenate([active, zeros_tile], axis=0)
    weight_full = weight.astype(jnp.float32)

    def per_tile(index):
        picks = sources[index]
        beside_all = [extended[picks[which]] for which in range(8)]
        upper = jnp.concatenate([beside_all[0][..., -1:, -1:], beside_all[1][..., -1:, :], beside_all[2][..., -1:, :1]], axis=-1)
        middle = jnp.concatenate([beside_all[3][..., :, -1:], active[index], beside_all[4][..., :, :1]], axis=-1)
        lower = jnp.concatenate([beside_all[5][..., :1, -1:], beside_all[6][..., :1, :], beside_all[7][..., :1, :1]], axis=-1)
        padded = jnp.concatenate([upper, middle, lower], axis=-2).astype(jnp.float32)
        frames, channels, height, breadth = (active.shape[1], active.shape[2], active.shape[3], active.shape[4])
        padded = jnp.concatenate([jnp.zeros((2,) + padded.shape[1:], jnp.float32), padded], axis=0)
        summed = jnp.zeros((frames, weight.shape[4], height, breadth), jnp.float32)
        for step_t in range(3):
            for step_y in range(3):
                for step_x in range(3):
                    window = padded[step_t:step_t + frames, :, step_y:step_y + height, step_x:step_x + breadth]
                    summed = summed + jnp.einsum('fchw,co->fohw', window, weight_full[step_t, step_y, step_x])
        return summed
    result = lax.map(per_tile, jnp.arange(active.shape[0], dtype=jnp.int32))
    return result + bias[None, None, :, None, None]

def reference(features, tile_list, neighbours, clip_frames, gain_one, weight_one, bias_one, gain_two, weight_two, bias_two):
    total_tiles = tile_list.shape[0]
    slot_of = jnp.zeros((total_tiles,), jnp.int32).at[tile_list].set(jnp.arange(total_tiles, dtype=jnp.int32))
    around_ids = neighbours[tile_list]
    sources = jnp.where(around_ids < 0, total_tiles, slot_of[jnp.maximum(around_ids, 0)]).astype(jnp.int32)
    inputs = features.astype(jnp.float32)
    first = rms_silu(inputs, gain_one).astype(jnp.bfloat16)
    second = rms_silu(layer(first, sources, weight_one, bias_one), gain_two).astype(jnp.bfloat16)
    branch = layer(second, sources, weight_two, bias_two)
    lengths = clip_frames[tile_list // TPC]
    visible = jnp.arange(features.shape[1], dtype=jnp.int32)[None, :] < lengths[:, None]
    return jnp.where(visible[:, :, None, None, None], inputs + branch, 0.0).astype(jnp.bfloat16)
```

```python
import functools

import jax
import jax.numpy as jnp
from jax import lax
from jax.experimental import pallas as pl
from jax.experimental.pallas import tpu as pltpu
from jax.sharding import PartitionSpec as P

NZ, NY, NCORE, NX = 8, 4, 2, 4
TILES = NZ * NY * NCORE
TPC = 4
C, H, W, F = 96, 16, 128, 2
REC = 5
KF = 9 * C + 32
T_LIST = 2
T_NEAR = T_LIST + TILES
T_CLIP = T_NEAR + TILES * 8
BF, F32 = jnp.bfloat16, jnp.float32

SMEM = pl.BlockSpec(memory_space=pltpu.SMEM)
VMEM = pl.BlockSpec(memory_space=pltpu.VMEM)


def params():
    return pltpu.CompilerParams(vmem_limit_bytes=56 * 1024 * 1024)


def sides(table):
    tile = table[T_LIST + table[0]]
    up = table[T_NEAR + tile * 8 + 1] >= 0
    left = table[T_NEAR + tile * 8 + 3] >= 0
    return up, left


def norm_silu(values, gain):
    inverse = lax.rsqrt(jnp.mean(values * values, axis=0, keepdims=True) + 1e-06)
    scaled = values * inverse * gain
    return scaled / (1.0 + jnp.exp(-scaled))


def rotate(values, by):
    return pltpu.roll(values, by, 1)


def lanes(rows):
    return lax.broadcasted_iota(jnp.int32, (rows, W), 1)


def record_kernel(table, features, out):
    up, left = sides(table)
    row = jnp.where(up, 0, H - 2)
    for f in range(F):
        for r in range(2):
            out[2 * f + r] = features[f, row + r]
    source = lax.broadcasted_iota(jnp.int32, (W, W), 0)
    target = lax.broadcasted_iota(jnp.int32, (W, W), 1) % 64
    first_col = jnp.where(left, 0, W - 2)
    wanted = jnp.where(source - first_col == (target // 16) % 2, target, -1)

    def step(n, acc):
        f, y = n // H, n % H
        pick = ((wanted // 32 == f) & (wanted % 16 == y) & (wanted >= 0)).astype(F32).astype(BF)
        return acc + jnp.dot(features[f, y], pick, preferred_element_type=F32)

    out[4] = lax.fori_loop(0, F * H, step, jnp.zeros((C, W), F32)).astype(BF)


def select_kernel(table, t0, t1, t2, t3, mine, other, inverse):
    held = (t0, t1, t2, t3)
    me = table[0]
    z, y, c = me // (NY * NCORE), (me // NCORE) % NY, me % NCORE

    def invert(i, _):
        inverse[table[T_LIST + i]] = i
        return 0

    lax.fori_loop(0, TILES, invert, 0)
    mine[...] = jnp.zeros_like(mine)
    other[...] = jnp.zeros_like(other)

    def place(tile):
        slot = inverse[jnp.maximum(tile, 0)]
        zs, ys, cs = slot // (NY * NCORE), (slot // NCORE) % NY, slot % NCORE
        away = jnp.where(c == 0, z - zs, zs - z)
        away = jnp.where(away < 0, away + NZ, away)
        label = jnp.where(cs == c, 0, 1)
        fits = (tile >= 0) & (ys == y) & ((away >= 1) & (away <= 3) | (label == 0) & ((away == 0) | (away == 4)))
        which = jnp.where(fits, jnp.minimum(away, 3), -1)
        return which, jnp.where(away == 4, 2, label)

    low = lanes(C) < 64
    for same, out in ((True, mine), (False, other)):
        core = c if same else 1 - c

        def dest(yd, _):
            near = T_NEAR + table[T_LIST + z * NY * NCORE + yd * NCORE + core] * 8
            vertical = place(jnp.maximum(table[near + 1], table[near + 6]))
            horizontal = place(jnp.maximum(table[near + 3], table[near + 4]))
            diagonal = place(
                jnp.maximum(
                    jnp.maximum(table[near], table[near + 2]), jnp.maximum(table[near + 5], table[near + 7])
                )
            )
            for k, ref in enumerate(held):

                @pl.when(vertical[0] == k)
                def _():
                    out[yd, 0:4] = ref[vertical[1], 0:4]

                @pl.when(horizontal[0] == k)
                def _():
                    out[yd, 4] = jnp.where(low, ref[horizontal[1], 4], out[yd, 4])

                @pl.when(diagonal[0] == k)
                def _():
                    out[yd, 4] = jnp.where(low, out[yd, 4], ref[diagonal[1], 4])

            return 0

        lax.fori_loop(0, NY, dest, 0)


def combine_kernel(table, mine, arrived, own, one, two, three):
    y = (table[0] // NCORE) % NY
    for by, out in enumerate((own, one, two, three)):
        to = (y + by) % NY
        out[...] = (mine[to].astype(F32) + arrived[to].astype(F32)).astype(BF)


def three_shifts(center, near, yy, left):
    before = rotate(center, 1)
    after = rotate(center, W - 1)
    moved = rotate(near, jnp.where(left, (W - yy) % W, W - 1 - yy))
    lane = lanes(C)
    before = jnp.where(lane == 0, jnp.where(left, moved, 0.0), before)
    after = jnp.where(lane == W - 1, jnp.where(left, 0.0, moved), after)
    return before.astype(BF), center.astype(BF), after.astype(BF)


def both_frames(weight_ref, weights):
    weights[0:C, 0 : 3 * KF] = weight_ref[...]
    weights[0:C, 3 * KF :] = jnp.zeros((C, KF), BF)
    weights[C:, 0:KF] = jnp.zeros((C, KF), BF)
    weights[C:, KF:] = weight_ref[...]


def row_pair(windows, weights, oy):
    parts = []
    for fr in range(2 * F):
        parts.append(
            jnp.concatenate(
                [
                    windows[fr, pl.ds(oy, 3)].reshape(9 * C, W),
                    windows[fr, pl.ds(oy + 1, 3)].reshape(9 * C, W),
                ],
                axis=1,
            )
        )
        parts.append(jnp.zeros((KF - 9 * C, 2 * W), BF))
    return jnp.dot(weights[...], jnp.concatenate(parts, axis=0), preferred_element_type=F32)


def first_kernel(
    table, own, prev, halo_own, halo_prev, weight, bias, gain_one, gain_two, out, raw, windows, weights, near, edge
):
    up, left = sides(table)
    both_frames(weight, weights)
    gain1 = gain_one[...]
    zero = jnp.zeros((C, W), BF)
    for fr in range(2 * F):
        source, halo, f = (prev, halo_prev, fr) if fr < F else (own, halo_own, fr - F)
        for r in range(2):
            raw[fr, r] = jnp.where(up, halo[2 * f + r], zero)
            raw[fr, H + 2 + r] = jnp.where(up, zero, halo[2 * f + r])
        raw[fr, 2 : H + 2] = source[f]
    src = lax.broadcasted_iota(jnp.int32, (W, W), 0)
    dst = lax.broadcasted_iota(jnp.int32, (W, W), 1)
    body = jnp.where((dst >= 2) & (dst < H + 2), dst - 2, -1000)
    above = jnp.where(dst < 2, 64 + H - 2 + dst, -1000)
    below = jnp.where((dst >= H + 2) & (dst < H + 4), 64 + dst - H - 2, -1000)
    wanted = jnp.maximum(body, jnp.where(up, above, below))
    for fr in range(2 * F):
        halo, f = (halo_prev, fr) if fr < F else (halo_own, fr - F)
        for col in range(2):
            pick = (src == wanted + f * 32 + col * 16).astype(F32).astype(BF)
            values = jnp.dot(halo[4], pick, preferred_element_type=F32)
            near[fr, col] = norm_silu(values, gain1)
        edge[fr] = jnp.zeros((C, W), F32)

    lane = lanes(C)

    def row_step(n, _):
        fr, yy = n // (H + 4), n % (H + 4)
        center = norm_silu(raw[fr, yy].astype(F32), gain1)
        beside = jnp.where(left, near[fr, 1], near[fr, 0])
        before, middle, after = three_shifts(center, beside, yy, left)
        windows[fr, yy, 0:C] = before
        windows[fr, yy, C : 2 * C] = middle
        windows[fr, yy, 2 * C :] = after
        moved = rotate(center, jnp.where(left, yy, yy + 1))
        edge[fr] = jnp.where(lane == yy, moved, edge[fr])
        return 0

    lax.fori_loop(0, 2 * F * (H + 4), row_step, 0)

    bias_col, gain2 = bias[...], gain_two[...]

    def rows_step(n, _):
        acc = row_pair(windows, weights, 2 * n)
        for f in range(F):
            value = norm_silu(acc[f * C : (f + 1) * C] + bias_col, gain2)
            for r in range(2):
                oy = 2 * n + r
                inside = ((oy > 0) | up) & ((oy < H + 1) | jnp.logical_not(up))
                out[f, oy] = jnp.where(inside, value[:, r * W : (r + 1) * W], 0.0).astype(BF)
        return 0

    lax.fori_loop(0, (H + 2) // 2, rows_step, 0)

    parts = []
    for fr in range(2 * F):
        a, b, e = near[fr, 0], near[fr, 1], edge[fr]
        cols = (jnp.where(left, a, e), jnp.where(left, b, a), jnp.where(left, e, b))
        for dy in range(3):
            for col in cols:
                parts.append((rotate(col, W - dy) if dy else col).astype(BF))
        parts.append(jnp.zeros((KF - 9 * C, W), BF))
    acc = jnp.dot(weights[...], jnp.concatenate(parts, axis=0), preferred_element_type=F32)
    inside = ((lane > 0) | up) & ((lane < H + 1) | jnp.logical_not(up)) & (lane < H + 2)
    for f in range(F):
        value = norm_silu(acc[f * C : (f + 1) * C] + bias_col, gain2)
        out[f, H + 2] = jnp.where(inside, value, 0.0).astype(BF)


def second_kernel(table, own, prev, features, weight, bias, out, windows, weights):
    _, left = sides(table)
    both_frames(weight, weights)

    def row_step(n, _):
        fr, yy = n // (H + 2), n % (H + 2)
        for source, base in ((prev, 0), (own, F)):

            @pl.when((fr >= base) & (fr < base + F))
            def _():
                f = fr - base
                before, middle, after = three_shifts(
                    source[f, yy].astype(F32), source[f, H + 2].astype(F32), yy, left
                )
                windows[fr, yy, 0:C] = before
                windows[fr, yy, C : 2 * C] = middle
                windows[fr, yy, 2 * C :] = after

        return 0

    lax.fori_loop(0, 2 * F * (H + 2), row_step, 0)
    tile = table[T_LIST + table[0]]
    length = table[T_CLIP + tile // TPC]
    start = table[1] * F
    bias_col = bias[...]

    def rows_step(n, _):
        acc = row_pair(windows, weights, 2 * n)
        for f in range(F):
            value = acc[f * C : (f + 1) * C] + bias_col
            for r in range(2):
                y = 2 * n + r
                total = features[f, y].astype(F32) + value[:, r * W : (r + 1) * W]
                out[f, y] = jnp.where(start + f < length, total, 0.0).astype(BF)
        return 0

    lax.fori_loop(0, H // 2, rows_step, 0)


def call(kernel, outs, kinds, scratch=()):
    single = not isinstance(outs, (list, tuple))
    return pl.pallas_call(
        kernel,
        out_shape=outs,
        in_specs=[SMEM if kind == "s" else VMEM for kind in kinds],
        out_specs=VMEM if single else [VMEM] * len(outs),
        scratch_shapes=list(scratch),
        compiler_params=params(),
    )


def shape(*extent):
    return jax.ShapeDtypeStruct(extent, BF)


def place_of(z, y, c):
    return (z % NZ) * NY * NCORE + (y % NY) * NCORE + c


def pairs(move):
    return [
        (place_of(z, y, c), place_of(*move(z, y, c))) for z in range(NZ) for y in range(NY) for c in range(NCORE)
    ]


def send(array, move):
    return lax.ppermute(array, "tile", pairs(move))


def later(array):
    return lax.ppermute(array, "group", [(i, i + 1) for i in range(NX - 1)])


def exchange(table, record):
    swap = lambda z, y, c: (z, y, 1 - c)
    along = lambda by: lambda z, y, c: (z + (by if c == 0 else -by), y, c)
    t0 = jnp.stack([record, send(record, swap)])
    t1 = send(t0, along(1))
    t2 = send(t0, along(2))
    t3 = send(jnp.concatenate([t1, t2[:1]], axis=0), along(2))
    mine, other = call(
        select_kernel, [shape(NY, REC, C, W)] * 2, "svvvv", [pltpu.SMEM((TILES,), jnp.int32)]
    )(table, t0, t1, t2, t3)
    arrived = send(other, swap)
    own, one, two, three = call(combine_kernel, [shape(REC, C, W)] * 4, "svv")(table, mine, arrived)
    total = own.astype(F32)
    for by, part in ((2, two), (1, one), (3, three)):
        total = total + send(part, lambda z, y, c, by=by: (z, y + by, c)).astype(F32)
    return total.astype(BF)


def deep(weight):
    flat = weight.reshape(3, 9 * C, C).transpose(2, 0, 1)
    return jnp.pad(flat, ((0, 0), (0, 0), (0, KF - 9 * C))).reshape(C, 3 * KF)


def per_device(
    features, tile_list, neighbours, clip_frames, gain_one, weight_one, bias_one, gain_two, weight_two, bias_two
):
    table = jnp.concatenate(
        [
            jnp.stack([lax.axis_index("tile"), lax.axis_index("group")]).astype(jnp.int32),
            tile_list,
            neighbours.reshape(-1),
            clip_frames,
        ]
    )
    own = features[0].transpose(0, 2, 1, 3)
    record = call(record_kernel, shape(REC, C, W), "sv")(table, own)
    prev = later(own)
    halo = exchange(table, record)
    halo_prev = later(halo)
    second = call(
        first_kernel,
        shape(F, H + 3, C, W),
        "svvvvvvvv",
        [
            pltpu.VMEM((2 * F, H + 4, C, W), BF),
            pltpu.VMEM((2 * F, H + 4, 3 * C, W), BF),
            pltpu.VMEM((2 * C, 4 * KF), BF),
            pltpu.VMEM((2 * F, 2, C, W), F32),
            pltpu.VMEM((2 * F, C, W), F32),
        ],
    )(
        table,
        own,
        prev,
        halo,
        halo_prev,
        deep(weight_one),
        bias_one[:, None],
        gain_one[:, None],
        gain_two[:, None],
    )
    second_prev = later(second)
    out = call(
        second_kernel,
        shape(F, H, C, W),
        "svvvvv",
        [pltpu.VMEM((2 * F, H + 2, 3 * C, W), BF), pltpu.VMEM((2 * C, 4 * KF), BF)],
    )(table, second, second_prev, own, deep(weight_two), bias_two[:, None])
    return out.transpose(0, 2, 1, 3)[None]


def solution(mesh):
    placed = (P("tile", "group", None, None, None), P(), P(), P(), P(), P(), P(), P(), P(), P())
    return jax.shard_map(
        per_device,
        mesh=mesh,
        in_specs=placed,
        out_specs=P("tile", "group", None, None, None),
        check_vma=False,
    )
```

```python
import functools

import jax
import jax.numpy as jnp
from jax import lax
from jax.experimental import pallas as pl
from jax.experimental.pallas import tpu as pltpu
from jax.sharding import PartitionSpec as P

NZ, NY, NCORE, NX = 8, 4, 2, 4
TILES = NZ * NY * NCORE
TPC = 4
C, H, W, F = 96, 16, 128, 2
REC = 5
KF = 9 * C + 32
T_LIST = 2
T_NEAR = T_LIST + TILES
T_CLIP = T_NEAR + TILES * 8
BF, F32 = jnp.bfloat16, jnp.float32

SMEM = pl.BlockSpec(memory_space=pltpu.SMEM)
VMEM = pl.BlockSpec(memory_space=pltpu.VMEM)
ANY = pl.BlockSpec(memory_space=pl.ANY)


def params(mib):
    return pltpu.CompilerParams(vmem_limit_bytes=mib * 1024 * 1024)


def sides(table):
    tile = table[T_LIST + table[0]]
    up = table[T_NEAR + tile * 8 + 1] >= 0
    left = table[T_NEAR + tile * 8 + 3] >= 0
    return up, left


def norm_silu(values, gain):
    inverse = lax.rsqrt(jnp.mean(values * values, axis=0, keepdims=True) + 1e-06)
    scaled = values * inverse * gain
    return scaled / (1.0 + jnp.exp(-scaled))


def rotate(values, by):
    return pltpu.roll(values, by, 1)


def lanes(rows):
    return lax.broadcasted_iota(jnp.int32, (rows, W), 1)


def write_record(features, up, left, out, base):
    row = jnp.where(up, 0, H - 2)
    for f in range(F):
        for r in range(2):
            out[base + 2 * f + r] = features[f, row + r]
    turn = jnp.where(left, 0, 2)
    lane = lanes(C)
    columns = jnp.zeros((C, W), F32)
    for f in range(F):
        for y in range(H):
            at = f * 32 + 2 * y
            moved = rotate(features[f, y].astype(F32), at + turn)
            columns = jnp.where(lane // 2 == at // 2, moved, columns)
    out[base + 4] = jnp.where(lane < 64, columns, rotate(columns, 64)).astype(BF)


def record_kernel(table, features, out):
    up, left = sides(table)
    write_record(features, up, left, out, 0)


def weights_kernel(one, two, out):
    same = lax.broadcasted_iota(jnp.int32, (C, C), 0) == lax.broadcasted_iota(jnp.int32, (C, C), 1)
    same = same.astype(F32).astype(BF)
    for n, source in enumerate((one, two)):
        out[n, 0:C, 3 * KF :] = jnp.zeros((C, KF), BF)
        out[n, C:, 0:KF] = jnp.zeros((C, KF), BF)
        for t in range(3):
            flipped = lax.dot_general(same, source[t], (((1,), (1,)), ((), ())), preferred_element_type=F32)
            flipped = jnp.concatenate([flipped.astype(BF), jnp.zeros((C, KF - 9 * C), BF)], axis=1)
            out[n, 0:C, t * KF : (t + 1) * KF] = flipped
            out[n, C:, (t + 1) * KF : (t + 2) * KF] = flipped


def select_kernel(table, t0, t1, t2, t3, _, mine, other, inverse):
    held = (t0, t1, t2, t3)
    me = table[0]
    z, y, c = me // (NY * NCORE), (me // NCORE) % NY, me % NCORE

    def invert(i, _):
        inverse[table[T_LIST + i]] = i
        return 0

    lax.fori_loop(0, TILES, invert, 0)
    mine[...] = jnp.zeros_like(mine)
    other[...] = jnp.zeros_like(other)

    def place(tile):
        slot = inverse[jnp.maximum(tile, 0)]
        zs, ys, cs = slot // (NY * NCORE), (slot // NCORE) % NY, slot % NCORE
        away = jnp.where(c == 0, z - zs, zs - z)
        away = jnp.where(away < 0, away + NZ, away)
        label = jnp.where(cs == c, 0, 1)
        fits = (tile >= 0) & (ys == y) & ((away >= 1) & (away <= 3) | (label == 0) & ((away == 0) | (away == 4)))
        which = jnp.where(fits, jnp.minimum(away, 3), -1)
        return which, jnp.where(away == 4, 2, label)

    low = lanes(C) < 64
    for same, out in ((True, mine), (False, other)):
        core = c if same else 1 - c

        def dest(yd, _):
            near = T_NEAR + table[T_LIST + z * NY * NCORE + yd * NCORE + core] * 8
            vertical = place(jnp.maximum(table[near + 1], table[near + 6]))
            horizontal = place(jnp.maximum(table[near + 3], table[near + 4]))
            diagonal = place(
                jnp.maximum(
                    jnp.maximum(table[near], table[near + 2]), jnp.maximum(table[near + 5], table[near + 7])
                )
            )
            for k, ref in enumerate(held):

                @pl.when(vertical[0] == k)
                def _():
                    out[yd, 0:4] = ref[vertical[1], 0:4]

                @pl.when(horizontal[0] == k)
                def _():
                    out[yd, 4] = jnp.where(low, ref[horizontal[1], 4], out[yd, 4])

                @pl.when(diagonal[0] == k)
                def _():
                    out[yd, 4] = jnp.where(low, out[yd, 4], ref[diagonal[1], 4])

            return 0

        lax.fori_loop(0, NY, dest, 0)


def combine_kernel(table, mine, arrived, own, one, two, three):
    y = (table[0] // NCORE) % NY
    for by, out in enumerate((own, one, two, three)):
        to = (y + by) % NY
        out[...] = (mine[to].astype(F32) + arrived[to].astype(F32)).astype(BF)


def three_shifts(center, at_left, at_right):
    lane = lanes(C)
    before = jnp.where(lane == 0, at_left, rotate(center, 1))
    after = jnp.where(lane == W - 1, at_right, rotate(center, W - 1))
    return before.astype(BF), center.astype(BF), after.astype(BF)


def put_window(windows, place, values):
    for k, value in enumerate(values):
        windows[(*place, slice(k * C, (k + 1) * C))] = value


def stack(parts):
    full = []
    for part in parts:
        full += [part, jnp.zeros((KF - 9 * C, part.shape[1]), BF)]
    return jnp.concatenate(full, axis=0)


def row_parts(windows, base, oy, count):
    return [
        jnp.concatenate([windows[base + fr, pl.ds(oy + r, 3)].reshape(9 * C, W) for r in range(count)], axis=1)
        for fr in range(2 * F)
    ]


def product(weights, parts):
    return jnp.dot(weights[...], stack(parts), preferred_element_type=F32)


def inner_first_kernel(table, own, prev, weights, vectors, _, out, windows):
    up, left = sides(table)
    bias, gain_one, gain_two = vectors[:, 0:1], vectors[:, 1:2], vectors[:, 2:3]
    write_record(prev, up, left, out, F * H)
    zero_ends(windows)
    for fr in range(2 * F):
        source, f = (prev, fr) if fr < F else (own, fr - F)

        def row_step(y, _):
            center = norm_silu(source[f, y].astype(F32), gain_one)
            put_window(windows, (fr, y + 1), three_shifts(center, 0.0, 0.0))
            return 0

        lax.fori_loop(0, H, row_step, 0, unroll=4)

    border_row, border_lane = jnp.where(up, 0, H - 1), jnp.where(left, 0, W - 1)
    lane = lanes(C)

    def rows_step(n, _):
        acc = product(weights.at[0], row_parts(windows, 0, 2 * n, 2))
        for f in range(F):
            value = norm_silu(acc[f * C : (f + 1) * C] + bias, gain_two)
            for r in range(2):
                y = 2 * n + r
                border = (lane == border_lane) | (y == border_row)
                out[f * H + y] = jnp.where(border, 0.0, value[:, r * W : (r + 1) * W]).astype(BF)
        return 0

    lax.fori_loop(0, H // 2, rows_step, 0)


def inner_second_kernel(own, second_own, second_prev, weights, vectors, _, out, windows):
    bias = vectors[:, 3:4]
    zero_ends(windows)
    for fr in range(2 * F):
        source, f = (second_prev, fr) if fr < F else (second_own, fr - F)

        def row_step(y, _):
            center = source[f * H + y].astype(F32)
            put_window(windows, (fr, y + 1), three_shifts(center, 0.0, 0.0))
            return 0

        lax.fori_loop(0, H, row_step, 0, unroll=4)

    def rows_step(n, _):
        acc = product(weights.at[1], row_parts(windows, 0, 2 * n, 2))
        for f in range(F):
            value = acc[f * C : (f + 1) * C] + bias
            for r in range(2):
                y = 2 * n + r
                out[f, y] = own[f, y].astype(F32) + value[:, r * W : (r + 1) * W]
        return 0

    lax.fori_loop(0, H // 2, rows_step, 0)


def zero_ends(windows):
    for fr in range(2 * F):
        for yy in (0, H + 1):
            windows[fr, yy] = jnp.zeros((3 * C, W), BF)


def band_parts(band, columns, base):
    parts = row_parts(band, base, 0, 2)
    for fr in range(2 * F):
        beside = [
            jnp.concatenate([columns[base + fr, j + dx, dy] for dy in range(3) for dx in range(3)], axis=0)
            for j in range(2)
        ]
        parts[fr] = jnp.concatenate([parts[fr]] + beside, axis=1)
    return parts


def put_column(columns, fr, k, value):
    columns[fr, k, 0] = rotate(value, 1).astype(BF)
    columns[fr, k, 1] = value.astype(BF)
    columns[fr, k, 2] = rotate(value, W - 1).astype(BF)


def outer_kernel(
    table, inner, record0, second_own, second_prev, halo0, halo1, halo2, weights, vectors,
    out, band1, columns1, band2, columns2
):
    up, left = sides(table)
    bias1, gain1, gain2 = vectors[:, 0:1], vectors[:, 1:2], vectors[:, 2:3]
    sources = ((second_prev, F * H, halo2), (second_own, F * H, halo1), (record0, 0, halo0))
    lane = lanes(C)

    src = lax.broadcasted_iota(jnp.int32, (W, 2 * W), 0)
    dst2 = lax.broadcasted_iota(jnp.int32, (W, 2 * W), 1)
    dst, col = dst2 % W, dst2 // W
    none = -1000
    body = jnp.where((dst >= 2) & (dst < H + 2), 2 * (dst - 2), none)
    above = jnp.where(dst < 2, 64 + 2 * (H - 2 + dst), none)
    below = jnp.where((dst >= H + 2) & (dst < H + 4), 64 + 2 * (dst - H - 2), none)
    corner = jnp.where(up, above, below)
    past = jnp.where(up, 0, H + 2)
    first_col = jnp.where(left, 0, W - 2)
    for fr in range(3 * F):
        f = fr % F
        record, base, halo = sources[fr // F]
        pick = (src == jnp.maximum(body, corner) + f * 32 + col).astype(F32).astype(BF)
        theirs = norm_silu(jnp.dot(halo[4], pick, preferred_element_type=F32), gain1)
        picks = [(src == body + f * 32 + col).astype(F32).astype(BF)]
        for r in range(2):
            picks.append(((src == first_col + col) & (dst == past + r)).astype(F32).astype(BF))
        mine = jnp.concatenate([record[base + 4], halo[2 * f], halo[2 * f + 1]], axis=1)
        ours = norm_silu(jnp.dot(mine, jnp.concatenate(picks, axis=0), preferred_element_type=F32), gain1)
        low, high = jnp.where(left, theirs, ours), jnp.where(left, ours, theirs)
        for k in range(4):
            put_column(columns1, fr, k, (low if k < 2 else high)[:, (k % 2) * W : (k % 2 + 1) * W])
        near = jnp.where(left, theirs[:, W:], theirs[:, :W])
        for r in range(4):
            other, self = halo[2 * f + r % 2], record[base + 2 * f + r % 2]
            raw = jnp.where(up, other if r < 2 else self, self if r < 2 else other)
            at = jnp.where(up, r, H + r)
            moved = rotate(near, jnp.where(left, (W - at) % W, W - 1 - at))
            center = norm_silu(raw.astype(F32), gain1)
            put_window(
                band1, (fr, r), three_shifts(center, jnp.where(left, moved, 0.0), jnp.where(left, 0.0, moved))
            )

    inside = (lane >= jnp.where(up, 3, 2)) & (lane < jnp.where(up, H + 2, H + 1))
    row_at, col_at = jnp.where(up, 0, 2), jnp.where(left, 0, 2)
    for p in range(2):
        acc = product(weights.at[0], band_parts(band1, columns1, F * p))
        for f in range(F):
            s = F * p + f
            value = norm_silu(acc[f * C : (f + 1) * C] + bias1, gain2)
            if p == 0:
                value = jnp.where(table[1] > 0, value, 0.0)
            beside = [value[:, 2 * W : 3 * W], value[:, 3 * W :]]
            near = jnp.where(left, beside[0], beside[1])
            for j in range(2):
                at = jnp.where(up, 1 + j, H + 1 + j)
                moved = rotate(near, jnp.where(left, W - at, W - 1 - at))
                center = value[:, j * W : (j + 1) * W]
                put_window(
                    band2,
                    (s, row_at + j),
                    three_shifts(center, jnp.where(left, moved, 0.0), jnp.where(left, 0.0, moved)),
                )
                band2[s, 2 - row_at + j] = jnp.zeros((3 * C, W), BF)
                put_column(columns2, s, col_at + j, jnp.where(inside, beside[j], 0.0))
                columns2[s, 2 - col_at + j] = jnp.zeros((3, C, W), BF)

    length = table[T_CLIP + table[T_LIST + table[0]] // TPC]
    start = table[1] * F
    acc = product(weights.at[1], band_parts(band2, columns2, 0))
    for f in range(F):
        value = acc[f * C : (f + 1) * C]
        for y in range(H):
            total = inner[f, y]
            for j in range(2):
                at = first_col + j
                moved = rotate(value[:, (2 + j) * W : (3 + j) * W], (at + W - 2 - y) % W)
                total = total + jnp.where(lane == at, moved, 0.0)
            if y < 2:
                total = total + jnp.where(up, value[:, y * W : (y + 1) * W], 0.0)
            if y >= H - 2:
                j = y - (H - 2)
                total = total + jnp.where(up, 0.0, value[:, j * W : (j + 1) * W])
            out[f, y] = jnp.where(start + f < length, total, 0.0).astype(BF)


def call(kernel, outs, kinds, scratch=(), mib=8, flops=0):
    single = not isinstance(outs, (list, tuple))
    return pl.pallas_call(
        kernel,
        out_shape=outs,
        in_specs=[{"s": SMEM, "v": VMEM, "-": ANY}[kind] for kind in kinds],
        out_specs=VMEM if single else [VMEM] * len(outs),
        scratch_shapes=list(scratch),
        compiler_params=params(mib),
        cost_estimate=pl.CostEstimate(flops=flops, bytes_accessed=2**20, transcendentals=0),
    )


def shape(*extent):
    return jax.ShapeDtypeStruct(extent, BF)


def place_of(z, y, c):
    return (z % NZ) * NY * NCORE + (y % NY) * NCORE + c


def pairs(move):
    return [
        (place_of(z, y, c), place_of(*move(z, y, c))) for z in range(NZ) for y in range(NY) for c in range(NCORE)
    ]


def send(array, move):
    return lax.ppermute(array, "tile", pairs(move))


def later(array, by=1):
    return lax.ppermute(array, "group", [(i, i + by) for i in range(NX - by)])


def spread(record):
    along = lambda by: lambda z, y, c: (z + (by if c == 0 else -by), y, c)
    t0 = jnp.stack([record, send(record, swap)])
    t1 = send(t0, along(1))
    t2 = send(t0, along(2))
    t3 = send(jnp.concatenate([t1, t2[:1]], axis=0), along(2))
    return t0, t1, t2, t3


def swap(z, y, c):
    return z, y, 1 - c


def deliver(table, held, after):
    mine, other = call(
        select_kernel, [shape(NY, REC, C, W)] * 2, "svvvv-", [pltpu.SMEM((TILES,), jnp.int32)]
    )(table, *held, after)
    arrived = send(other, swap)
    own, one, two, three = call(combine_kernel, [shape(REC, C, W)] * 4, "svv")(table, mine, arrived)
    total = own.astype(F32)
    for by, part in ((2, two), (1, one), (3, three)):
        total = total + send(part, lambda z, y, c, by=by: (z, y + by, c)).astype(F32)
    return total.astype(BF)


def per_device(
    features, tile_list, neighbours, clip_frames, gain_one, weight_one, bias_one, gain_two, weight_two, bias_two
):
    table = jnp.concatenate(
        [
            jnp.stack([lax.axis_index("tile"), lax.axis_index("group")]).astype(jnp.int32),
            tile_list,
            neighbours.reshape(-1),
            clip_frames,
        ]
    )
    vectors = jnp.stack([bias_one, gain_one, gain_two, bias_two], axis=1)
    own = features[0].transpose(0, 2, 1, 3)
    prev = later(own)
    record = call(record_kernel, shape(REC, C, W), "sv")(table, own)
    weights = call(weights_kernel, shape(2, 2 * C, 4 * KF), "vv", mib=16)(
        weight_one.reshape(3, 9 * C, C), weight_two.reshape(3, 9 * C, C)
    )
    held = spread(record)
    window = pltpu.VMEM((2 * F, H + 2, 3 * C, W), BF)
    second = call(
        inner_first_kernel, shape(F * H + REC, C, W), "svvvv-", [window], 24, 8 * 10**9
    )(table, own, prev, weights, vectors, held[1])
    second_prev = later(second)
    halo = deliver(table, held, second)
    halo1, halo2 = later(halo), later(halo, 2)
    inner = call(
        inner_second_kernel, jax.ShapeDtypeStruct((F, H, C, W), F32), "vvvvv-", [window], 24, 8 * 10**9
    )(own, second, second_prev, weights, vectors, halo)
    out = call(
        outer_kernel,
        shape(F, H, C, W),
        "s" + "v" * 9,
        [
            pltpu.VMEM((3 * F, 4, 3 * C, W), BF),
            pltpu.VMEM((3 * F, 4, 3, C, W), BF),
            pltpu.VMEM((2 * F, 4, 3 * C, W), BF),
            pltpu.VMEM((2 * F, 4, 3, C, W), BF),
        ],
        24,
        4 * 10**9,
    )(table, inner, record, second, second_prev, halo, halo1, halo2, weights, vectors)
    return out.transpose(0, 2, 1, 3)[None]


def solution(mesh):
    placed = (P("tile", "group", None, None, None), P(), P(), P(), P(), P(), P(), P(), P(), P())
    return jax.shard_map(
        per_device,
        mesh=mesh,
        in_specs=placed,
        out_specs=P("tile", "group", None, None, None),
        check_vma=False,
    )
```

```python
import functools

import jax
import jax.numpy as jnp
from jax import lax
from jax.experimental import pallas as pl
from jax.experimental.pallas import tpu as pltpu
from jax.sharding import PartitionSpec as P

NZ, NY, NCORE, NX = 8, 4, 2, 4
TILES = NZ * NY * NCORE
TPC = 4
C, H, W, F = 96, 16, 128, 2
REC = 5
KF = 9 * C + 32
T_LIST = 2
T_NEAR = T_LIST + TILES
T_CLIP = T_NEAR + TILES * 8
BF, F32 = jnp.bfloat16, jnp.float32

SMEM = pl.BlockSpec(memory_space=pltpu.SMEM)
VMEM = pl.BlockSpec(memory_space=pltpu.VMEM)
ANY = pl.BlockSpec(memory_space=pl.ANY)


def params(mib):
    return pltpu.CompilerParams(vmem_limit_bytes=mib * 1024 * 1024)


def sides(table):
    tile = table[T_LIST + table[0]]
    up = table[T_NEAR + tile * 8 + 1] >= 0
    left = table[T_NEAR + tile * 8 + 3] >= 0
    return up, left


def norm_silu(values, gain):
    inverse = lax.rsqrt(jnp.mean(values * values, axis=0, keepdims=True) + 1e-06)
    scaled = values * inverse * gain
    return scaled / (1.0 + jnp.exp(-scaled))


def rotate(values, by):
    return pltpu.roll(values, by, 1)


def lanes(rows):
    return lax.broadcasted_iota(jnp.int32, (rows, W), 1)


def write_record(features, up, left, out, base):
    row = jnp.where(up, 0, H - 2)
    for f in range(F):
        for r in range(2):
            out[base + 2 * f + r] = features[f, row + r]
    turn = jnp.where(left, 0, 2)
    lane = lanes(C)
    columns = jnp.zeros((C, W), F32)
    for f in range(F):
        for y in range(H):
            at = f * 32 + 2 * y
            moved = rotate(features[f, y].astype(F32), at + turn)
            columns = jnp.where(lane // 2 == at // 2, moved, columns)
    out[base + 4] = jnp.where(lane < 64, columns, rotate(columns, 64)).astype(BF)


def record_kernel(ids, tiles, near, features, out):
    tile = tiles[ids[0]]
    up, left = near[1, tile] >= 0, near[3, tile] >= 0
    write_record(features, up, left, out, 0)


def weights_kernel(one, two, _, out):
    same = lax.broadcasted_iota(jnp.int32, (C, C), 0) == lax.broadcasted_iota(jnp.int32, (C, C), 1)
    same = same.astype(F32).astype(BF)
    for n, source in enumerate((one, two)):
        out[n, 0:C, 3 * KF :] = jnp.zeros((C, KF), BF)
        out[n, C:, 0:KF] = jnp.zeros((C, KF), BF)
        for t in range(3):
            flipped = lax.dot_general(same, source[t], (((1,), (1,)), ((), ())), preferred_element_type=F32)
            flipped = jnp.concatenate([flipped.astype(BF), jnp.zeros((C, KF - 9 * C), BF)], axis=1)
            out[n, 0:C, t * KF : (t + 1) * KF] = flipped
            out[n, C:, (t + 1) * KF : (t + 2) * KF] = flipped


def plan_kernel(table, _, out, inverse):
    me = table[0]
    z, y, c = me // (NY * NCORE), (me // NCORE) % NY, me % NCORE

    def invert(i, _):
        inverse[table[T_LIST + i]] = i
        return 0

    lax.fori_loop(0, TILES, invert, 0)

    def place(tile):
        slot = inverse[jnp.maximum(tile, 0)]
        zs, ys, cs = slot // (NY * NCORE), (slot // NCORE) % NY, slot % NCORE
        away = jnp.where(c == 0, z - zs, zs - z)
        away = jnp.where(away < 0, away + NZ, away)
        label = jnp.where(cs == c, 0, 1)
        fits = (tile >= 0) & (ys == y) & ((away >= 1) & (away <= 3) | (label == 0) & ((away == 0) | (away == 4)))
        return jnp.where(fits, jnp.minimum(away, 3), -1), jnp.where(away == 4, 0, jnp.where(away == 3, 1 + label, label))

    for n in range(2 * NY):
        core = c if n < NY else 1 - c
        near = T_NEAR + table[T_LIST + z * NY * NCORE + (n % NY) * NCORE + core] * 8
        vertical = jnp.maximum(table[near + 1], table[near + 6])
        horizontal = jnp.maximum(table[near + 3], table[near + 4])
        diagonal = jnp.maximum(
            jnp.maximum(table[near], table[near + 2]), jnp.maximum(table[near + 5], table[near + 7])
        )
        for k, tile in enumerate((vertical, horizontal, diagonal)):
            which, index = place(tile)
            out[6 * n + 2 * k] = which
            out[6 * n + 2 * k + 1] = index


def select_kernel(plan, t0, t1, t2, t3, _, mine, other):
    held = (t0, t1, t2, t3)
    mine[...] = jnp.zeros_like(mine)
    other[...] = jnp.zeros_like(other)
    low = lanes(C) < 64
    for n in range(2 * NY):
        out, yd = (mine, other)[n // NY], n % NY
        for k, ref in enumerate(held):

            @pl.when(plan[6 * n] == k)
            def _():
                out[yd, 0:4] = ref[plan[6 * n + 1], 0:4]

            @pl.when(plan[6 * n + 2] == k)
            def _():
                out[yd, 4] = jnp.where(low, ref[plan[6 * n + 3], 4], out[yd, 4])

            @pl.when(plan[6 * n + 4] == k)
            def _():
                out[yd, 4] = jnp.where(low, out[yd, 4], ref[plan[6 * n + 5], 4])


def combine_kernel(table, mine, arrived, own, one, two, three):
    y = (table[0] // NCORE) % NY
    for by, out in enumerate((own, one, two, three)):
        to = (y + by) % NY
        out[...] = (mine[to].astype(F32) + arrived[to].astype(F32)).astype(BF)


def three_shifts(center, at_left, at_right):
    lane = lanes(C)
    before = jnp.where(lane == 0, at_left, rotate(center, 1))
    after = jnp.where(lane == W - 1, at_right, rotate(center, W - 1))
    return before.astype(BF), center.astype(BF), after.astype(BF)


def put_window(windows, place, values):
    for k, value in enumerate(values):
        windows[(*place, slice(k * C, (k + 1) * C))] = value


def stack(parts):
    full = []
    for part in parts:
        full += [part, jnp.zeros((KF - 9 * C, part.shape[1]), BF)]
    return jnp.concatenate(full, axis=0)


def row_parts(frames, oy, count):
    return [
        jnp.concatenate([windows[f, pl.ds(oy + r, 3)].reshape(9 * C, W) for r in range(count)], axis=1)
        for windows, f in frames
    ]


def frames_of(*windows):
    return [(ref, f) for ref in windows for f in range(F)]


def product(weights, parts):
    return jnp.dot(weights[...], stack(parts), preferred_element_type=F32)


def half_product(weights, windows, half, oy):
    return product(weights.at[:, pl.ds(half * F * KF, F * KF)], row_parts(frames_of(windows), oy, 2))


def first_windows(source, gain, exists, windows):
    zero_ends(windows)
    for f in range(F):

        def row_step(y, _):
            center = jnp.where(exists, norm_silu(source[f, y].astype(F32), gain), 0.0)
            put_window(windows, (f, y + 1), three_shifts(center, 0.0, 0.0))
            return 0

        lax.fori_loop(0, H, row_step, 0, unroll=4)


def own_first_kernel(own, weights, vectors, out, windows):
    first_windows(own, vectors[:, 1:2], True, windows)

    def rows_step(n, _):
        out[n] = half_product(weights.at[0], windows, 1, 2 * n)
        return 0

    lax.fori_loop(0, H // 2, rows_step, 0)


def second_windows(source, exists, windows):
    zero_ends(windows)
    for f in range(F):

        def row_step(y, _):
            center = jnp.where(exists, source[f * H + y].astype(F32), 0.0)
            put_window(windows, (f, y + 1), three_shifts(center, 0.0, 0.0))
            return 0

        lax.fori_loop(0, H, row_step, 0, unroll=4)


def own_second_kernel(own, second, weights, vectors, out, windows):
    bias = vectors[:, 3:4]
    second_windows(second, True, windows)

    def rows_step(n, _):
        acc = half_product(weights.at[1], windows, 1, 2 * n)
        for f in range(F):
            value = acc[f * C : (f + 1) * C] + bias
            for r in range(2):
                y = 2 * n + r
                out[f, y] = own[f, y].astype(F32) + value[:, r * W : (r + 1) * W]
        return 0

    lax.fori_loop(0, H // 2, rows_step, 0)


def inner_first_kernel(table, prev, partial, weights, vectors, _, _plan, out, windows):
    up, left = sides(table)
    bias, gain_one, gain_two = vectors[:, 0:1], vectors[:, 1:2], vectors[:, 2:3]
    write_record(prev, up, left, out, F * H)
    first_windows(prev, gain_one, table[1] > 0, windows)
    border_row, border_lane = jnp.where(up, 0, H - 1), jnp.where(left, 0, W - 1)
    lane = lanes(C)

    def rows_step(n, _):
        acc = partial[n] + half_product(weights.at[0], windows, 0, 2 * n)
        for f in range(F):
            value = norm_silu(acc[f * C : (f + 1) * C] + bias, gain_two)
            for r in range(2):
                y = 2 * n + r
                border = (lane == border_lane) | (y == border_row)
                out[f * H + y] = jnp.where(border, 0.0, value[:, r * W : (r + 1) * W]).astype(BF)
        return 0

    lax.fori_loop(0, H // 2, rows_step, 0)


def inner_second_kernel(table, partial, second_prev, weights, _, out, windows):
    second_windows(second_prev, table[1] > 0, windows)

    def rows_step(n, _):
        acc = half_product(weights.at[1], windows, 0, 2 * n)
        for f in range(F):
            for r in range(2):
                y = 2 * n + r
                out[f, y] = partial[f, y] + acc[f * C : (f + 1) * C, r * W : (r + 1) * W]
        return 0

    lax.fori_loop(0, H // 2, rows_step, 0)


def zero_ends(windows):
    for fr in range(F):
        for yy in (0, H + 1):
            windows[fr, yy] = jnp.zeros((3 * C, W), BF)


def band_parts(band, columns, base):
    parts = row_parts([(band, base + fr) for fr in range(2 * F)], 0, 2)
    for fr in range(2 * F):
        beside = [
            jnp.concatenate([columns[base + fr, j + dx, dy] for dy in range(3) for dx in range(3)], axis=0)
            for j in range(2)
        ]
        parts[fr] = jnp.concatenate([parts[fr]] + beside, axis=1)
    return parts


def put_column(columns, fr, k, value):
    columns[fr, k, 0] = rotate(value, 1).astype(BF)
    columns[fr, k, 1] = value.astype(BF)
    columns[fr, k, 2] = rotate(value, W - 1).astype(BF)


def outer_kernel(
    table, inner, record0, second_own, second_prev, halo0, halo1, halo2, weights, vectors,
    out, band1, columns1, band2, columns2
):
    up, left = sides(table)
    bias1, gain1, gain2 = vectors[:, 0:1], vectors[:, 1:2], vectors[:, 2:3]
    sources = ((second_prev, F * H, halo2), (second_own, F * H, halo1), (record0, 0, halo0))
    lane = lanes(C)

    src = lax.broadcasted_iota(jnp.int32, (W, 2 * W), 0)
    dst2 = lax.broadcasted_iota(jnp.int32, (W, 2 * W), 1)
    dst, col = dst2 % W, dst2 // W
    none = -1000
    body = jnp.where((dst >= 2) & (dst < H + 2), 2 * (dst - 2), none)
    above = jnp.where(dst < 2, 64 + 2 * (H - 2 + dst), none)
    below = jnp.where((dst >= H + 2) & (dst < H + 4), 64 + 2 * (dst - H - 2), none)
    corner = jnp.where(up, above, below)
    past = jnp.where(up, 0, H + 2)
    first_col = jnp.where(left, 0, W - 2)
    for fr in range(3 * F):
        f = fr % F
        record, base, halo = sources[fr // F]
        exists = table[1] >= 2 - fr // F
        pick = (src == jnp.maximum(body, corner) + f * 32 + col).astype(F32).astype(BF)
        theirs = jnp.dot(halo[4], pick, preferred_element_type=F32)
        theirs = norm_silu(jnp.where(exists, theirs, 0.0), gain1)
        picks = [(src == body + f * 32 + col).astype(F32).astype(BF)]
        for r in range(2):
            picks.append(((src == first_col + col) & (dst == past + r)).astype(F32).astype(BF))
        mine = jnp.concatenate([record[base + 4], halo[2 * f], halo[2 * f + 1]], axis=1)
        ours = jnp.dot(mine, jnp.concatenate(picks, axis=0), preferred_element_type=F32)
        ours = norm_silu(jnp.where(exists, ours, 0.0), gain1)
        low, high = jnp.where(left, theirs, ours), jnp.where(left, ours, theirs)
        for k in range(4):
            put_column(columns1, fr, k, (low if k < 2 else high)[:, (k % 2) * W : (k % 2 + 1) * W])
        near = jnp.where(left, theirs[:, W:], theirs[:, :W])
        for r in range(4):
            other, self = halo[2 * f + r % 2], record[base + 2 * f + r % 2]
            raw = jnp.where(up, other if r < 2 else self, self if r < 2 else other)
            at = jnp.where(up, r, H + r)
            moved = rotate(near, jnp.where(left, (W - at) % W, W - 1 - at))
            center = norm_silu(jnp.where(exists, raw.astype(F32), 0.0), gain1)
            put_window(
                band1, (fr, r), three_shifts(center, jnp.where(left, moved, 0.0), jnp.where(left, 0.0, moved))
            )

    inside = (lane >= jnp.where(up, 3, 2)) & (lane < jnp.where(up, H + 2, H + 1))
    row_at, col_at = jnp.where(up, 0, 2), jnp.where(left, 0, 2)
    for p in range(2):
        acc = product(weights.at[0], band_parts(band1, columns1, F * p))
        for f in range(F):
            s = F * p + f
            value = norm_silu(acc[f * C : (f + 1) * C] + bias1, gain2)
            if p == 0:
                value = jnp.where(table[1] > 0, value, 0.0)
            beside = [value[:, 2 * W : 3 * W], value[:, 3 * W :]]
            near = jnp.where(left, beside[0], beside[1])
            for j in range(2):
                at = jnp.where(up, 1 + j, H + 1 + j)
                moved = rotate(near, jnp.where(left, W - at, W - 1 - at))
                center = value[:, j * W : (j + 1) * W]
                put_window(
                    band2,
                    (s, row_at + j),
                    three_shifts(center, jnp.where(left, moved, 0.0), jnp.where(left, 0.0, moved)),
                )
                band2[s, 2 - row_at + j] = jnp.zeros((3 * C, W), BF)
                put_column(columns2, s, col_at + j, jnp.where(inside, beside[j], 0.0))
                columns2[s, 2 - col_at + j] = jnp.zeros((3, C, W), BF)

    length = table[T_CLIP + table[T_LIST + table[0]] // TPC]
    start = table[1] * F
    acc = product(weights.at[1], band_parts(band2, columns2, 0))
    for f in range(F):
        value = acc[f * C : (f + 1) * C]
        for y in range(H):
            total = inner[f, y]
            for j in range(2):
                at = first_col + j
                moved = rotate(value[:, (2 + j) * W : (3 + j) * W], (at + W - 2 - y) % W)
                total = total + jnp.where(lane == at, moved, 0.0)
            if y < 2:
                total = total + jnp.where(up, value[:, y * W : (y + 1) * W], 0.0)
            if y >= H - 2:
                j = y - (H - 2)
                total = total + jnp.where(up, 0.0, value[:, j * W : (j + 1) * W])
            out[f, y] = jnp.where(start + f < length, total, 0.0).astype(BF)


def call(kernel, outs, kinds, scratch=(), mib=8, flops=0):
    single = not isinstance(outs, (list, tuple))
    return pl.pallas_call(
        kernel,
        out_shape=outs,
        in_specs=[{"s": SMEM, "v": VMEM, "-": ANY}[kind] for kind in kinds],
        out_specs=VMEM if single else [VMEM] * len(outs),
        scratch_shapes=list(scratch),
        compiler_params=params(mib),
        cost_estimate=pl.CostEstimate(flops=flops, bytes_accessed=2**20, transcendentals=0),
    )


def shape(*extent):
    return jax.ShapeDtypeStruct(extent, BF)


def place_of(z, y, c):
    return (z % NZ) * NY * NCORE + (y % NY) * NCORE + c


def pairs(move):
    return [
        (place_of(z, y, c), place_of(*move(z, y, c))) for z in range(NZ) for y in range(NY) for c in range(NCORE)
    ]


def send(array, move):
    return lax.ppermute(array, "tile", pairs(move))


def later(array, by=1):
    return lax.ppermute(array, "group", [(i, (i + by) % NX) for i in range(NX)])


def spread(record):
    along = lambda by: lambda z, y, c: (z + (by if c == 0 else -by), y, c)
    t0 = jnp.stack([record, send(record, swap)])
    t1 = send(t0, along(1))
    t2 = send(t0, along(2))
    t3 = send(jnp.concatenate([t2[:1], t1], axis=0), along(2))
    return t0, t1, t2, t3


def swap(z, y, c):
    return z, y, 1 - c


def deliver(table, plan, held, after):
    mine, other = call(select_kernel, [shape(NY, REC, C, W)] * 2, "svvvv-")(plan, *held, after)
    arrived = send(other, swap)
    own, one, two, three = call(combine_kernel, [shape(REC, C, W)] * 4, "svv")(table, mine, arrived)
    total = own.astype(F32)
    for by, part in ((2, two), (1, one), (3, three)):
        total = total + send(part, lambda z, y, c, by=by: (z, y + by, c)).astype(F32)
    return total.astype(BF)


def per_device(
    features, tile_list, neighbours, clip_frames, gain_one, weight_one, bias_one, gain_two, weight_two, bias_two
):
    ids = jnp.stack([lax.axis_index("tile"), lax.axis_index("group")]).astype(jnp.int32)
    table = jnp.concatenate(
        [
            ids,
            tile_list,
            neighbours.reshape(-1),
            clip_frames,
        ]
    )
    vectors = jnp.stack([bias_one, gain_one, gain_two, bias_two], axis=1)
    own = features[0].transpose(0, 2, 1, 3)
    prev = later(own)
    record = call(record_kernel, shape(REC, C, W), "sssv")(ids, tile_list, neighbours.T, own)
    held = spread(record)
    weights = call(weights_kernel, shape(2, 2 * C, 4 * KF), "vv-", mib=16)(
        weight_one.reshape(3, 9 * C, C), weight_two.reshape(3, 9 * C, C), held[0]
    )
    plan = pl.pallas_call(
        plan_kernel,
        out_shape=jax.ShapeDtypeStruct((12 * NY,), jnp.int32),
        in_specs=[SMEM, ANY],
        out_specs=SMEM,
        scratch_shapes=[pltpu.SMEM((TILES,), jnp.int32)],
    )(table, held[0])
    scratch = [pltpu.VMEM((F, H + 2, 3 * C, W), BF)]
    own_one = call(
        own_first_kernel, jax.ShapeDtypeStruct((H // 2, 2 * C, 2 * W), F32), "vvv", scratch, 16, 3 * 10**9
    )(own, weights, vectors)
    second = call(
        inner_first_kernel, shape(F * H + REC, C, W), "svvvv-s", scratch, 16, 8 * 10**9
    )(table, prev, own_one, weights, vectors, held[1], plan)
    whole = jax.ShapeDtypeStruct((F, H, C, W), F32)
    own_two = call(own_second_kernel, whole, "vvvv", scratch, 16, 10**9)(own, second, weights, vectors)
    second_prev = later(second)
    halo = deliver(table, plan, held, second)
    halo1, halo2 = later(halo), later(halo, 2)
    inner = call(inner_second_kernel, whole, "svvv-", scratch, 16, 12 * 10**9)(
        table, own_two, second_prev, weights, halo
    )
    out = call(
        outer_kernel,
        shape(F, H, C, W),
        "s" + "v" * 9,
        [
            pltpu.VMEM((3 * F, 4, 3 * C, W), BF),
            pltpu.VMEM((3 * F, 4, 3, C, W), BF),
            pltpu.VMEM((2 * F, 4, 3 * C, W), BF),
            pltpu.VMEM((2 * F, 4, 3, C, W), BF),
        ],
        24,
        4 * 10**9,
    )(table, inner, record, second, second_prev, halo, halo1, halo2, weights, vectors)
    return out.transpose(0, 2, 1, 3)[None]


def solution(mesh):
    placed = (P("tile", "group", None, None, None), P(), P(), P(), P(), P(), P(), P(), P(), P())
    return jax.shard_map(
        per_device,
        mesh=mesh,
        in_specs=placed,
        out_specs=P("tile", "group", None, None, None),
        check_vma=False,
    )
```

```python
import functools

import jax
import jax.numpy as jnp
from jax import lax
from jax.experimental import pallas as pl
from jax.experimental.pallas import tpu as pltpu
from jax.sharding import PartitionSpec as P

NZ, NY, NCORE, NX = 8, 4, 2, 4
TILES = NZ * NY * NCORE
TPC = 4
C, H, W, F = 96, 16, 128, 2
HALF = H // 2
CUT = HALF + 1
REC = 5
KF = 9 * C + 32
P_UP, P_LEFT, P_GROUP, P_Y, P_LENGTH = range(12 * NY, 12 * NY + 5)
BF, F32 = jnp.bfloat16, jnp.float32

SMEM = pl.BlockSpec(memory_space=pltpu.SMEM)
VMEM = pl.BlockSpec(memory_space=pltpu.VMEM)
ANY = pl.BlockSpec(memory_space=pl.ANY)


def params(mib):
    return pltpu.CompilerParams(vmem_limit_bytes=mib * 1024 * 1024)


def sides(plan):
    return plan[P_UP] > 0, plan[P_LEFT] > 0


def norm_silu(values, gain):
    inverse = lax.rsqrt(jnp.mean(values * values, axis=0, keepdims=True) + 1e-06)
    scaled = values * inverse * gain
    return scaled / (1.0 + jnp.exp(-scaled))


def rotate(values, by):
    return pltpu.roll(values, by, 1)


def lanes(rows):
    return lax.broadcasted_iota(jnp.int32, (rows, W), 1)


def row_of(upper, lower, f, y):
    return upper[f, y] if y < CUT else lower[f, y - CUT]


def write_record(upper, lower, up, left, out, base):
    for f in range(F):
        for r in range(2):
            out[base + 2 * f + r] = jnp.where(up, upper[f, r], lower[f, H - 2 - CUT + r])
    turn = jnp.where(left, 0, 2)
    lane = lanes(C)
    columns = jnp.zeros((C, W), F32)
    for f in range(F):
        for y in range(H):
            at = f * 32 + 2 * y
            moved = rotate(row_of(upper, lower, f, y).astype(F32), at + turn)
            columns = jnp.where(lane // 2 == at // 2, moved, columns)
    out[base + 4] = jnp.where(lane < 64, columns, rotate(columns, 64)).astype(BF)


def record_kernel(ids, tiles, near, upper, lower, out):
    tile = tiles[ids[0]]
    up, left = near[1, tile] >= 0, near[3, tile] >= 0
    write_record(upper, lower, up, left, out, 0)


def weights_kernel(one, two, bias_one, gain_one, gain_two, bias_two, _, out, vectors):
    same = lax.broadcasted_iota(jnp.int32, (C, C), 0) == lax.broadcasted_iota(jnp.int32, (C, C), 1)
    columns = [jnp.sum(jnp.where(same, v[...], 0.0), axis=1, keepdims=True) for v in (bias_one, gain_one, gain_two, bias_two)]
    vectors[...] = jnp.concatenate(columns, axis=1)
    same = same.astype(F32).astype(BF)
    for n, source in enumerate((one, two)):
        out[n, 0:C, 3 * KF :] = jnp.zeros((C, KF), BF)
        out[n, C:, 0:KF] = jnp.zeros((C, KF), BF)
        for t in range(3):
            flipped = lax.dot_general(same, source[t], (((1,), (1,)), ((), ())), preferred_element_type=F32)
            flipped = jnp.concatenate([flipped.astype(BF), jnp.zeros((C, KF - 9 * C), BF)], axis=1)
            out[n, 0:C, t * KF : (t + 1) * KF] = flipped
            out[n, C:, (t + 1) * KF : (t + 2) * KF] = flipped


def plan_kernel(ids, tiles, near, clips, _, out, inverse):
    me = ids[0]
    z, y, c = me // (NY * NCORE), (me // NCORE) % NY, me % NCORE
    own = tiles[me]
    out[P_UP] = jnp.where(near[1, own] >= 0, 1, 0)
    out[P_LEFT] = jnp.where(near[3, own] >= 0, 1, 0)
    out[P_GROUP] = ids[1]
    out[P_Y] = y
    out[P_LENGTH] = clips[own // TPC]

    def invert(i, _):
        inverse[tiles[i]] = i
        return 0

    lax.fori_loop(0, TILES, invert, 0, unroll=16)

    def place(tile):
        slot = inverse[jnp.maximum(tile, 0)]
        zs, ys, cs = slot // (NY * NCORE), (slot // NCORE) % NY, slot % NCORE
        away = jnp.where(c == 0, z - zs, zs - z)
        away = jnp.where(away < 0, away + NZ, away)
        label = jnp.where(cs == c, 0, 1)
        fits = (tile >= 0) & (ys == y) & ((away >= 1) & (away <= 3) | (label == 0) & ((away == 0) | (away == 4)))
        return jnp.where(fits, jnp.minimum(away, 3), -1), jnp.where(away == 4, 0, jnp.where(away == 3, 1 + label, label))

    for n in range(2 * NY):
        core = c if n < NY else 1 - c
        tile = tiles[z * NY * NCORE + (n % NY) * NCORE + core]
        vertical = jnp.maximum(near[1, tile], near[6, tile])
        horizontal = jnp.maximum(near[3, tile], near[4, tile])
        diagonal = jnp.maximum(jnp.maximum(near[0, tile], near[2, tile]), jnp.maximum(near[5, tile], near[7, tile]))
        for k, tile in enumerate((vertical, horizontal, diagonal)):
            which, index = place(tile)
            out[6 * n + 2 * k] = which
            out[6 * n + 2 * k + 1] = index


def select_kernel(plan, t0, t1, t2, t3, _, mine, other):
    held = (t0, t1, t2, t3)
    mine[...] = jnp.zeros_like(mine)
    other[...] = jnp.zeros_like(other)
    low = lanes(C) < 64
    for n in range(2 * NY):
        out, yd = (mine, other)[n // NY], n % NY
        for k, ref in enumerate(held):

            @pl.when(plan[6 * n] == k)
            def _():
                out[yd, 0:4] = ref[plan[6 * n + 1], 0:4]

            @pl.when(plan[6 * n + 2] == k)
            def _():
                out[yd, 4] = jnp.where(low, ref[plan[6 * n + 3], 4], out[yd, 4])

            @pl.when(plan[6 * n + 4] == k)
            def _():
                out[yd, 4] = jnp.where(low, out[yd, 4], ref[plan[6 * n + 5], 4])


def forward_kernel(t1, t2, _, out):
    out[0] = t2[0]
    out[1:] = t1[...]


def combine_kernel(plan, mine, arrived, own, one, two, three):
    y = plan[P_Y]
    for by, out in enumerate((own, one, two, three)):
        to = (y + by) % NY
        out[...] = (mine[to].astype(F32) + arrived[to].astype(F32)).astype(BF)


def three_shifts(center, at_left, at_right):
    lane = lanes(C)
    before = jnp.where(lane == 0, at_left, rotate(center, 1))
    after = jnp.where(lane == W - 1, at_right, rotate(center, W - 1))
    return before.astype(BF), center.astype(BF), after.astype(BF)


def put_window(windows, place, values):
    for k, value in enumerate(values):
        windows[(*place, slice(k * C, (k + 1) * C))] = value


def stack(parts):
    full = []
    for part in parts:
        full += [part, jnp.zeros((KF - 9 * C, part.shape[1]), BF)]
    return jnp.concatenate(full, axis=0)


def row_parts(frames, oy, count):
    return [
        jnp.concatenate([windows[f, pl.ds(oy + r, 3)].reshape(9 * C, W) for r in range(count)], axis=1)
        for windows, f in frames
    ]


def frames_of(*windows):
    return [(ref, f) for ref in windows for f in range(F)]


def product(weights, parts):
    return jnp.dot(weights[...], stack(parts), preferred_element_type=F32)


def half_product(weights, windows, half, oy):
    return product(weights.at[:, pl.ds(half * F * KF, F * KF)], row_parts(frames_of(windows), oy, 2))


def first_window(raw, gain, exists, windows, place):
    center = jnp.where(exists, norm_silu(raw.astype(F32), gain), 0.0)
    put_window(windows, place, three_shifts(center, 0.0, 0.0))


def second_window(raw, exists, windows, place):
    put_window(windows, place, three_shifts(jnp.where(exists, raw.astype(F32), 0.0), 0.0, 0.0))


def each_row(count, step):
    def body(y, _):
        step(y)
        return 0

    lax.fori_loop(0, count, body, 0, unroll=True if count < 4 else 4)


def zero_end(windows, yy):
    for f in range(F):
        windows[f, yy] = jnp.zeros((3 * C, W), BF)


def own_first_kernel(upper, lower, weights, vectors, out, windows):
    gain = vectors[:, 1:2]
    zero_end(windows, 0)
    zero_end(windows, H + 1)
    for f in range(F):
        each_row(CUT, lambda y: first_window(upper[f, y], gain, True, windows, (f, y + 1)))
        each_row(H - CUT, lambda y: first_window(lower[f, y], gain, True, windows, (f, y + 1 + CUT)))

    def rows_step(n, _):
        out[n] = half_product(weights.at[0], windows, 1, 2 * n)
        return 0

    lax.fori_loop(0, H // 2, rows_step, 0)


def write_second(plan, partial, weights, vectors, out, windows, first, stride):
    up, left = sides(plan)
    bias, gain_two = vectors[:, 0:1], vectors[:, 2:3]
    border_row, border_lane = jnp.where(up, 0, H - 1), jnp.where(left, 0, W - 1)
    lane = lanes(C)

    def rows_step(n, _):
        acc = partial[n + first // 2] + half_product(weights.at[0], windows, 0, 2 * n)
        for f in range(F):
            value = norm_silu(acc[f * C : (f + 1) * C] + bias, gain_two)
            for r in range(2):
                y = 2 * n + r
                border = (lane == border_lane) | (y + first == border_row)
                out[f * stride + first + y] = jnp.where(border, 0.0, value[:, r * W : (r + 1) * W]).astype(BF)
        return 0

    lax.fori_loop(0, HALF // 2, rows_step, 0)


def inner_upper_kernel(plan, prev, partial, weights, vectors, out, windows):
    gain, exists = vectors[:, 1:2], plan[P_GROUP] > 0
    zero_end(windows, 0)
    for f in range(F):
        each_row(CUT, lambda y: first_window(prev[f, y], gain, exists, windows, (f, y + 1)))
    write_second(plan, partial, weights, vectors, out, windows, 0, HALF)


def inner_lower_kernel(plan, upper, lower, partial, weights, vectors, _, done, out, windows):
    gain, exists = vectors[:, 1:2], plan[P_GROUP] > 0
    zero_end(windows, HALF + 1)
    for f in range(F):
        each_row(2, lambda y: first_window(upper[f, HALF - 1 + y], gain, exists, windows, (f, y)))
        each_row(H - CUT, lambda y: first_window(lower[f, y], gain, exists, windows, (f, y + 2)))
    for f in range(F):
        out[f * H : f * H + HALF] = done[f * HALF : (f + 1) * HALF]
    write_second(plan, partial, weights, vectors, out, windows, HALF, H)
    up, left = sides(plan)
    write_record(upper, lower, up, left, out, F * H)


def second_windows(source, exists, windows):
    zero_end(windows, 0)
    zero_end(windows, H + 1)
    for f in range(F):
        each_row(H, lambda y: second_window(source[f * H + y], exists, windows, (f, y + 1)))


def own_second_kernel(own_upper, own_lower, second, weights, vectors, out, windows):
    bias = vectors[:, 3:4]
    second_windows(second, True, windows)
    for n in range(H // 2):
        acc = half_product(weights.at[1], windows, 1, 2 * n)
        for f in range(F):
            value = acc[f * C : (f + 1) * C] + bias
            for r in range(2):
                y = 2 * n + r
                out[f, y] = row_of(own_upper, own_lower, f, y).astype(F32) + value[:, r * W : (r + 1) * W]


def inner_second_kernel(plan, partial, second, weights, _, out, windows):
    second_windows(second, plan[P_GROUP] > 0, windows)

    def rows_step(n, _):
        acc = half_product(weights.at[1], windows, 0, 2 * n)
        for f in range(F):
            for r in range(2):
                y = 2 * n + r
                out[f, y] = partial[f, y] + acc[f * C : (f + 1) * C, r * W : (r + 1) * W]
        return 0

    lax.fori_loop(0, H // 2, rows_step, 0)


def band_parts(band, columns, base):
    parts = row_parts([(band, base + fr) for fr in range(2 * F)], 0, 2)
    for fr in range(2 * F):
        beside = [
            jnp.concatenate([columns[base + fr, j + dx, dy] for dy in range(3) for dx in range(3)], axis=0)
            for j in range(2)
        ]
        parts[fr] = jnp.concatenate([parts[fr]] + beside, axis=1)
    return parts


def put_column(columns, fr, k, value):
    columns[fr, k, 0] = rotate(value, 1).astype(BF)
    columns[fr, k, 1] = value.astype(BF)
    columns[fr, k, 2] = rotate(value, W - 1).astype(BF)


def outer_kernel(
    plan, inner, record0, second_own, second_prev, halo0, halo1, halo2, weights, vectors,
    out, band1, columns1, band2, columns2
):
    up, left = sides(plan)
    bias1, gain1, gain2 = vectors[:, 0:1], vectors[:, 1:2], vectors[:, 2:3]
    sources = ((second_prev, F * H, halo2), (second_own, F * H, halo1), (record0, 0, halo0))
    lane = lanes(C)

    src = lax.broadcasted_iota(jnp.int32, (W, 2 * W), 0)
    dst2 = lax.broadcasted_iota(jnp.int32, (W, 2 * W), 1)
    dst, col = dst2 % W, dst2 // W
    none = -1000
    body = jnp.where((dst >= 2) & (dst < H + 2), 2 * (dst - 2), none)
    above = jnp.where(dst < 2, 64 + 2 * (H - 2 + dst), none)
    below = jnp.where((dst >= H + 2) & (dst < H + 4), 64 + 2 * (dst - H - 2), none)
    corner = jnp.where(up, above, below)
    past = jnp.where(up, 0, H + 2)
    first_col = jnp.where(left, 0, W - 2)
    for fr in range(3 * F):
        f = fr % F
        record, base, halo = sources[fr // F]
        exists = plan[P_GROUP] >= 2 - fr // F
        pick = (src == jnp.maximum(body, corner) + f * 32 + col).astype(F32).astype(BF)
        theirs = jnp.dot(halo[4], pick, preferred_element_type=F32)
        theirs = norm_silu(jnp.where(exists, theirs, 0.0), gain1)
        picks = [(src == body + f * 32 + col).astype(F32).astype(BF)]
        for r in range(2):
            picks.append(((src == first_col + col) & (dst == past + r)).astype(F32).astype(BF))
        mine = jnp.concatenate([record[base + 4], halo[2 * f], halo[2 * f + 1]], axis=1)
        ours = jnp.dot(mine, jnp.concatenate(picks, axis=0), preferred_element_type=F32)
        ours = norm_silu(jnp.where(exists, ours, 0.0), gain1)
        low, high = jnp.where(left, theirs, ours), jnp.where(left, ours, theirs)
        for k in range(4):
            put_column(columns1, fr, k, (low if k < 2 else high)[:, (k % 2) * W : (k % 2 + 1) * W])
        near = jnp.where(left, theirs[:, W:], theirs[:, :W])
        for r in range(4):
            other, self = halo[2 * f + r % 2], record[base + 2 * f + r % 2]
            raw = jnp.where(up, other if r < 2 else self, self if r < 2 else other)
            at = jnp.where(up, r, H + r)
            moved = rotate(near, jnp.where(left, (W - at) % W, W - 1 - at))
            center = norm_silu(jnp.where(exists, raw.astype(F32), 0.0), gain1)
            put_window(
                band1, (fr, r), three_shifts(center, jnp.where(left, moved, 0.0), jnp.where(left, 0.0, moved))
            )

    inside = (lane >= jnp.where(up, 3, 2)) & (lane < jnp.where(up, H + 2, H + 1))
    row_at, col_at = jnp.where(up, 0, 2), jnp.where(left, 0, 2)
    for p in range(2):
        acc = product(weights.at[0], band_parts(band1, columns1, F * p))
        for f in range(F):
            s = F * p + f
            value = norm_silu(acc[f * C : (f + 1) * C] + bias1, gain2)
            if p == 0:
                value = jnp.where(plan[P_GROUP] > 0, value, 0.0)
            beside = [value[:, 2 * W : 3 * W], value[:, 3 * W :]]
            near = jnp.where(left, beside[0], beside[1])
            for j in range(2):
                at = jnp.where(up, 1 + j, H + 1 + j)
                moved = rotate(near, jnp.where(left, W - at, W - 1 - at))
                center = value[:, j * W : (j + 1) * W]
                put_window(
                    band2,
                    (s, row_at + j),
                    three_shifts(center, jnp.where(left, moved, 0.0), jnp.where(left, 0.0, moved)),
                )
                band2[s, 2 - row_at + j] = jnp.zeros((3 * C, W), BF)
                put_column(columns2, s, col_at + j, jnp.where(inside, beside[j], 0.0))
                columns2[s, 2 - col_at + j] = jnp.zeros((3, C, W), BF)

    length = plan[P_LENGTH]
    start = plan[P_GROUP] * F
    acc = product(weights.at[1], band_parts(band2, columns2, 0))
    for f in range(F):
        value = acc[f * C : (f + 1) * C]
        for y in range(H):
            total = inner[f, y]
            for j in range(2):
                at = first_col + j
                moved = rotate(value[:, (2 + j) * W : (3 + j) * W], (at + W - 2 - y) % W)
                total = total + jnp.where(lane == at, moved, 0.0)
            if y < 2:
                total = total + jnp.where(up, value[:, y * W : (y + 1) * W], 0.0)
            if y >= H - 2:
                j = y - (H - 2)
                total = total + jnp.where(up, 0.0, value[:, j * W : (j + 1) * W])
            out[f, y] = jnp.where(start + f < length, total, 0.0).astype(BF)


def call(kernel, outs, kinds, scratch=(), mib=8, flops=0):
    single = not isinstance(outs, (list, tuple))
    return pl.pallas_call(
        kernel,
        out_shape=outs,
        in_specs=[{"s": SMEM, "v": VMEM, "-": ANY}[kind] for kind in kinds],
        out_specs=VMEM if single else [VMEM] * len(outs),
        scratch_shapes=list(scratch),
        compiler_params=params(mib),
        cost_estimate=pl.CostEstimate(flops=flops, bytes_accessed=2**20, transcendentals=0),
    )


def shape(*extent):
    return jax.ShapeDtypeStruct(extent, BF)


def place_of(z, y, c):
    return (z % NZ) * NY * NCORE + (y % NY) * NCORE + c


def pairs(move):
    return [
        (place_of(z, y, c), place_of(*move(z, y, c))) for z in range(NZ) for y in range(NY) for c in range(NCORE)
    ]


def send(array, move):
    return lax.ppermute(array, "tile", pairs(move))


def later(array, by=1):
    return lax.ppermute(array, "group", [(i, (i + by) % NX) for i in range(NX)])


def spread(record):
    t0 = jnp.stack([record, send(record, swap)])
    t1 = send(t0, along(1))
    t2 = send(t0, along(2))
    return t0, t1, t2


def along(by):
    return lambda z, y, c: (z + (by if c == 0 else -by), y, c)


def swap(z, y, c):
    return z, y, 1 - c


def deliver(plan, held, after):
    mine, other = call(select_kernel, [shape(NY, REC, C, W)] * 2, "svvvv-")(plan, *held, after)
    arrived = send(other, swap)
    own, one, two, three = call(combine_kernel, [shape(REC, C, W)] * 4, "svv")(plan, mine, arrived)
    total = own.astype(F32)
    for by, part in ((2, two), (1, one), (3, three)):
        total = total + send(part, lambda z, y, c, by=by: (z, y + by, c)).astype(F32)
    return total.astype(BF)


def per_device(
    features, tile_list, neighbours, clip_frames, gain_one, weight_one, bias_one, gain_two, weight_two, bias_two
):
    ids = jnp.stack([lax.axis_index("tile"), lax.axis_index("group")]).astype(jnp.int32)
    own = [features[0, :, :, rows].transpose(0, 2, 1, 3) for rows in (slice(0, CUT), slice(CUT, H))]
    prev = [later(part) for part in own]
    near = neighbours.T
    record = call(record_kernel, shape(REC, C, W), "sssvv")(ids, tile_list, near, *own)
    t0, t1, t2 = spread(record)
    plan = pl.pallas_call(
        plan_kernel,
        out_shape=jax.ShapeDtypeStruct((12 * NY + 5,), jnp.int32),
        in_specs=[SMEM] * 4 + [ANY],
        out_specs=SMEM,
        scratch_shapes=[pltpu.SMEM((TILES,), jnp.int32)],
    )(ids, tile_list, near, clip_frames, t0)
    weights, vectors = call(
        weights_kernel, [shape(2, 2 * C, 4 * KF), jax.ShapeDtypeStruct((C, 4), F32)], "vvvvvv-", mib=16
    )(
        weight_one.reshape(3, 9 * C, C),
        weight_two.reshape(3, 9 * C, C),
        *(v.reshape(1, C) for v in (bias_one, gain_one, gain_two, bias_two)),
        t0,
    )
    scratch = [pltpu.VMEM((F, H + 2, 3 * C, W), BF)]
    half = [pltpu.VMEM((F, HALF + 2, 3 * C, W), BF)]
    own_one = call(
        own_first_kernel, jax.ShapeDtypeStruct((H // 2, 2 * C, 2 * W), F32), "vvvv", scratch, 16, 10**9
    )(*own, weights, vectors)
    upper = call(inner_upper_kernel, shape(H, C, W), "svvvv", half, 12, 2 * 10**9)(
        plan, prev[0], own_one, weights, vectors
    )
    onward = call(forward_kernel, shape(3, REC, C, W), "vv-")(t1, t2, upper)
    t3 = send(onward, along(2))
    second = call(inner_lower_kernel, shape(F * H + REC, C, W), "svvvvv-v", half, 12, 4 * 10**9)(
        plan, *prev, own_one, weights, vectors, onward, upper
    )
    second_prev = later(second)
    whole = jax.ShapeDtypeStruct((F, H, C, W), F32)
    own_two = call(own_second_kernel, whole, "vvvvv", scratch, 16, 10**9)(*own, second, weights, vectors)
    halo = deliver(plan, (t0, t1, t2, t3), second)
    halo1, halo2 = later(halo), later(halo, 2)
    inner = call(inner_second_kernel, whole, "svvv-", scratch, 16, 12 * 10**9)(
        plan, own_two, second_prev, weights, halo
    )
    out = call(
        outer_kernel,
        shape(F, H, C, W),
        "s" + "v" * 9,
        [
            pltpu.VMEM((3 * F, 4, 3 * C, W), BF),
            pltpu.VMEM((3 * F, 4, 3, C, W), BF),
            pltpu.VMEM((2 * F, 4, 3 * C, W), BF),
            pltpu.VMEM((2 * F, 4, 3, C, W), BF),
        ],
        24,
        4 * 10**9,
    )(plan, inner, record, second, second_prev, halo, halo1, halo2, weights, vectors)
    return out.transpose(0, 2, 1, 3)[None]


def solution(mesh):
    placed = (P("tile", "group", None, None, None), P(), P(), P(), P(), P(), P(), P(), P(), P())
    return jax.shard_map(
        per_device,
        mesh=mesh,
        in_specs=placed,
        out_specs=P("tile", "group", None, None, None),
        check_vma=False,
    )
```

```python
import functools

import jax
import jax.numpy as jnp
from jax import lax
from jax.experimental import pallas as pl
from jax.experimental.pallas import tpu as pltpu
from jax.sharding import PartitionSpec as P

NZ, NY, NCORE, NX = 8, 4, 2, 4
TILES = NZ * NY * NCORE
TPC = 4
C, H, W, F = 96, 16, 128, 2
REC = 5
KF = 9 * C + 32
T_LIST = 2
T_NEAR = T_LIST + TILES
T_CLIP = T_NEAR + TILES * 8
BF, F32 = jnp.bfloat16, jnp.float32

SMEM = pl.BlockSpec(memory_space=pltpu.SMEM)
VMEM = pl.BlockSpec(memory_space=pltpu.VMEM)
ANY = pl.BlockSpec(memory_space=pl.ANY)


def params(mib):
    return pltpu.CompilerParams(vmem_limit_bytes=mib * 1024 * 1024)


def sides(table):
    tile = table[T_LIST + table[0]]
    up = table[T_NEAR + tile * 8 + 1] >= 0
    left = table[T_NEAR + tile * 8 + 3] >= 0
    return up, left


def norm_silu(values, gain):
    inverse = lax.rsqrt(jnp.mean(values * values, axis=0, keepdims=True) + 1e-06)
    scaled = values * inverse * gain
    return scaled / (1.0 + jnp.exp(-scaled))


def rotate(values, by):
    return pltpu.roll(values, by, 1)


def lanes(rows):
    return lax.broadcasted_iota(jnp.int32, (rows, W), 1)


def write_record(features, up, left, out, base):
    row = jnp.where(up, 0, H - 2)
    for f in range(F):
        for r in range(2):
            out[base + 2 * f + r] = features[f, row + r]
    turn = jnp.where(left, 0, 2)
    lane = lanes(C)
    columns = jnp.zeros((C, W), F32)
    for f in range(F):
        for y in range(H):
            at = f * 32 + 2 * y
            moved = rotate(features[f, y].astype(F32), at + turn)
            columns = jnp.where(lane // 2 == at // 2, moved, columns)
    out[base + 4] = jnp.where(lane < 64, columns, rotate(columns, 64)).astype(BF)


def record_kernel(ids, tiles, near, features, out):
    tile = tiles[ids[0]]
    up, left = near[1, tile] >= 0, near[3, tile] >= 0
    write_record(features, up, left, out, 0)


def weights_kernel(one, two, _, out):
    same = lax.broadcasted_iota(jnp.int32, (C, C), 0) == lax.broadcasted_iota(jnp.int32, (C, C), 1)
    same = same.astype(F32).astype(BF)
    for n, source in enumerate((one, two)):
        out[n, 0:C, 3 * KF :] = jnp.zeros((C, KF), BF)
        out[n, C:, 0:KF] = jnp.zeros((C, KF), BF)
        for t in range(3):
            flipped = lax.dot_general(same, source[t], (((1,), (1,)), ((), ())), preferred_element_type=F32)
            flipped = jnp.concatenate([flipped.astype(BF), jnp.zeros((C, KF - 9 * C), BF)], axis=1)
            out[n, 0:C, t * KF : (t + 1) * KF] = flipped
            out[n, C:, (t + 1) * KF : (t + 2) * KF] = flipped


def plan_kernel(table, _, out, inverse):
    me = table[0]
    z, y, c = me // (NY * NCORE), (me // NCORE) % NY, me % NCORE

    def invert(i, _):
        inverse[table[T_LIST + i]] = i
        return 0

    lax.fori_loop(0, TILES, invert, 0)

    def place(tile):
        slot = inverse[jnp.maximum(tile, 0)]
        zs, ys, cs = slot // (NY * NCORE), (slot // NCORE) % NY, slot % NCORE
        away = jnp.where(c == 0, z - zs, zs - z)
        away = jnp.where(away < 0, away + NZ, away)
        label = jnp.where(cs == c, 0, 1)
        fits = (tile >= 0) & (ys == y) & ((away >= 1) & (away <= 3) | (label == 0) & ((away == 0) | (away == 4)))
        return jnp.where(fits, jnp.minimum(away, 3), -1), jnp.where(away == 4, 0, jnp.where(away == 3, 1 + label, label))

    for n in range(2 * NY):
        core = c if n < NY else 1 - c
        near = T_NEAR + table[T_LIST + z * NY * NCORE + (n % NY) * NCORE + core] * 8
        vertical = jnp.maximum(table[near + 1], table[near + 6])
        horizontal = jnp.maximum(table[near + 3], table[near + 4])
        diagonal = jnp.maximum(
            jnp.maximum(table[near], table[near + 2]), jnp.maximum(table[near + 5], table[near + 7])
        )
        for k, tile in enumerate((vertical, horizontal, diagonal)):
            which, index = place(tile)
            out[6 * n + 2 * k] = which
            out[6 * n + 2 * k + 1] = index


def select_kernel(plan, t0, t1, t2, t3, _, mine, other):
    held = (t0, t1, t2, t3)
    mine[...] = jnp.zeros_like(mine)
    other[...] = jnp.zeros_like(other)
    low = lanes(C) < 64
    for n in range(2 * NY):
        out, yd = (mine, other)[n // NY], n % NY
        for k, ref in enumerate(held):

            @pl.when(plan[6 * n] == k)
            def _():
                out[yd, 0:4] = ref[plan[6 * n + 1], 0:4]

            @pl.when(plan[6 * n + 2] == k)
            def _():
                out[yd, 4] = jnp.where(low, ref[plan[6 * n + 3], 4], out[yd, 4])

            @pl.when(plan[6 * n + 4] == k)
            def _():
                out[yd, 4] = jnp.where(low, out[yd, 4], ref[plan[6 * n + 5], 4])


def combine_kernel(table, mine, arrived, own, one, two, three):
    y = (table[0] // NCORE) % NY
    for by, out in enumerate((own, one, two, three)):
        to = (y + by) % NY
        out[...] = (mine[to].astype(F32) + arrived[to].astype(F32)).astype(BF)


def three_shifts(center, at_left, at_right):
    lane = lanes(C)
    before = jnp.where(lane == 0, at_left, rotate(center, 1))
    after = jnp.where(lane == W - 1, at_right, rotate(center, W - 1))
    return before.astype(BF), center.astype(BF), after.astype(BF)


def put_window(windows, place, values):
    for k, value in enumerate(values):
        windows[(*place, slice(k * C, (k + 1) * C))] = value


def stack(parts):
    full = []
    for part in parts:
        full += [part, jnp.zeros((KF - 9 * C, part.shape[1]), BF)]
    return jnp.concatenate(full, axis=0)


def row_parts(frames, oy, count):
    return [
        jnp.concatenate([windows[f, pl.ds(oy + r, 3)].reshape(9 * C, W) for r in range(count)], axis=1)
        for windows, f in frames
    ]


def frames_of(*windows):
    return [(ref, f) for ref in windows for f in range(F)]


def product(weights, parts):
    return jnp.dot(weights[...], stack(parts), preferred_element_type=F32)


def half_product(weights, windows, half, oy):
    return product(weights.at[:, pl.ds(half * F * KF, F * KF)], row_parts(frames_of(windows), oy, 2))


def first_windows(source, gain, exists, windows):
    zero_ends(windows)
    for f in range(F):

        def row_step(y, _):
            center = jnp.where(exists, norm_silu(source[f, y].astype(F32), gain), 0.0)
            put_window(windows, (f, y + 1), three_shifts(center, 0.0, 0.0))
            return 0

        for y in range(H):
            row_step(y, 0)


def own_first_kernel(own, weights, vectors, out, windows):
    first_windows(own, vectors[:, 1:2], True, windows)

    def rows_step(n, _):
        out[n] = half_product(weights.at[0], windows, 1, 2 * n)
        return 0

    for n in range(H // 2):
        rows_step(n, 0)


def second_windows(source, exists, windows):
    zero_ends(windows)
    for f in range(F):

        def row_step(y, _):
            center = jnp.where(exists, source[f * H + y].astype(F32), 0.0)
            put_window(windows, (f, y + 1), three_shifts(center, 0.0, 0.0))
            return 0

        for y in range(H):
            row_step(y, 0)


def own_second_kernel(own, second, weights, vectors, out, windows):
    bias = vectors[:, 3:4]
    second_windows(second, True, windows)

    def rows_step(n, _):
        acc = half_product(weights.at[1], windows, 1, 2 * n)
        for f in range(F):
            value = acc[f * C : (f + 1) * C] + bias
            for r in range(2):
                y = 2 * n + r
                out[f, y] = own[f, y].astype(F32) + value[:, r * W : (r + 1) * W]
        return 0

    for n in range(H // 2):
        rows_step(n, 0)


def inner_first_kernel(table, prev, partial, weights, vectors, _, _plan, out, windows):
    up, left = sides(table)
    bias, gain_one, gain_two = vectors[:, 0:1], vectors[:, 1:2], vectors[:, 2:3]
    write_record(prev, up, left, out, F * H)
    first_windows(prev, gain_one, table[1] > 0, windows)
    border_row, border_lane = jnp.where(up, 0, H - 1), jnp.where(left, 0, W - 1)
    lane = lanes(C)

    def rows_step(n, _):
        acc = partial[n] + half_product(weights.at[0], windows, 0, 2 * n)
        for f in range(F):
            value = norm_silu(acc[f * C : (f + 1) * C] + bias, gain_two)
            for r in range(2):
                y = 2 * n + r
                border = (lane == border_lane) | (y == border_row)
                out[f * H + y] = jnp.where(border, 0.0, value[:, r * W : (r + 1) * W]).astype(BF)
        return 0

    for n in range(H // 2):
        rows_step(n, 0)


def inner_second_kernel(table, partial, second_prev, weights, _, out, windows):
    second_windows(second_prev, table[1] > 0, windows)

    def rows_step(n, _):
        acc = half_product(weights.at[1], windows, 0, 2 * n)
        for f in range(F):
            for r in range(2):
                y = 2 * n + r
                out[f, y] = partial[f, y] + acc[f * C : (f + 1) * C, r * W : (r + 1) * W]
        return 0

    for n in range(H // 2):
        rows_step(n, 0)


def zero_ends(windows):
    for fr in range(F):
        for yy in (0, H + 1):
            windows[fr, yy] = jnp.zeros((3 * C, W), BF)


def band_parts(band, columns, base):
    parts = row_parts([(band, base + fr) for fr in range(2 * F)], 0, 2)
    for fr in range(2 * F):
        beside = [
            jnp.concatenate([columns[base + fr, j + dx, dy] for dy in range(3) for dx in range(3)], axis=0)
            for j in range(2)
        ]
        parts[fr] = jnp.concatenate([parts[fr]] + beside, axis=1)
    return parts


def put_column(columns, fr, k, value):
    columns[fr, k, 0] = rotate(value, 1).astype(BF)
    columns[fr, k, 1] = value.astype(BF)
    columns[fr, k, 2] = rotate(value, W - 1).astype(BF)


def outer_kernel(
    table, inner, record0, second_own, second_prev, halo0, halo1, halo2, weights, vectors,
    out, band1, columns1, band2, columns2
):
    up, left = sides(table)
    bias1, gain1, gain2 = vectors[:, 0:1], vectors[:, 1:2], vectors[:, 2:3]
    sources = ((second_prev, F * H, halo2), (second_own, F * H, halo1), (record0, 0, halo0))
    lane = lanes(C)

    src = lax.broadcasted_iota(jnp.int32, (W, 2 * W), 0)
    dst2 = lax.broadcasted_iota(jnp.int32, (W, 2 * W), 1)
    dst, col = dst2 % W, dst2 // W
    none = -1000
    body = jnp.where((dst >= 2) & (dst < H + 2), 2 * (dst - 2), none)
    above = jnp.where(dst < 2, 64 + 2 * (H - 2 + dst), none)
    below = jnp.where((dst >= H + 2) & (dst < H + 4), 64 + 2 * (dst - H - 2), none)
    corner = jnp.where(up, above, below)
    past = jnp.where(up, 0, H + 2)
    first_col = jnp.where(left, 0, W - 2)
    for fr in range(3 * F):
        f = fr % F
        record, base, halo = sources[fr // F]
        exists = table[1] >= 2 - fr // F
        pick = (src == jnp.maximum(body, corner) + f * 32 + col).astype(F32).astype(BF)
        theirs = jnp.dot(halo[4], pick, preferred_element_type=F32)
        theirs = norm_silu(jnp.where(exists, theirs, 0.0), gain1)
        picks = [(src == body + f * 32 + col).astype(F32).astype(BF)]
        for r in range(2):
            picks.append(((src == first_col + col) & (dst == past + r)).astype(F32).astype(BF))
        mine = jnp.concatenate([record[base + 4], halo[2 * f], halo[2 * f + 1]], axis=1)
        ours = jnp.dot(mine, jnp.concatenate(picks, axis=0), preferred_element_type=F32)
        ours = norm_silu(jnp.where(exists, ours, 0.0), gain1)
        low, high = jnp.where(left, theirs, ours), jnp.where(left, ours, theirs)
        for k in range(4):
            put_column(columns1, fr, k, (low if k < 2 else high)[:, (k % 2) * W : (k % 2 + 1) * W])
        near = jnp.where(left, theirs[:, W:], theirs[:, :W])
        for r in range(4):
            other, self = halo[2 * f + r % 2], record[base + 2 * f + r % 2]
            raw = jnp.where(up, other if r < 2 else self, self if r < 2 else other)
            at = jnp.where(up, r, H + r)
            moved = rotate(near, jnp.where(left, (W - at) % W, W - 1 - at))
            center = norm_silu(jnp.where(exists, raw.astype(F32), 0.0), gain1)
            put_window(
                band1, (fr, r), three_shifts(center, jnp.where(left, moved, 0.0), jnp.where(left, 0.0, moved))
            )

    inside = (lane >= jnp.where(up, 3, 2)) & (lane < jnp.where(up, H + 2, H + 1))
    row_at, col_at = jnp.where(up, 0, 2), jnp.where(left, 0, 2)
    for p in range(2):
        acc = product(weights.at[0], band_parts(band1, columns1, F * p))
        for f in range(F):
            s = F * p + f
            value = norm_silu(acc[f * C : (f + 1) * C] + bias1, gain2)
            if p == 0:
                value = jnp.where(table[1] > 0, value, 0.0)
            beside = [value[:, 2 * W : 3 * W], value[:, 3 * W :]]
            near = jnp.where(left, beside[0], beside[1])
            for j in range(2):
                at = jnp.where(up, 1 + j, H + 1 + j)
                moved = rotate(near, jnp.where(left, W - at, W - 1 - at))
                center = value[:, j * W : (j + 1) * W]
                put_window(
                    band2,
                    (s, row_at + j),
                    three_shifts(center, jnp.where(left, moved, 0.0), jnp.where(left, 0.0, moved)),
                )
                band2[s, 2 - row_at + j] = jnp.zeros((3 * C, W), BF)
                put_column(columns2, s, col_at + j, jnp.where(inside, beside[j], 0.0))
                columns2[s, 2 - col_at + j] = jnp.zeros((3, C, W), BF)

    length = table[T_CLIP + table[T_LIST + table[0]] // TPC]
    start = table[1] * F
    acc = product(weights.at[1], band_parts(band2, columns2, 0))
    for f in range(F):
        value = acc[f * C : (f + 1) * C]
        for y in range(H):
            total = inner[f, y]
            for j in range(2):
                at = first_col + j
                moved = rotate(value[:, (2 + j) * W : (3 + j) * W], (at + W - 2 - y) % W)
                total = total + jnp.where(lane == at, moved, 0.0)
            if y < 2:
                total = total + jnp.where(up, value[:, y * W : (y + 1) * W], 0.0)
            if y >= H - 2:
                j = y - (H - 2)
                total = total + jnp.where(up, 0.0, value[:, j * W : (j + 1) * W])
            out[f, y] = jnp.where(start + f < length, total, 0.0).astype(BF)


def call(kernel, outs, kinds, scratch=(), mib=8, flops=0):
    single = not isinstance(outs, (list, tuple))
    return pl.pallas_call(
        kernel,
        out_shape=outs,
        in_specs=[{"s": SMEM, "v": VMEM, "-": ANY}[kind] for kind in kinds],
        out_specs=VMEM if single else [VMEM] * len(outs),
        scratch_shapes=list(scratch),
        compiler_params=params(mib),
        cost_estimate=pl.CostEstimate(flops=flops, bytes_accessed=2**20, transcendentals=0),
    )


def shape(*extent):
    return jax.ShapeDtypeStruct(extent, BF)


def place_of(z, y, c):
    return (z % NZ) * NY * NCORE + (y % NY) * NCORE + c


def pairs(move):
    return [
        (place_of(z, y, c), place_of(*move(z, y, c))) for z in range(NZ) for y in range(NY) for c in range(NCORE)
    ]


def send(array, move):
    return lax.ppermute(array, "tile", pairs(move))


def later(array, by=1):
    return lax.ppermute(array, "group", [(i, (i + by) % NX) for i in range(NX)])


def spread(record):
    along = lambda by: lambda z, y, c: (z + (by if c == 0 else -by), y, c)
    t0 = jnp.stack([record, send(record, swap)])
    t1 = send(t0, along(1))
    t2 = send(t0, along(2))
    t3 = send(jnp.concatenate([t2[:1], t1], axis=0), along(2))
    return t0, t1, t2, t3


def swap(z, y, c):
    return z, y, 1 - c


def deliver(table, plan, held, after):
    mine, other = call(select_kernel, [shape(NY, REC, C, W)] * 2, "svvvv-")(plan, *held, after)
    arrived = send(other, swap)
    own, one, two, three = call(combine_kernel, [shape(REC, C, W)] * 4, "svv")(table, mine, arrived)
    total = own.astype(F32)
    for by, part in ((2, two), (1, one), (3, three)):
        total = total + send(part, lambda z, y, c, by=by: (z, y + by, c)).astype(F32)
    return total.astype(BF)


def per_device(
    features, tile_list, neighbours, clip_frames, gain_one, weight_one, bias_one, gain_two, weight_two, bias_two
):
    ids = jnp.stack([lax.axis_index("tile"), lax.axis_index("group")]).astype(jnp.int32)
    table = jnp.concatenate(
        [
            ids,
            tile_list,
            neighbours.reshape(-1),
            clip_frames,
        ]
    )
    vectors = jnp.stack([bias_one, gain_one, gain_two, bias_two], axis=1)
    own = features[0].transpose(0, 2, 1, 3)
    prev = later(own)
    record = call(record_kernel, shape(REC, C, W), "sssv")(ids, tile_list, neighbours.T, own)
    held = spread(record)
    weights = call(weights_kernel, shape(2, 2 * C, 4 * KF), "vv-", mib=16)(
        weight_one.reshape(3, 9 * C, C), weight_two.reshape(3, 9 * C, C), held[0]
    )
    plan = pl.pallas_call(
        plan_kernel,
        out_shape=jax.ShapeDtypeStruct((12 * NY,), jnp.int32),
        in_specs=[SMEM, ANY],
        out_specs=SMEM,
        scratch_shapes=[pltpu.SMEM((TILES,), jnp.int32)],
    )(table, held[0])
    scratch = [pltpu.VMEM((F, H + 2, 3 * C, W), BF)]
    own_one = call(
        own_first_kernel, jax.ShapeDtypeStruct((H // 2, 2 * C, 2 * W), F32), "vvv", scratch, 16, 3 * 10**9
    )(own, weights, vectors)
    second = call(
        inner_first_kernel, shape(F * H + REC, C, W), "svvvv-s", scratch, 16, 8 * 10**9
    )(table, prev, own_one, weights, vectors, held[1], plan)
    whole = jax.ShapeDtypeStruct((F, H, C, W), F32)
    own_two = call(own_second_kernel, whole, "vvvv", scratch, 16, 10**9)(own, second, weights, vectors)
    second_prev = later(second)
    halo = deliver(table, plan, held, second)
    halo1, halo2 = later(halo), later(halo, 2)
    inner = call(inner_second_kernel, whole, "svvv-", scratch, 16, 12 * 10**9)(
        table, own_two, second_prev, weights, halo
    )
    out = call(
        outer_kernel,
        shape(F, H, C, W),
        "s" + "v" * 9,
        [
            pltpu.VMEM((3 * F, 4, 3 * C, W), BF),
            pltpu.VMEM((3 * F, 4, 3, C, W), BF),
            pltpu.VMEM((2 * F, 4, 3 * C, W), BF),
            pltpu.VMEM((2 * F, 4, 3, C, W), BF),
        ],
        24,
        4 * 10**9,
    )(table, inner, record, second, second_prev, halo, halo1, halo2, weights, vectors)
    return out.transpose(0, 2, 1, 3)[None]


def solution(mesh):
    placed = (P("tile", "group", None, None, None), P(), P(), P(), P(), P(), P(), P(), P(), P())
    return jax.shard_map(
        per_device,
        mesh=mesh,
        in_specs=placed,
        out_specs=P("tile", "group", None, None, None),
        check_vma=False,
    )
```

```python
import functools

import jax
import jax.numpy as jnp
from jax import lax
from jax.experimental import pallas as pl
from jax.experimental.pallas import tpu as pltpu
from jax.sharding import PartitionSpec as P

NZ, NY, NCORE, NX = 8, 4, 2, 4
TILES = NZ * NY * NCORE
TPC = 4
C, H, W, F = 96, 16, 128, 2
REC = 5
KF = 9 * C + 32
T_LIST = 2
T_NEAR = T_LIST + TILES
T_CLIP = T_NEAR + TILES * 8
BF, F32 = jnp.bfloat16, jnp.float32

SMEM = pl.BlockSpec(memory_space=pltpu.SMEM)
VMEM = pl.BlockSpec(memory_space=pltpu.VMEM)
ANY = pl.BlockSpec(memory_space=pl.ANY)


def params(mib):
    return pltpu.CompilerParams(vmem_limit_bytes=mib * 1024 * 1024)


def sides(table):
    tile = table[T_LIST + table[0]]
    up = table[T_NEAR + tile * 8 + 1] >= 0
    left = table[T_NEAR + tile * 8 + 3] >= 0
    return up, left


def norm_silu(values, gain):
    inverse = lax.rsqrt(jnp.mean(values * values, axis=0, keepdims=True) + 1e-06)
    scaled = values * inverse * gain
    return scaled / (1.0 + jnp.exp(-scaled))


def rotate(values, by):
    return pltpu.roll(values, by, 1)


def lanes(rows):
    return lax.broadcasted_iota(jnp.int32, (rows, W), 1)


def write_record(features, up, left, out, base):
    row = jnp.where(up, 0, H - 2)
    for f in range(F):
        for r in range(2):
            out[base + 2 * f + r] = features[f, row + r]
    turn = jnp.where(left, 0, 2)
    lane = lanes(C)
    columns = jnp.zeros((C, W), F32)
    for f in range(F):
        for y in range(H):
            at = f * 32 + 2 * y
            moved = rotate(features[f, y].astype(F32), at + turn)
            columns = jnp.where(lane // 2 == at // 2, moved, columns)
    out[base + 4] = jnp.where(lane < 64, columns, rotate(columns, 64)).astype(BF)


def record_kernel(ids, tiles, near, features, out):
    tile = tiles[ids[0]]
    up, left = near[1, tile] >= 0, near[3, tile] >= 0
    write_record(features, up, left, out, 0)


def weights_kernel(one, two, _, out):
    same = lax.broadcasted_iota(jnp.int32, (C, C), 0) == lax.broadcasted_iota(jnp.int32, (C, C), 1)
    same = same.astype(F32).astype(BF)
    for n, source in enumerate((one, two)):
        out[n, 0:C, 3 * KF :] = jnp.zeros((C, KF), BF)
        out[n, C:, 0:KF] = jnp.zeros((C, KF), BF)
        for t in range(3):
            flipped = lax.dot_general(same, source[t], (((1,), (1,)), ((), ())), preferred_element_type=F32)
            flipped = jnp.concatenate([flipped.astype(BF), jnp.zeros((C, KF - 9 * C), BF)], axis=1)
            out[n, 0:C, t * KF : (t + 1) * KF] = flipped
            out[n, C:, (t + 1) * KF : (t + 2) * KF] = flipped


def plan_kernel(table, _, out, inverse):
    me = table[0]
    z, y, c = me // (NY * NCORE), (me // NCORE) % NY, me % NCORE

    def invert(i, _):
        inverse[table[T_LIST + i]] = i
        return 0

    lax.fori_loop(0, TILES, invert, 0)

    def place(tile):
        slot = inverse[jnp.maximum(tile, 0)]
        zs, ys, cs = slot // (NY * NCORE), (slot // NCORE) % NY, slot % NCORE
        away = jnp.where(c == 0, z - zs, zs - z)
        away = jnp.where(away < 0, away + NZ, away)
        label = jnp.where(cs == c, 0, 1)
        fits = (tile >= 0) & (ys == y) & ((away >= 1) & (away <= 3) | (label == 0) & ((away == 0) | (away == 4)))
        return jnp.where(fits, jnp.minimum(away, 3), -1), jnp.where(away == 4, 0, jnp.where(away == 3, 1 + label, label))

    for n in range(2 * NY):
        core = c if n < NY else 1 - c
        near = T_NEAR + table[T_LIST + z * NY * NCORE + (n % NY) * NCORE + core] * 8
        vertical = jnp.maximum(table[near + 1], table[near + 6])
        horizontal = jnp.maximum(table[near + 3], table[near + 4])
        diagonal = jnp.maximum(
            jnp.maximum(table[near], table[near + 2]), jnp.maximum(table[near + 5], table[near + 7])
        )
        for k, tile in enumerate((vertical, horizontal, diagonal)):
            which, index = place(tile)
            out[6 * n + 2 * k] = which
            out[6 * n + 2 * k + 1] = index


def select_kernel(plan, t0, t1, t2, t3, _, mine, other):
    held = (t0, t1, t2, t3)
    mine[...] = jnp.zeros_like(mine)
    other[...] = jnp.zeros_like(other)
    low = lanes(C) < 64
    for n in range(2 * NY):
        out, yd = (mine, other)[n // NY], n % NY
        for k, ref in enumerate(held):

            @pl.when(plan[6 * n] == k)
            def _():
                out[yd, 0:4] = ref[plan[6 * n + 1], 0:4]

            @pl.when(plan[6 * n + 2] == k)
            def _():
                out[yd, 4] = jnp.where(low, ref[plan[6 * n + 3], 4], out[yd, 4])

            @pl.when(plan[6 * n + 4] == k)
            def _():
                out[yd, 4] = jnp.where(low, out[yd, 4], ref[plan[6 * n + 5], 4])


def combine_kernel(table, mine, arrived, own, one, two, three):
    y = (table[0] // NCORE) % NY
    for by, out in enumerate((own, one, two, three)):
        to = (y + by) % NY
        out[...] = (mine[to].astype(F32) + arrived[to].astype(F32)).astype(BF)


def three_shifts(center, at_left, at_right):
    lane = lanes(C)
    before = jnp.where(lane == 0, at_left, rotate(center, 1))
    after = jnp.where(lane == W - 1, at_right, rotate(center, W - 1))
    return before.astype(BF), center.astype(BF), after.astype(BF)


def put_window(windows, place, values):
    for k, value in enumerate(values):
        windows[(*place, slice(k * C, (k + 1) * C))] = value


def stack(parts):
    full = []
    for part in parts:
        full += [part, jnp.zeros((KF - 9 * C, part.shape[1]), BF)]
    return jnp.concatenate(full, axis=0)


def row_parts(frames, oy, count):
    return [
        jnp.concatenate([windows[f, pl.ds(oy + r, 3)].reshape(9 * C, W) for r in range(count)], axis=1)
        for windows, f in frames
    ]


def frames_of(*windows):
    return [(ref, f) for ref in windows for f in range(F)]


def product(weights, parts):
    return jnp.dot(weights[...], stack(parts), preferred_element_type=F32)


def half_product(weights, windows, half, oy):
    return product(weights.at[:, pl.ds(half * F * KF, F * KF)], row_parts(frames_of(windows), oy, 2))


def first_windows(source, gain, exists, windows):
    zero_ends(windows)
    for f in range(F):

        def row_step(y, _):
            center = jnp.where(exists, norm_silu(source[f, y].astype(F32), gain), 0.0)
            put_window(windows, (f, y + 1), three_shifts(center, 0.0, 0.0))
            return 0

        for y in range(H):
            row_step(y, 0)


def own_first_kernel(own, weights, vectors, out, windows):
    first_windows(own, vectors[:, 1:2], True, windows)

    def rows_step(n, _):
        out[n] = half_product(weights.at[0], windows, 1, 2 * n)
        return 0

    for n in range(H // 2):
        rows_step(n, 0)


def second_windows(source, exists, windows):
    zero_ends(windows)
    for f in range(F):

        def row_step(y, _):
            center = jnp.where(exists, source[f * H + y].astype(F32), 0.0)
            put_window(windows, (f, y + 1), three_shifts(center, 0.0, 0.0))
            return 0

        for y in range(H):
            row_step(y, 0)


def own_second_kernel(own, second, weights, vectors, out, windows):
    bias = vectors[:, 3:4]
    second_windows(second, True, windows)

    def rows_step(n, _):
        acc = half_product(weights.at[1], windows, 1, 2 * n)
        for f in range(F):
            value = acc[f * C : (f + 1) * C] + bias
            for r in range(2):
                y = 2 * n + r
                out[f, y] = own[f, y].astype(F32) + value[:, r * W : (r + 1) * W]
        return 0

    for n in range(H // 2):
        rows_step(n, 0)


def inner_first_kernel(table, prev, partial, weights, vectors, _, _plan, out, windows):
    up, left = sides(table)
    bias, gain_one, gain_two = vectors[:, 0:1], vectors[:, 1:2], vectors[:, 2:3]
    write_record(prev, up, left, out, F * H)
    first_windows(prev, gain_one, table[1] > 0, windows)
    border_row, border_lane = jnp.where(up, 0, H - 1), jnp.where(left, 0, W - 1)
    lane = lanes(C)

    def rows_step(n, _):
        acc = partial[n] + half_product(weights.at[0], windows, 0, 2 * n)
        for f in range(F):
            value = norm_silu(acc[f * C : (f + 1) * C] + bias, gain_two)
            for r in range(2):
                y = 2 * n + r
                border = (lane == border_lane) | (y == border_row)
                out[f * H + y] = jnp.where(border, 0.0, value[:, r * W : (r + 1) * W]).astype(BF)
        return 0

    for n in range(H // 2):
        rows_step(n, 0)


def inner_second_kernel(table, partial, second_prev, weights, _, out, windows):
    second_windows(second_prev, table[1] > 0, windows)

    def rows_step(n, _):
        acc = half_product(weights.at[1], windows, 0, 2 * n)
        for f in range(F):
            for r in range(2):
                y = 2 * n + r
                out[f, y] = partial[f, y] + acc[f * C : (f + 1) * C, r * W : (r + 1) * W]
        return 0

    for n in range(H // 2):
        rows_step(n, 0)


def zero_ends(windows):
    for fr in range(F):
        for yy in (0, H + 1):
            windows[fr, yy] = jnp.zeros((3 * C, W), BF)


def band_parts(frames):
    parts = row_parts([(band, f) for band, _, f in frames], 0, 2)
    for n, (_, columns, f) in enumerate(frames):
        beside = jnp.concatenate([columns[f, dx, dy] for dy in range(3) for dx in range(3)], axis=0)
        parts[n] = jnp.concatenate([parts[n], beside], axis=1)
    return parts


def put_columns(columns, f, values):
    low = lanes(C) < 64
    for k in range(3):
        value = jnp.where(low, values[k], rotate(values[k + 1], 64))
        columns[f, k, 0] = rotate(value, 1).astype(BF)
        columns[f, k, 1] = value.astype(BF)
        columns[f, k, 2] = rotate(value, W - 1).astype(BF)


def border_windows(table, vectors, record, base, halo, exists, band, columns):
    up, left = sides(table)
    gain = vectors[:, 1:2]
    src = lax.broadcasted_iota(jnp.int32, (W, 2 * W), 0)
    dst2 = lax.broadcasted_iota(jnp.int32, (W, 2 * W), 1)
    dst, col = dst2 % W, dst2 // W
    none = -1000
    body = jnp.where((dst >= 2) & (dst < H + 2), 2 * (dst - 2), none)
    above = jnp.where(dst < 2, 64 + 2 * (H - 2 + dst), none)
    below = jnp.where((dst >= H + 2) & (dst < H + 4), 64 + 2 * (dst - H - 2), none)
    corner = jnp.where(up, above, below)
    past = jnp.where(up, 0, H + 2)
    first_col = jnp.where(left, 0, W - 2)
    for f in range(F):
        pick = (src == jnp.maximum(body, corner) + f * 32 + col).astype(F32).astype(BF)
        theirs = jnp.dot(halo[4], pick, preferred_element_type=F32)
        theirs = norm_silu(jnp.where(exists, theirs, 0.0), gain)
        picks = [(src == body + f * 32 + col).astype(F32).astype(BF)]
        for r in range(2):
            picks.append(((src == first_col + col) & (dst == past + r)).astype(F32).astype(BF))
        mine = jnp.concatenate([record[base + 4], halo[2 * f], halo[2 * f + 1]], axis=1)
        ours = jnp.dot(mine, jnp.concatenate(picks, axis=0), preferred_element_type=F32)
        ours = norm_silu(jnp.where(exists, ours, 0.0), gain)
        low, high = jnp.where(left, theirs, ours), jnp.where(left, ours, theirs)
        put_columns(columns, f, [low[:, :W], low[:, W:], high[:, :W], high[:, W:]])
        near = jnp.where(left, theirs[:, W:], theirs[:, :W])
        for r in range(4):
            other, self = halo[2 * f + r % 2], record[base + 2 * f + r % 2]
            raw = jnp.where(up, other if r < 2 else self, self if r < 2 else other)
            at = jnp.where(up, r, H + r)
            moved = rotate(near, jnp.where(left, (W - at) % W, W - 1 - at))
            center = norm_silu(jnp.where(exists, raw.astype(F32), 0.0), gain)
            put_window(
                band, (f, r), three_shifts(center, jnp.where(left, moved, 0.0), jnp.where(left, 0.0, moved))
            )


def own_border_kernel(table, record, halo, vectors, _, band, columns):
    border_windows(table, vectors, record, 0, halo, True, band, columns)


def outer_kernel(
    table, inner, band0, columns0, second_own, second_prev, halo1, halo2, weights, vectors,
    out, band1, columns1, band2, columns2, band, columns
):
    up, left = sides(table)
    bias1, gain2 = vectors[:, 0:1], vectors[:, 2:3]
    lane = lanes(C)
    first_col = jnp.where(left, 0, W - 2)
    border_windows(table, vectors, second_own, F * H, halo1, table[1] >= 1, band1, columns1)
    border_windows(table, vectors, second_prev, F * H, halo2, table[1] >= 2, band2, columns2)
    frames = [(b, c, f) for b, c in ((band2, columns2), (band1, columns1), (band0, columns0)) for f in range(F)]

    inside = (lane >= jnp.where(up, 3, 2)) & (lane < jnp.where(up, H + 2, H + 1))
    row_at = jnp.where(up, 0, 2)
    for p in range(2):
        acc = product(weights.at[0], band_parts(frames[F * p : F * p + 2 * F]))
        for f in range(F):
            s = F * p + f
            value = norm_silu(acc[f * C : (f + 1) * C] + bias1, gain2)
            if p == 0:
                value = jnp.where(table[1] > 0, value, 0.0)
            beside = [value[:, 2 * W :], rotate(value[:, 2 * W :], 64)]
            near = jnp.where(left, beside[0], beside[1])
            for j in range(2):
                at = jnp.where(up, 1 + j, H + 1 + j)
                moved = rotate(near, jnp.where(left, W - at, W - 1 - at))
                center = value[:, j * W : (j + 1) * W]
                put_window(
                    band,
                    (s, row_at + j),
                    three_shifts(center, jnp.where(left, moved, 0.0), jnp.where(left, 0.0, moved)),
                )
                band[s, 2 - row_at + j] = jnp.zeros((3 * C, W), BF)
            kept = [jnp.where(inside, b, 0.0) for b in beside]
            low, high = [jnp.where(left, k, 0.0) for k in kept], [jnp.where(left, 0.0, k) for k in kept]
            put_columns(columns, s, low + high)

    length = table[T_CLIP + table[T_LIST + table[0]] // TPC]
    start = table[1] * F
    acc = product(weights.at[1], band_parts([(band, columns, s) for s in range(2 * F)]))
    for f in range(F):
        value = acc[f * C : (f + 1) * C]
        for y in range(H):
            total = inner[f, y]
            for j in range(2):
                at = first_col + j
                moved = rotate(value[:, 2 * W :], (at + 2 * W - 64 * j - 2 - y) % W)
                total = total + jnp.where(lane == at, moved, 0.0)
            if y < 2:
                total = total + jnp.where(up, value[:, y * W : (y + 1) * W], 0.0)
            if y >= H - 2:
                j = y - (H - 2)
                total = total + jnp.where(up, 0.0, value[:, j * W : (j + 1) * W])
            out[f, y] = jnp.where(start + f < length, total, 0.0).astype(BF)


def call(kernel, outs, kinds, scratch=(), mib=8, flops=0):
    single = not isinstance(outs, (list, tuple))
    return pl.pallas_call(
        kernel,
        out_shape=outs,
        in_specs=[{"s": SMEM, "v": VMEM, "-": ANY}[kind] for kind in kinds],
        out_specs=VMEM if single else [VMEM] * len(outs),
        scratch_shapes=list(scratch),
        compiler_params=params(mib),
        cost_estimate=pl.CostEstimate(flops=flops, bytes_accessed=2**20, transcendentals=0),
    )


def shape(*extent):
    return jax.ShapeDtypeStruct(extent, BF)


def place_of(z, y, c):
    return (z % NZ) * NY * NCORE + (y % NY) * NCORE + c


def pairs(move):
    return [
        (place_of(z, y, c), place_of(*move(z, y, c))) for z in range(NZ) for y in range(NY) for c in range(NCORE)
    ]


def send(array, move):
    return lax.ppermute(array, "tile", pairs(move))


def later(array, by=1):
    return lax.ppermute(array, "group", [(i, (i + by) % NX) for i in range(NX)])


def spread(record):
    along = lambda by: lambda z, y, c: (z + (by if c == 0 else -by), y, c)
    t0 = jnp.stack([record, send(record, swap)])
    t1 = send(t0, along(1))
    t2 = send(t0, along(2))
    t3 = send(jnp.concatenate([t2[:1], t1], axis=0), along(2))
    return t0, t1, t2, t3


def swap(z, y, c):
    return z, y, 1 - c


def deliver(table, plan, held, after):
    mine, other = call(select_kernel, [shape(NY, REC, C, W)] * 2, "svvvv-")(plan, *held, after)
    arrived = send(other, swap)
    own, one, two, three = call(combine_kernel, [shape(REC, C, W)] * 4, "svv")(table, mine, arrived)
    total = own.astype(F32)
    for by, part in ((2, two), (1, one), (3, three)):
        total = total + send(part, lambda z, y, c, by=by: (z, y + by, c)).astype(F32)
    return total.astype(BF)


def per_device(
    features, tile_list, neighbours, clip_frames, gain_one, weight_one, bias_one, gain_two, weight_two, bias_two
):
    ids = jnp.stack([lax.axis_index("tile"), lax.axis_index("group")]).astype(jnp.int32)
    table = jnp.concatenate(
        [
            ids,
            tile_list,
            neighbours.reshape(-1),
            clip_frames,
        ]
    )
    vectors = jnp.stack([bias_one, gain_one, gain_two, bias_two], axis=1)
    own = features[0].transpose(0, 2, 1, 3)
    prev = later(own)
    record = call(record_kernel, shape(REC, C, W), "sssv")(ids, tile_list, neighbours.T, own)
    held = spread(record)
    weights = call(weights_kernel, shape(2, 2 * C, 4 * KF), "vv-", mib=16)(
        weight_one.reshape(3, 9 * C, C), weight_two.reshape(3, 9 * C, C), held[0]
    )
    plan = pl.pallas_call(
        plan_kernel,
        out_shape=jax.ShapeDtypeStruct((12 * NY,), jnp.int32),
        in_specs=[SMEM, ANY],
        out_specs=SMEM,
        scratch_shapes=[pltpu.SMEM((TILES,), jnp.int32)],
    )(table, held[0])
    scratch = [pltpu.VMEM((F, H + 2, 3 * C, W), BF)]
    own_one = call(
        own_first_kernel, jax.ShapeDtypeStruct((H // 2, 2 * C, 2 * W), F32), "vvv", scratch, 16, 3 * 10**9
    )(own, weights, vectors)
    second = call(
        inner_first_kernel, shape(F * H + REC, C, W), "svvvv-s", scratch, 16, 8 * 10**9
    )(table, prev, own_one, weights, vectors, held[1], plan)
    whole = jax.ShapeDtypeStruct((F, H, C, W), F32)
    own_two = call(own_second_kernel, whole, "vvvv", scratch, 16, 10**9)(own, second, weights, vectors)
    second_prev = later(second)
    halo = deliver(table, plan, held, second)
    halo1, halo2 = later(halo), later(halo, 2)
    inner = call(inner_second_kernel, whole, "svvv-", scratch, 16, 12 * 10**9)(
        table, own_two, second_prev, weights, halo
    )
    edges = [shape(F, 4, 3 * C, W), shape(F, 3, 3, C, W)]
    border0 = call(own_border_kernel, edges, "svvv-")(table, record, halo, vectors, inner)
    out = call(
        outer_kernel,
        shape(F, H, C, W),
        "s" + "v" * 9,
        [
            pltpu.VMEM((F, 4, 3 * C, W), BF),
            pltpu.VMEM((F, 3, 3, C, W), BF),
            pltpu.VMEM((F, 4, 3 * C, W), BF),
            pltpu.VMEM((F, 3, 3, C, W), BF),
            pltpu.VMEM((2 * F, 4, 3 * C, W), BF),
            pltpu.VMEM((2 * F, 3, 3, C, W), BF),
        ],
        24,
        4 * 10**9,
    )(table, inner, *border0, second, second_prev, halo1, halo2, weights, vectors)
    return out.transpose(0, 2, 1, 3)[None]


def solution(mesh):
    placed = (P("tile", "group", None, None, None), P(), P(), P(), P(), P(), P(), P(), P(), P())
    return jax.shard_map(
        per_device,
        mesh=mesh,
        in_specs=placed,
        out_specs=P("tile", "group", None, None, None),
        check_vma=False,
    )
```

```python
import functools

import jax
import jax.numpy as jnp
from jax import lax
from jax.experimental import pallas as pl
from jax.experimental.pallas import tpu as pltpu
from jax.sharding import PartitionSpec as P

NZ, NY, NCORE, NX = 8, 4, 2, 4
TILES = NZ * NY * NCORE
TPC = 4
C, H, W, F = 96, 16, 128, 2
REC = 5
KF = 9 * C + 32
T_LIST = 2
T_NEAR = T_LIST + TILES
T_CLIP = T_NEAR + TILES * 8
BF, F32 = jnp.bfloat16, jnp.float32

SMEM = pl.BlockSpec(memory_space=pltpu.SMEM)
VMEM = pl.BlockSpec(memory_space=pltpu.VMEM)
ANY = pl.BlockSpec(memory_space=pl.ANY)


def params(mib):
    return pltpu.CompilerParams(vmem_limit_bytes=mib * 1024 * 1024)


def sides(table):
    tile = table[T_LIST + table[0]]
    up = table[T_NEAR + tile * 8 + 1] >= 0
    left = table[T_NEAR + tile * 8 + 3] >= 0
    return up, left


def norm_silu(values, gain):
    inverse = lax.rsqrt(jnp.mean(values * values, axis=0, keepdims=True) + 1e-06)
    scaled = values * inverse * gain
    return scaled / (1.0 + jnp.exp(-scaled))


def rotate(values, by):
    return pltpu.roll(values, by, 1)


def lanes(rows):
    return lax.broadcasted_iota(jnp.int32, (rows, W), 1)


def write_record(features, up, left, out, base):
    row = jnp.where(up, 0, H - 2)
    for f in range(F):
        for r in range(2):
            out[base + 2 * f + r] = features[f, row + r]
    turn = jnp.where(left, 0, 2)
    lane = lanes(C)
    columns = jnp.zeros((C, W), F32)
    for f in range(F):
        for y in range(H):
            at = f * 32 + 2 * y
            moved = rotate(features[f, y].astype(F32), at + turn)
            columns = jnp.where(lane // 2 == at // 2, moved, columns)
    out[base + 4] = jnp.where(lane < 64, columns, rotate(columns, 64)).astype(BF)
    return columns


def record_kernel(ids, tiles, near, features, out, packed):
    tile = tiles[ids[0]]
    up, left = near[1, tile] >= 0, near[3, tile] >= 0
    columns = write_record(features, up, left, out, 0)
    for n in range(2 * F):
        packed[2 * n] = out[n, 0 : C // 2]
        packed[2 * n + 1] = out[n, C // 2 :]
    packed[4 * F] = jnp.where(lanes(C // 2) < 64, columns[: C // 2], rotate(columns[C // 2 :], 64)).astype(BF)


def weights_kernel(one, two, _, out):
    same = lax.broadcasted_iota(jnp.int32, (C, C), 0) == lax.broadcasted_iota(jnp.int32, (C, C), 1)
    same = same.astype(F32).astype(BF)
    for n, source in enumerate((one, two)):
        out[n, 0:C, 3 * KF :] = jnp.zeros((C, KF), BF)
        out[n, C:, 0:KF] = jnp.zeros((C, KF), BF)
        for t in range(3):
            flipped = lax.dot_general(same, source[t], (((1,), (1,)), ((), ())), preferred_element_type=F32)
            flipped = jnp.concatenate([flipped.astype(BF), jnp.zeros((C, KF - 9 * C), BF)], axis=1)
            out[n, 0:C, t * KF : (t + 1) * KF] = flipped
            out[n, C:, (t + 1) * KF : (t + 2) * KF] = flipped


def plan_kernel(table, _, out, inverse):
    me = table[0]
    z, y, c = me // (NY * NCORE), (me // NCORE) % NY, me % NCORE

    def invert(i, _):
        inverse[table[T_LIST + i]] = i
        return 0

    lax.fori_loop(0, TILES, invert, 0)

    def place(tile):
        slot = inverse[jnp.maximum(tile, 0)]
        zs, ys, cs = slot // (NY * NCORE), (slot // NCORE) % NY, slot % NCORE
        away = jnp.where(c == 0, z - zs, zs - z)
        away = jnp.where(away < 0, away + NZ, away)
        label = jnp.where(cs == c, 0, 1)
        fits = (tile >= 0) & (ys == y) & ((away >= 1) & (away <= 3) | (label == 0) & ((away == 0) | (away == 4)))
        return jnp.where(fits, jnp.minimum(away, 3), -1), jnp.where(away == 4, 0, jnp.where(away == 3, 1 + label, label))

    for n in range(2 * NY):
        core = c if n < NY else 1 - c
        near = T_NEAR + table[T_LIST + z * NY * NCORE + (n % NY) * NCORE + core] * 8
        vertical = jnp.maximum(table[near + 1], table[near + 6])
        horizontal = jnp.maximum(table[near + 3], table[near + 4])
        diagonal = jnp.maximum(
            jnp.maximum(table[near], table[near + 2]), jnp.maximum(table[near + 5], table[near + 7])
        )
        for k, tile in enumerate((vertical, horizontal, diagonal)):
            which, index = place(tile)
            out[6 * n + 2 * k] = which
            out[6 * n + 2 * k + 1] = index


def unpack_columns(block):
    values = block.astype(F32)
    turned, low = rotate(values, 64), lanes(C // 2) < 64
    both = [jnp.where(low, values, turned), jnp.where(low, turned, values)]
    return jnp.concatenate(both, axis=0).astype(BF)


def select_kernel(plan, t0, t1, t2, t3, _, mine, other):
    held = (t0, t1, t2, t3)
    mine[...] = jnp.zeros_like(mine)
    other[...] = jnp.zeros_like(other)
    low = lanes(C) < 64
    for n in range(2 * NY):
        out, yd = (mine, other)[n // NY], n % NY
        for k, ref in enumerate(held):

            @pl.when(plan[6 * n] == k)
            def _():
                for b in range(2 * F):
                    out[yd, b, 0 : C // 2] = ref[plan[6 * n + 1], 2 * b]
                    out[yd, b, C // 2 :] = ref[plan[6 * n + 1], 2 * b + 1]

            @pl.when(plan[6 * n + 2] == k)
            def _():
                out[yd, 4] = jnp.where(low, unpack_columns(ref[plan[6 * n + 3], 4 * F]), out[yd, 4])

            @pl.when(plan[6 * n + 4] == k)
            def _():
                out[yd, 4] = jnp.where(low, out[yd, 4], unpack_columns(ref[plan[6 * n + 5], 4 * F]))


def combine_kernel(table, mine, arrived, own, one, two, three):
    y = (table[0] // NCORE) % NY
    for by, out in enumerate((own, one, two, three)):
        to = (y + by) % NY
        out[...] = (mine[to].astype(F32) + arrived[to].astype(F32)).astype(BF)


def three_shifts(center, at_left, at_right):
    lane = lanes(C)
    before = jnp.where(lane == 0, at_left, rotate(center, 1))
    after = jnp.where(lane == W - 1, at_right, rotate(center, W - 1))
    return before.astype(BF), center.astype(BF), after.astype(BF)


def put_window(windows, place, values):
    for k, value in enumerate(values):
        windows[(*place, slice(k * C, (k + 1) * C))] = value


def stack(parts):
    full = []
    for part in parts:
        full += [part, jnp.zeros((KF - 9 * C, part.shape[1]), BF)]
    return jnp.concatenate(full, axis=0)


def row_parts(frames, oy, count):
    return [
        jnp.concatenate([windows[f, pl.ds(oy + r, 3)].reshape(9 * C, W) for r in range(count)], axis=1)
        for windows, f in frames
    ]


def frames_of(*windows):
    return [(ref, f) for ref in windows for f in range(F)]


def product(weights, parts):
    return jnp.dot(weights[...], stack(parts), preferred_element_type=F32)


def half_product(weights, windows, half, oy):
    return product(weights.at[:, pl.ds(half * F * KF, F * KF)], row_parts(frames_of(windows), oy, 2))


def first_windows(source, gain, exists, windows):
    zero_ends(windows)
    for f in range(F):

        def row_step(y, _):
            center = jnp.where(exists, norm_silu(source[f, y].astype(F32), gain), 0.0)
            put_window(windows, (f, y + 1), three_shifts(center, 0.0, 0.0))
            return 0

        for y in range(H):
            row_step(y, 0)


def own_first_kernel(own, weights, vectors, out, windows):
    first_windows(own, vectors[:, 1:2], True, windows)

    def rows_step(n, _):
        out[n] = half_product(weights.at[0], windows, 1, 2 * n)
        return 0

    for n in range(H // 2):
        rows_step(n, 0)


def second_windows(source, exists, windows):
    zero_ends(windows)
    for f in range(F):

        def row_step(y, _):
            center = jnp.where(exists, source[f * H + y].astype(F32), 0.0)
            put_window(windows, (f, y + 1), three_shifts(center, 0.0, 0.0))
            return 0

        for y in range(H):
            row_step(y, 0)


def own_second_kernel(own, second, weights, vectors, out, windows):
    bias = vectors[:, 3:4]
    second_windows(second, True, windows)

    def rows_step(n, _):
        acc = half_product(weights.at[1], windows, 1, 2 * n)
        for f in range(F):
            value = acc[f * C : (f + 1) * C] + bias
            for r in range(2):
                y = 2 * n + r
                out[f, y] = own[f, y].astype(F32) + value[:, r * W : (r + 1) * W]
        return 0

    for n in range(H // 2):
        rows_step(n, 0)


def inner_first_kernel(table, prev, partial, weights, vectors, _, _plan, out, windows):
    up, left = sides(table)
    bias, gain_one, gain_two = vectors[:, 0:1], vectors[:, 1:2], vectors[:, 2:3]
    write_record(prev, up, left, out, F * H)
    first_windows(prev, gain_one, table[1] > 0, windows)
    border_row, border_lane = jnp.where(up, 0, H - 1), jnp.where(left, 0, W - 1)
    lane = lanes(C)

    def rows_step(n, _):
        acc = partial[n] + half_product(weights.at[0], windows, 0, 2 * n)
        for f in range(F):
            value = norm_silu(acc[f * C : (f + 1) * C] + bias, gain_two)
            for r in range(2):
                y = 2 * n + r
                border = (lane == border_lane) | (y == border_row)
                out[f * H + y] = jnp.where(border, 0.0, value[:, r * W : (r + 1) * W]).astype(BF)
        return 0

    for n in range(H // 2):
        rows_step(n, 0)


def inner_second_kernel(table, partial, second_prev, weights, _, out, windows):
    second_windows(second_prev, table[1] > 0, windows)

    def rows_step(n, _):
        acc = half_product(weights.at[1], windows, 0, 2 * n)
        for f in range(F):
            for r in range(2):
                y = 2 * n + r
                out[f, y] = partial[f, y] + acc[f * C : (f + 1) * C, r * W : (r + 1) * W]
        return 0

    for n in range(H // 2):
        rows_step(n, 0)


def zero_ends(windows):
    for fr in range(F):
        for yy in (0, H + 1):
            windows[fr, yy] = jnp.zeros((3 * C, W), BF)


def band_parts(band, columns, base):
    parts = row_parts([(band, base + fr) for fr in range(2 * F)], 0, 2)
    for fr in range(2 * F):
        beside = [
            jnp.concatenate([columns[base + fr, j + dx, dy] for dy in range(3) for dx in range(3)], axis=0)
            for j in range(2)
        ]
        parts[fr] = jnp.concatenate([parts[fr]] + beside, axis=1)
    return parts


def put_column(columns, fr, k, value):
    columns[fr, k, 0] = rotate(value, 1).astype(BF)
    columns[fr, k, 1] = value.astype(BF)
    columns[fr, k, 2] = rotate(value, W - 1).astype(BF)


def outer_kernel(
    table, inner, record0, second_own, second_prev, halo0, halo1, halo2, weights, vectors,
    out, band1, columns1, band2, columns2
):
    up, left = sides(table)
    bias1, gain1, gain2 = vectors[:, 0:1], vectors[:, 1:2], vectors[:, 2:3]
    sources = ((second_prev, F * H, halo2), (second_own, F * H, halo1), (record0, 0, halo0))
    lane = lanes(C)

    src = lax.broadcasted_iota(jnp.int32, (W, 2 * W), 0)
    dst2 = lax.broadcasted_iota(jnp.int32, (W, 2 * W), 1)
    dst, col = dst2 % W, dst2 // W
    none = -1000
    body = jnp.where((dst >= 2) & (dst < H + 2), 2 * (dst - 2), none)
    above = jnp.where(dst < 2, 64 + 2 * (H - 2 + dst), none)
    below = jnp.where((dst >= H + 2) & (dst < H + 4), 64 + 2 * (dst - H - 2), none)
    corner = jnp.where(up, above, below)
    past = jnp.where(up, 0, H + 2)
    first_col = jnp.where(left, 0, W - 2)
    for fr in range(3 * F):
        f = fr % F
        record, base, halo = sources[fr // F]
        exists = table[1] >= 2 - fr // F
        pick = (src == jnp.maximum(body, corner) + f * 32 + col).astype(F32).astype(BF)
        theirs = jnp.dot(halo[4], pick, preferred_element_type=F32)
        theirs = norm_silu(jnp.where(exists, theirs, 0.0), gain1)
        picks = [(src == body + f * 32 + col).astype(F32).astype(BF)]
        for r in range(2):
            picks.append(((src == first_col + col) & (dst == past + r)).astype(F32).astype(BF))
        mine = jnp.concatenate([record[base + 4], halo[2 * f], halo[2 * f + 1]], axis=1)
        ours = jnp.dot(mine, jnp.concatenate(picks, axis=0), preferred_element_type=F32)
        ours = norm_silu(jnp.where(exists, ours, 0.0), gain1)
        low, high = jnp.where(left, theirs, ours), jnp.where(left, ours, theirs)
        for k in range(4):
            put_column(columns1, fr, k, (low if k < 2 else high)[:, (k % 2) * W : (k % 2 + 1) * W])
        near = jnp.where(left, theirs[:, W:], theirs[:, :W])
        for r in range(4):
            other, self = halo[2 * f + r % 2], record[base + 2 * f + r % 2]
            raw = jnp.where(up, other if r < 2 else self, self if r < 2 else other)
            at = jnp.where(up, r, H + r)
            moved = rotate(near, jnp.where(left, (W - at) % W, W - 1 - at))
            center = norm_silu(jnp.where(exists, raw.astype(F32), 0.0), gain1)
            put_window(
                band1, (fr, r), three_shifts(center, jnp.where(left, moved, 0.0), jnp.where(left, 0.0, moved))
            )

    inside = (lane >= jnp.where(up, 3, 2)) & (lane < jnp.where(up, H + 2, H + 1))
    row_at, col_at = jnp.where(up, 0, 2), jnp.where(left, 0, 2)
    for p in range(2):
        acc = product(weights.at[0], band_parts(band1, columns1, F * p))
        for f in range(F):
            s = F * p + f
            value = norm_silu(acc[f * C : (f + 1) * C] + bias1, gain2)
            if p == 0:
                value = jnp.where(table[1] > 0, value, 0.0)
            beside = [value[:, 2 * W : 3 * W], value[:, 3 * W :]]
            near = jnp.where(left, beside[0], beside[1])
            for j in range(2):
                at = jnp.where(up, 1 + j, H + 1 + j)
                moved = rotate(near, jnp.where(left, W - at, W - 1 - at))
                center = value[:, j * W : (j + 1) * W]
                put_window(
                    band2,
                    (s, row_at + j),
                    three_shifts(center, jnp.where(left, moved, 0.0), jnp.where(left, 0.0, moved)),
                )
                band2[s, 2 - row_at + j] = jnp.zeros((3 * C, W), BF)
                put_column(columns2, s, col_at + j, jnp.where(inside, beside[j], 0.0))
                columns2[s, 2 - col_at + j] = jnp.zeros((3, C, W), BF)

    length = table[T_CLIP + table[T_LIST + table[0]] // TPC]
    start = table[1] * F
    acc = product(weights.at[1], band_parts(band2, columns2, 0))
    for f in range(F):
        value = acc[f * C : (f + 1) * C]
        for y in range(H):
            total = inner[f, y]
            for j in range(2):
                at = first_col + j
                moved = rotate(value[:, (2 + j) * W : (3 + j) * W], (at + W - 2 - y) % W)
                total = total + jnp.where(lane == at, moved, 0.0)
            if y < 2:
                total = total + jnp.where(up, value[:, y * W : (y + 1) * W], 0.0)
            if y >= H - 2:
                j = y - (H - 2)
                total = total + jnp.where(up, 0.0, value[:, j * W : (j + 1) * W])
            out[f, y] = jnp.where(start + f < length, total, 0.0).astype(BF)


def call(kernel, outs, kinds, scratch=(), mib=8, flops=0):
    single = not isinstance(outs, (list, tuple))
    return pl.pallas_call(
        kernel,
        out_shape=outs,
        in_specs=[{"s": SMEM, "v": VMEM, "-": ANY}[kind] for kind in kinds],
        out_specs=VMEM if single else [VMEM] * len(outs),
        scratch_shapes=list(scratch),
        compiler_params=params(mib),
        cost_estimate=pl.CostEstimate(flops=flops, bytes_accessed=2**20, transcendentals=0),
    )


def shape(*extent):
    return jax.ShapeDtypeStruct(extent, BF)


def place_of(z, y, c):
    return (z % NZ) * NY * NCORE + (y % NY) * NCORE + c


def pairs(move):
    return [
        (place_of(z, y, c), place_of(*move(z, y, c))) for z in range(NZ) for y in range(NY) for c in range(NCORE)
    ]


def send(array, move):
    return lax.ppermute(array, "tile", pairs(move))


def later(array, by=1):
    return lax.ppermute(array, "group", [(i, (i + by) % NX) for i in range(NX)])


def spread(record):
    along = lambda by: lambda z, y, c: (z + (by if c == 0 else -by), y, c)
    t0 = jnp.stack([record, send(record, swap)])
    t1 = send(t0, along(1))
    t2 = send(t0, along(2))
    t3 = send(jnp.concatenate([t2[:1], t1], axis=0), along(2))
    return t0, t1, t2, t3


def swap(z, y, c):
    return z, y, 1 - c


def deliver(table, plan, held, after):
    mine, other = call(select_kernel, [shape(NY, REC, C, W)] * 2, "svvvv-")(plan, *held, after)
    arrived = send(other, swap)
    own, one, two, three = call(combine_kernel, [shape(REC, C, W)] * 4, "svv")(table, mine, arrived)
    total = own.astype(F32)
    for by, part in ((2, two), (1, one), (3, three)):
        total = total + send(part, lambda z, y, c, by=by: (z, y + by, c)).astype(F32)
    return total.astype(BF)


def per_device(
    features, tile_list, neighbours, clip_frames, gain_one, weight_one, bias_one, gain_two, weight_two, bias_two
):
    ids = jnp.stack([lax.axis_index("tile"), lax.axis_index("group")]).astype(jnp.int32)
    table = jnp.concatenate(
        [
            ids,
            tile_list,
            neighbours.reshape(-1),
            clip_frames,
        ]
    )
    vectors = jnp.stack([bias_one, gain_one, gain_two, bias_two], axis=1)
    own = features[0].transpose(0, 2, 1, 3)
    prev = later(own)
    record, packed = call(record_kernel, [shape(REC, C, W), shape(4 * F + 1, C // 2, W)], "sssv")(ids, tile_list, neighbours.T, own)
    held = spread(packed)
    weights = call(weights_kernel, shape(2, 2 * C, 4 * KF), "vv-", mib=16)(
        weight_one.reshape(3, 9 * C, C), weight_two.reshape(3, 9 * C, C), held[0]
    )
    plan = pl.pallas_call(
        plan_kernel,
        out_shape=jax.ShapeDtypeStruct((12 * NY,), jnp.int32),
        in_specs=[SMEM, ANY],
        out_specs=SMEM,
        scratch_shapes=[pltpu.SMEM((TILES,), jnp.int32)],
    )(table, held[0])
    scratch = [pltpu.VMEM((F, H + 2, 3 * C, W), BF)]
    own_one = call(
        own_first_kernel, jax.ShapeDtypeStruct((H // 2, 2 * C, 2 * W), F32), "vvv", scratch, 16, 3 * 10**9
    )(own, weights, vectors)
    second = call(
        inner_first_kernel, shape(F * H + REC, C, W), "svvvv-s", scratch, 16, 8 * 10**9
    )(table, prev, own_one, weights, vectors, held[1], plan)
    whole = jax.ShapeDtypeStruct((F, H, C, W), F32)
    own_two = call(own_second_kernel, whole, "vvvv", scratch, 16, 10**9)(own, second, weights, vectors)
    second_prev = later(second)
    halo = deliver(table, plan, held, second)
    halo1, halo2 = later(halo), later(halo, 2)
    inner = call(inner_second_kernel, whole, "svvv-", scratch, 16, 12 * 10**9)(
        table, own_two, second_prev, weights, halo
    )
    out = call(
        outer_kernel,
        shape(F, H, C, W),
        "s" + "v" * 9,
        [
            pltpu.VMEM((3 * F, 4, 3 * C, W), BF),
            pltpu.VMEM((3 * F, 4, 3, C, W), BF),
            pltpu.VMEM((2 * F, 4, 3 * C, W), BF),
            pltpu.VMEM((2 * F, 4, 3, C, W), BF),
        ],
        24,
        4 * 10**9,
    )(table, inner, record, second, second_prev, halo, halo1, halo2, weights, vectors)
    return out.transpose(0, 2, 1, 3)[None]


def solution(mesh):
    placed = (P("tile", "group", None, None, None), P(), P(), P(), P(), P(), P(), P(), P(), P())
    return jax.shard_map(
        per_device,
        mesh=mesh,
        in_specs=placed,
        out_specs=P("tile", "group", None, None, None),
        check_vma=False,
    )
```

```python
import functools

import jax
import jax.numpy as jnp
from jax import lax
from jax.experimental import pallas as pl
from jax.experimental.pallas import tpu as pltpu
from jax.sharding import PartitionSpec as P

NZ, NY, NCORE, NX = 8, 4, 2, 4
TILES = NZ * NY * NCORE
TPC = 4
C, H, W, F = 96, 16, 128, 2
REC = 5
KF = 9 * C + 32
T_LIST = 2
T_NEAR = T_LIST + TILES
T_CLIP = T_NEAR + TILES * 8
BF, F32 = jnp.bfloat16, jnp.float32

SMEM = pl.BlockSpec(memory_space=pltpu.SMEM)
VMEM = pl.BlockSpec(memory_space=pltpu.VMEM)
ANY = pl.BlockSpec(memory_space=pl.ANY)


def params(mib):
    return pltpu.CompilerParams(vmem_limit_bytes=mib * 1024 * 1024)


def sides(table):
    tile = table[T_LIST + table[0]]
    up = table[T_NEAR + tile * 8 + 1] >= 0
    left = table[T_NEAR + tile * 8 + 3] >= 0
    return up, left


def norm_silu(values, gain):
    inverse = lax.rsqrt(jnp.mean(values * values, axis=0, keepdims=True) + 1e-06)
    scaled = values * inverse * gain
    return scaled / (1.0 + jnp.exp(-scaled))


def rotate(values, by):
    return pltpu.roll(values, by, 1)


def lanes(rows):
    return lax.broadcasted_iota(jnp.int32, (rows, W), 1)


def write_record(features, up, left, out, base):
    row = jnp.where(up, 0, H - 2)
    for f in range(F):
        for r in range(2):
            out[base + 2 * f + r] = features[f, row + r]
    turn = jnp.where(left, 0, 2)
    lane = lanes(C)
    columns = jnp.zeros((C, W), F32)
    for f in range(F):
        for y in range(H):
            at = f * 32 + 2 * y
            moved = rotate(features[f, y].astype(F32), at + turn)
            columns = jnp.where(lane // 2 == at // 2, moved, columns)
    out[base + 4] = jnp.where(lane < 64, columns, rotate(columns, 64)).astype(BF)
    return columns


def record_kernel(ids, tiles, near, features, out, packed):
    tile = tiles[ids[0]]
    up, left = near[1, tile] >= 0, near[3, tile] >= 0
    columns = write_record(features, up, left, out, 0)
    for n in range(2 * F):
        packed[2 * n] = out[n, 0 : C // 2]
        packed[2 * n + 1] = out[n, C // 2 :]
    packed[4 * F] = jnp.where(lanes(C // 2) < 64, columns[: C // 2], rotate(columns[C // 2 :], 64)).astype(BF)


def weights_kernel(one, two, _, out):
    same = lax.broadcasted_iota(jnp.int32, (C, C), 0) == lax.broadcasted_iota(jnp.int32, (C, C), 1)
    same = same.astype(F32).astype(BF)
    for n, source in enumerate((one, two)):
        out[n, 0:C, 3 * KF :] = jnp.zeros((C, KF), BF)
        out[n, C:, 0:KF] = jnp.zeros((C, KF), BF)
        for t in range(3):
            flipped = lax.dot_general(same, source[t], (((1,), (1,)), ((), ())), preferred_element_type=F32)
            flipped = jnp.concatenate([flipped.astype(BF), jnp.zeros((C, KF - 9 * C), BF)], axis=1)
            out[n, 0:C, t * KF : (t + 1) * KF] = flipped
            out[n, C:, (t + 1) * KF : (t + 2) * KF] = flipped


def plan_kernel(table, _, out, inverse):
    me = table[0]
    z, y, c = me // (NY * NCORE), (me // NCORE) % NY, me % NCORE

    def invert(i, _):
        inverse[table[T_LIST + i]] = i
        return 0

    lax.fori_loop(0, TILES, invert, 0)

    def place(tile):
        slot = inverse[jnp.maximum(tile, 0)]
        zs, ys, cs = slot // (NY * NCORE), (slot // NCORE) % NY, slot % NCORE
        away = jnp.where(c == 0, z - zs, zs - z)
        away = jnp.where(away < 0, away + NZ, away)
        label = jnp.where(cs == c, 0, 1)
        fits = (tile >= 0) & (ys == y) & ((away >= 1) & (away <= 3) | (label == 0) & ((away == 0) | (away == 4)))
        return jnp.where(fits, jnp.minimum(away, 3), -1), jnp.where(away == 4, 0, jnp.where(away == 3, 1 + label, label))

    for n in range(2 * NY):
        core = c if n < NY else 1 - c
        near = T_NEAR + table[T_LIST + z * NY * NCORE + (n % NY) * NCORE + core] * 8
        vertical = jnp.maximum(table[near + 1], table[near + 6])
        horizontal = jnp.maximum(table[near + 3], table[near + 4])
        diagonal = jnp.maximum(
            jnp.maximum(table[near], table[near + 2]), jnp.maximum(table[near + 5], table[near + 7])
        )
        for k, tile in enumerate((vertical, horizontal, diagonal)):
            which, index = place(tile)
            out[6 * n + 2 * k] = which
            out[6 * n + 2 * k + 1] = index


def unpack_columns(block):
    values = block.astype(F32)
    turned, low = rotate(values, 64), lanes(C // 2) < 64
    both = [jnp.where(low, values, turned), jnp.where(low, turned, values)]
    return jnp.concatenate(both, axis=0).astype(BF)


def select_kernel(first, plan, t0, t1, t2, t3, _, out):
    held = (t0, t1, t2, t3)
    out[...] = jnp.zeros_like(out)
    low = lanes(C) < 64
    for yd in range(NY):
        n = first + yd
        for k, ref in enumerate(held):

            @pl.when(plan[6 * n] == k)
            def _():
                for b in range(2 * F):
                    out[yd, b, 0 : C // 2] = ref[plan[6 * n + 1], 2 * b]
                    out[yd, b, C // 2 :] = ref[plan[6 * n + 1], 2 * b + 1]

            @pl.when(plan[6 * n + 2] == k)
            def _():
                out[yd, 4] = jnp.where(low, unpack_columns(ref[plan[6 * n + 3], 4 * F]), out[yd, 4])

            @pl.when(plan[6 * n + 4] == k)
            def _():
                out[yd, 4] = jnp.where(low, out[yd, 4], unpack_columns(ref[plan[6 * n + 5], 4 * F]))


def combine_kernel(table, mine, arrived, own, one, two, three):
    y = (table[0] // NCORE) % NY
    for by, out in enumerate((own, one, two, three)):
        to = (y + by) % NY
        out[...] = (mine[to].astype(F32) + arrived[to].astype(F32)).astype(BF)


def three_shifts(center, at_left, at_right):
    lane = lanes(C)
    before = jnp.where(lane == 0, at_left, rotate(center, 1))
    after = jnp.where(lane == W - 1, at_right, rotate(center, W - 1))
    return before.astype(BF), center.astype(BF), after.astype(BF)


def put_window(windows, place, values):
    for k, value in enumerate(values):
        windows[(*place, slice(k * C, (k + 1) * C))] = value


def stack(parts):
    full = []
    for part in parts:
        full += [part, jnp.zeros((KF - 9 * C, part.shape[1]), BF)]
    return jnp.concatenate(full, axis=0)


def row_parts(frames, oy, count):
    return [
        jnp.concatenate([windows[f, pl.ds(oy + r, 3)].reshape(9 * C, W) for r in range(count)], axis=1)
        for windows, f in frames
    ]


def frames_of(*windows):
    return [(ref, f) for ref in windows for f in range(F)]


def product(weights, parts):
    return jnp.dot(weights[...], stack(parts), preferred_element_type=F32)


def half_product(weights, windows, half, oy):
    return product(weights.at[:, pl.ds(half * F * KF, F * KF)], row_parts(frames_of(windows), oy, 2))


def first_windows(source, gain, exists, windows):
    zero_ends(windows)
    for f in range(F):

        def row_step(y, _):
            center = jnp.where(exists, norm_silu(source[f, y].astype(F32), gain), 0.0)
            put_window(windows, (f, y + 1), three_shifts(center, 0.0, 0.0))
            return 0

        for y in range(H):
            row_step(y, 0)


def own_first_kernel(own, weights, vectors, out, windows):
    first_windows(own, vectors[:, 1:2], True, windows)

    def rows_step(n, _):
        out[n] = half_product(weights.at[0], windows, 1, 2 * n)
        return 0

    for n in range(H // 2):
        rows_step(n, 0)


def second_windows(source, exists, windows):
    zero_ends(windows)
    for f in range(F):

        def row_step(y, _):
            center = jnp.where(exists, source[f * H + y].astype(F32), 0.0)
            put_window(windows, (f, y + 1), three_shifts(center, 0.0, 0.0))
            return 0

        for y in range(H):
            row_step(y, 0)


def own_second_kernel(own, second, weights, vectors, out, windows):
    bias = vectors[:, 3:4]
    second_windows(second, True, windows)

    def rows_step(n, _):
        acc = half_product(weights.at[1], windows, 1, 2 * n)
        for f in range(F):
            value = acc[f * C : (f + 1) * C] + bias
            for r in range(2):
                y = 2 * n + r
                out[f, y] = own[f, y].astype(F32) + value[:, r * W : (r + 1) * W]
        return 0

    for n in range(H // 2):
        rows_step(n, 0)


def inner_first_kernel(table, prev, partial, weights, vectors, _, _plan, out, windows):
    up, left = sides(table)
    bias, gain_one, gain_two = vectors[:, 0:1], vectors[:, 1:2], vectors[:, 2:3]
    write_record(prev, up, left, out, F * H)
    first_windows(prev, gain_one, table[1] > 0, windows)
    border_row, border_lane = jnp.where(up, 0, H - 1), jnp.where(left, 0, W - 1)
    lane = lanes(C)

    def rows_step(n, _):
        acc = partial[n] + half_product(weights.at[0], windows, 0, 2 * n)
        for f in range(F):
            value = norm_silu(acc[f * C : (f + 1) * C] + bias, gain_two)
            for r in range(2):
                y = 2 * n + r
                border = (lane == border_lane) | (y == border_row)
                out[f * H + y] = jnp.where(border, 0.0, value[:, r * W : (r + 1) * W]).astype(BF)
        return 0

    for n in range(H // 2):
        rows_step(n, 0)


def inner_second_kernel(table, partial, second_prev, weights, _, out, windows):
    second_windows(second_prev, table[1] > 0, windows)

    def rows_step(n, _):
        acc = half_product(weights.at[1], windows, 0, 2 * n)
        for f in range(F):
            for r in range(2):
                y = 2 * n + r
                out[f, y] = partial[f, y] + acc[f * C : (f + 1) * C, r * W : (r + 1) * W]
        return 0

    for n in range(H // 2):
        rows_step(n, 0)


def zero_ends(windows):
    for fr in range(F):
        for yy in (0, H + 1):
            windows[fr, yy] = jnp.zeros((3 * C, W), BF)


def band_parts(band, columns, base):
    parts = row_parts([(band, base + fr) for fr in range(2 * F)], 0, 2)
    for fr in range(2 * F):
        beside = [
            jnp.concatenate([columns[base + fr, j + dx, dy] for dy in range(3) for dx in range(3)], axis=0)
            for j in range(2)
        ]
        parts[fr] = jnp.concatenate([parts[fr]] + beside, axis=1)
    return parts


def put_column(columns, fr, k, value):
    columns[fr, k, 0] = rotate(value, 1).astype(BF)
    columns[fr, k, 1] = value.astype(BF)
    columns[fr, k, 2] = rotate(value, W - 1).astype(BF)


def outer_kernel(
    table, inner, record0, second_own, second_prev, halo0, halo1, halo2, weights, vectors,
    out, band1, columns1, band2, columns2
):
    up, left = sides(table)
    bias1, gain1, gain2 = vectors[:, 0:1], vectors[:, 1:2], vectors[:, 2:3]
    sources = ((second_prev, F * H, halo2), (second_own, F * H, halo1), (record0, 0, halo0))
    lane = lanes(C)

    src = lax.broadcasted_iota(jnp.int32, (W, 2 * W), 0)
    dst2 = lax.broadcasted_iota(jnp.int32, (W, 2 * W), 1)
    dst, col = dst2 % W, dst2 // W
    none = -1000
    body = jnp.where((dst >= 2) & (dst < H + 2), 2 * (dst - 2), none)
    above = jnp.where(dst < 2, 64 + 2 * (H - 2 + dst), none)
    below = jnp.where((dst >= H + 2) & (dst < H + 4), 64 + 2 * (dst - H - 2), none)
    corner = jnp.where(up, above, below)
    past = jnp.where(up, 0, H + 2)
    first_col = jnp.where(left, 0, W - 2)
    for fr in range(3 * F):
        f = fr % F
        record, base, halo = sources[fr // F]
        exists = table[1] >= 2 - fr // F
        pick = (src == jnp.maximum(body, corner) + f * 32 + col).astype(F32).astype(BF)
        theirs = jnp.dot(halo[4], pick, preferred_element_type=F32)
        theirs = norm_silu(jnp.where(exists, theirs, 0.0), gain1)
        picks = [(src == body + f * 32 + col).astype(F32).astype(BF)]
        for r in range(2):
            picks.append(((src == first_col + col) & (dst == past + r)).astype(F32).astype(BF))
        mine = jnp.concatenate([record[base + 4], halo[2 * f], halo[2 * f + 1]], axis=1)
        ours = jnp.dot(mine, jnp.concatenate(picks, axis=0), preferred_element_type=F32)
        ours = norm_silu(jnp.where(exists, ours, 0.0), gain1)
        low, high = jnp.where(left, theirs, ours), jnp.where(left, ours, theirs)
        for k in range(4):
            put_column(columns1, fr, k, (low if k < 2 else high)[:, (k % 2) * W : (k % 2 + 1) * W])
        near = jnp.where(left, theirs[:, W:], theirs[:, :W])
        for r in range(4):
            other, self = halo[2 * f + r % 2], record[base + 2 * f + r % 2]
            raw = jnp.where(up, other if r < 2 else self, self if r < 2 else other)
            at = jnp.where(up, r, H + r)
            moved = rotate(near, jnp.where(left, (W - at) % W, W - 1 - at))
            center = norm_silu(jnp.where(exists, raw.astype(F32), 0.0), gain1)
            put_window(
                band1, (fr, r), three_shifts(center, jnp.where(left, moved, 0.0), jnp.where(left, 0.0, moved))
            )

    inside = (lane >= jnp.where(up, 3, 2)) & (lane < jnp.where(up, H + 2, H + 1))
    row_at, col_at = jnp.where(up, 0, 2), jnp.where(left, 0, 2)
    for p in range(2):
        acc = product(weights.at[0], band_parts(band1, columns1, F * p))
        for f in range(F):
            s = F * p + f
            value = norm_silu(acc[f * C : (f + 1) * C] + bias1, gain2)
            if p == 0:
                value = jnp.where(table[1] > 0, value, 0.0)
            beside = [value[:, 2 * W : 3 * W], value[:, 3 * W :]]
            near = jnp.where(left, beside[0], beside[1])
            for j in range(2):
                at = jnp.where(up, 1 + j, H + 1 + j)
                moved = rotate(near, jnp.where(left, W - at, W - 1 - at))
                center = value[:, j * W : (j + 1) * W]
                put_window(
                    band2,
                    (s, row_at + j),
                    three_shifts(center, jnp.where(left, moved, 0.0), jnp.where(left, 0.0, moved)),
                )
                band2[s, 2 - row_at + j] = jnp.zeros((3 * C, W), BF)
                put_column(columns2, s, col_at + j, jnp.where(inside, beside[j], 0.0))
                columns2[s, 2 - col_at + j] = jnp.zeros((3, C, W), BF)

    length = table[T_CLIP + table[T_LIST + table[0]] // TPC]
    start = table[1] * F
    acc = product(weights.at[1], band_parts(band2, columns2, 0))
    for f in range(F):
        value = acc[f * C : (f + 1) * C]
        for y in range(H):
            total = inner[f, y]
            for j in range(2):
                at = first_col + j
                moved = rotate(value[:, (2 + j) * W : (3 + j) * W], (at + W - 2 - y) % W)
                total = total + jnp.where(lane == at, moved, 0.0)
            if y < 2:
                total = total + jnp.where(up, value[:, y * W : (y + 1) * W], 0.0)
            if y >= H - 2:
                j = y - (H - 2)
                total = total + jnp.where(up, 0.0, value[:, j * W : (j + 1) * W])
            out[f, y] = jnp.where(start + f < length, total, 0.0).astype(BF)


def call(kernel, outs, kinds, scratch=(), mib=8, flops=0):
    single = not isinstance(outs, (list, tuple))
    return pl.pallas_call(
        kernel,
        out_shape=outs,
        in_specs=[{"s": SMEM, "v": VMEM, "-": ANY}[kind] for kind in kinds],
        out_specs=VMEM if single else [VMEM] * len(outs),
        scratch_shapes=list(scratch),
        compiler_params=params(mib),
        cost_estimate=pl.CostEstimate(flops=flops, bytes_accessed=2**20, transcendentals=0),
    )


def shape(*extent):
    return jax.ShapeDtypeStruct(extent, BF)


def place_of(z, y, c):
    return (z % NZ) * NY * NCORE + (y % NY) * NCORE + c


def pairs(move):
    return [
        (place_of(z, y, c), place_of(*move(z, y, c))) for z in range(NZ) for y in range(NY) for c in range(NCORE)
    ]


def send(array, move):
    return lax.ppermute(array, "tile", pairs(move))


def later(array, by=1):
    return lax.ppermute(array, "group", [(i, (i + by) % NX) for i in range(NX)])


def spread(record):
    along = lambda by: lambda z, y, c: (z + (by if c == 0 else -by), y, c)
    t0 = jnp.stack([record, send(record, swap)])
    t1 = send(t0, along(1))
    t2 = send(t0, along(2))
    t3 = send(jnp.concatenate([t2[:1], t1], axis=0), along(2))
    return t0, t1, t2, t3


def swap(z, y, c):
    return z, y, 1 - c


def deliver(table, plan, held, after):
    other = call(functools.partial(select_kernel, NY), shape(NY, REC, C, W), "svvvv-")(plan, *held, after)
    arrived = send(other, swap)
    mine = call(functools.partial(select_kernel, 0), shape(NY, REC, C, W), "svvvv-")(plan, *held, other)
    own, one, two, three = call(combine_kernel, [shape(REC, C, W)] * 4, "svv")(table, mine, arrived)
    total = own.astype(F32)
    for by, part in ((2, two), (1, one), (3, three)):
        total = total + send(part, lambda z, y, c, by=by: (z, y + by, c)).astype(F32)
    return total.astype(BF)


def per_device(
    features, tile_list, neighbours, clip_frames, gain_one, weight_one, bias_one, gain_two, weight_two, bias_two
):
    ids = jnp.stack([lax.axis_index("tile"), lax.axis_index("group")]).astype(jnp.int32)
    table = jnp.concatenate(
        [
            ids,
            tile_list,
            neighbours.reshape(-1),
            clip_frames,
        ]
    )
    vectors = jnp.stack([bias_one, gain_one, gain_two, bias_two], axis=1)
    own = features[0].transpose(0, 2, 1, 3)
    prev = later(own)
    record, packed = call(record_kernel, [shape(REC, C, W), shape(4 * F + 1, C // 2, W)], "sssv")(ids, tile_list, neighbours.T, own)
    held = spread(packed)
    weights = call(weights_kernel, shape(2, 2 * C, 4 * KF), "vv-", mib=16)(
        weight_one.reshape(3, 9 * C, C), weight_two.reshape(3, 9 * C, C), held[0]
    )
    plan = pl.pallas_call(
        plan_kernel,
        out_shape=jax.ShapeDtypeStruct((12 * NY,), jnp.int32),
        in_specs=[SMEM, ANY],
        out_specs=SMEM,
        scratch_shapes=[pltpu.SMEM((TILES,), jnp.int32)],
    )(table, held[0])
    scratch = [pltpu.VMEM((F, H + 2, 3 * C, W), BF)]
    own_one = call(
        own_first_kernel, jax.ShapeDtypeStruct((H // 2, 2 * C, 2 * W), F32), "vvv", scratch, 16, 3 * 10**9
    )(own, weights, vectors)
    second = call(
        inner_first_kernel, shape(F * H + REC, C, W), "svvvv-s", scratch, 16, 8 * 10**9
    )(table, prev, own_one, weights, vectors, held[1], plan)
    whole = jax.ShapeDtypeStruct((F, H, C, W), F32)
    own_two = call(own_second_kernel, whole, "vvvv", scratch, 16, 10**9)(own, second, weights, vectors)
    second_prev = later(second)
    halo = deliver(table, plan, held, second)
    halo1, halo2 = later(halo), later(halo, 2)
    inner = call(inner_second_kernel, whole, "svvv-", scratch, 16, 12 * 10**9)(
        table, own_two, second_prev, weights, halo
    )
    out = call(
        outer_kernel,
        shape(F, H, C, W),
        "s" + "v" * 9,
        [
            pltpu.VMEM((3 * F, 4, 3 * C, W), BF),
            pltpu.VMEM((3 * F, 4, 3, C, W), BF),
            pltpu.VMEM((2 * F, 4, 3 * C, W), BF),
            pltpu.VMEM((2 * F, 4, 3, C, W), BF),
        ],
        24,
        4 * 10**9,
    )(table, inner, record, second, second_prev, halo, halo1, halo2, weights, vectors)
    return out.transpose(0, 2, 1, 3)[None]


def solution(mesh):
    placed = (P("tile", "group", None, None, None), P(), P(), P(), P(), P(), P(), P(), P(), P())
    return jax.shard_map(
        per_device,
        mesh=mesh,
        in_specs=placed,
        out_specs=P("tile", "group", None, None, None),
        check_vma=False,
    )
```

```python
import functools

import jax
import jax.numpy as jnp
from jax import lax
from jax.experimental import pallas as pl
from jax.experimental.pallas import tpu as pltpu
from jax.sharding import PartitionSpec as P

NZ, NY, NCORE, NX = 8, 4, 2, 4
TILES = NZ * NY * NCORE
TPC = 4
C, H, W, F = 96, 16, 128, 2
REC = 5
KF = 9 * C + 32
T_LIST = 2
T_NEAR = T_LIST + TILES
T_CLIP = T_NEAR + TILES * 8
BF, F32 = jnp.bfloat16, jnp.float32

SMEM = pl.BlockSpec(memory_space=pltpu.SMEM)
VMEM = pl.BlockSpec(memory_space=pltpu.VMEM)
ANY = pl.BlockSpec(memory_space=pl.ANY)


def params(mib):
    return pltpu.CompilerParams(vmem_limit_bytes=mib * 1024 * 1024)


def sides(table):
    tile = table[T_LIST + table[0]]
    up = table[T_NEAR + tile * 8 + 1] >= 0
    left = table[T_NEAR + tile * 8 + 3] >= 0
    return up, left


def norm_silu(values, gain):
    inverse = lax.rsqrt(jnp.mean(values * values, axis=0, keepdims=True) + 1e-06)
    scaled = values * inverse * gain
    return scaled / (1.0 + jnp.exp(-scaled))


def rotate(values, by):
    return pltpu.roll(values, by, 1)


def lanes(rows):
    return lax.broadcasted_iota(jnp.int32, (rows, W), 1)


def write_record(features, up, left, out, base):
    row = jnp.where(up, 0, H - 2)
    for f in range(F):
        for r in range(2):
            out[base + 2 * f + r] = features[f, row + r]
    turn = jnp.where(left, 0, 2)
    lane = lanes(C)
    columns = jnp.zeros((C, W), F32)
    for f in range(F):
        for y in range(H):
            at = f * 32 + 2 * y
            moved = rotate(features[f, y].astype(F32), at + turn)
            columns = jnp.where(lane // 2 == at // 2, moved, columns)
    out[base + 4] = jnp.where(lane < 64, columns, rotate(columns, 64)).astype(BF)
    return columns


def record_kernel(ids, tiles, near, features, out, packed):
    tile = tiles[ids[0]]
    up, left = near[1, tile] >= 0, near[3, tile] >= 0
    columns = write_record(features, up, left, out, 0)
    for n in range(2 * F):
        packed[2 * n] = out[n, 0 : C // 2]
        packed[2 * n + 1] = out[n, C // 2 :]
    packed[4 * F] = jnp.where(lanes(C // 2) < 64, columns[: C // 2], rotate(columns[C // 2 :], 64)).astype(BF)


def weights_kernel(one, two, _, out):
    same = lax.broadcasted_iota(jnp.int32, (C, C), 0) == lax.broadcasted_iota(jnp.int32, (C, C), 1)
    same = same.astype(F32).astype(BF)
    for n, source in enumerate((one, two)):
        out[n, 0:C, 3 * KF :] = jnp.zeros((C, KF), BF)
        out[n, C:, 0:KF] = jnp.zeros((C, KF), BF)
        for t in range(3):
            flipped = lax.dot_general(same, source[t], (((1,), (1,)), ((), ())), preferred_element_type=F32)
            flipped = jnp.concatenate([flipped.astype(BF), jnp.zeros((C, KF - 9 * C), BF)], axis=1)
            out[n, 0:C, t * KF : (t + 1) * KF] = flipped
            out[n, C:, (t + 1) * KF : (t + 2) * KF] = flipped


def plan_kernel(table, _, out, inverse):
    me = table[0]
    z, y, c = me // (NY * NCORE), (me // NCORE) % NY, me % NCORE

    def invert(i, _):
        inverse[table[T_LIST + i]] = i
        return 0

    lax.fori_loop(0, TILES, invert, 0)

    def place(tile):
        slot = inverse[jnp.maximum(tile, 0)]
        zs, ys, cs = slot // (NY * NCORE), (slot // NCORE) % NY, slot % NCORE
        away = jnp.where(c == 0, z - zs, zs - z)
        away = jnp.where(away < 0, away + NZ, away)
        label = jnp.where(cs == c, 0, 1)
        fits = (tile >= 0) & (ys == y) & ((away >= 1) & (away <= 3) | (label == 0) & ((away == 0) | (away == 4)))
        return jnp.where(fits, jnp.minimum(away, 3), -1), jnp.where(away == 4, 0, jnp.where(away == 3, 1 + label, label))

    for n in range(2 * NY):
        core = c if n < NY else 1 - c
        near = T_NEAR + table[T_LIST + z * NY * NCORE + (n % NY) * NCORE + core] * 8
        vertical = jnp.maximum(table[near + 1], table[near + 6])
        horizontal = jnp.maximum(table[near + 3], table[near + 4])
        diagonal = jnp.maximum(
            jnp.maximum(table[near], table[near + 2]), jnp.maximum(table[near + 5], table[near + 7])
        )
        for k, tile in enumerate((vertical, horizontal, diagonal)):
            which, index = place(tile)
            out[6 * n + 2 * k] = which
            out[6 * n + 2 * k + 1] = index


def unpack_columns(block):
    values = block.astype(F32)
    turned, low = rotate(values, 64), lanes(C // 2) < 64
    both = [jnp.where(low, values, turned), jnp.where(low, turned, values)]
    return jnp.concatenate(both, axis=0).astype(BF)


def select_kernel(first, plan, t0, t1, t2, t3, _, out):
    held = (t0, t1, t2, t3)
    out[...] = jnp.zeros_like(out)
    low = lanes(C) < 64
    for yd in range(NY):
        n = first + yd
        for k, ref in enumerate(held):

            @pl.when(plan[6 * n] == k)
            def _():
                for b in range(2 * F):
                    out[yd, b, 0 : C // 2] = ref[plan[6 * n + 1], 2 * b]
                    out[yd, b, C // 2 :] = ref[plan[6 * n + 1], 2 * b + 1]

            @pl.when(plan[6 * n + 2] == k)
            def _():
                out[yd, 4] = jnp.where(low, unpack_columns(ref[plan[6 * n + 3], 4 * F]), out[yd, 4])

            @pl.when(plan[6 * n + 4] == k)
            def _():
                out[yd, 4] = jnp.where(low, out[yd, 4], unpack_columns(ref[plan[6 * n + 5], 4 * F]))


def combine_kernel(table, mine, arrived, own, one, two, three):
    y = (table[0] // NCORE) % NY
    for by, out in enumerate((own, one, two, three)):
        to = (y + by) % NY
        out[...] = (mine[to].astype(F32) + arrived[to].astype(F32)).astype(BF)


def three_shifts(center, at_left, at_right):
    lane = lanes(C)
    before = jnp.where(lane == 0, at_left, rotate(center, 1))
    after = jnp.where(lane == W - 1, at_right, rotate(center, W - 1))
    return before.astype(BF), center.astype(BF), after.astype(BF)


def put_window(windows, place, values):
    for k, value in enumerate(values):
        windows[(*place, slice(k * C, (k + 1) * C))] = value


def stack(parts):
    full = []
    for part in parts:
        full += [part, jnp.zeros((KF - 9 * C, part.shape[1]), BF)]
    return jnp.concatenate(full, axis=0)


def row_parts(frames, oy, count):
    return [
        jnp.concatenate([windows[f, pl.ds(oy + r, 3)].reshape(9 * C, W) for r in range(count)], axis=1)
        for windows, f in frames
    ]


def frames_of(*windows):
    return [(ref, f) for ref in windows for f in range(F)]


def product(weights, parts):
    return jnp.dot(weights[...], stack(parts), preferred_element_type=F32)


def half_product(weights, windows, half, oy):
    return product(weights.at[:, pl.ds(half * F * KF, F * KF)], row_parts(frames_of(windows), oy, 2))


def first_windows(source, gain, exists, windows):
    zero_ends(windows)
    for f in range(F):

        def row_step(y, _):
            center = jnp.where(exists, norm_silu(source[f, y].astype(F32), gain), 0.0)
            put_window(windows, (f, y + 1), three_shifts(center, 0.0, 0.0))
            return 0

        for y in range(H):
            row_step(y, 0)


def own_first_kernel(own, weights, vectors, out, windows):
    first_windows(own, vectors[:, 1:2], True, windows)

    def rows_step(n, _):
        out[n] = half_product(weights.at[0], windows, 1, 2 * n)
        return 0

    for n in range(H // 2):
        rows_step(n, 0)


def second_windows(source, exists, windows):
    zero_ends(windows)
    for f in range(F):

        def row_step(y, _):
            center = jnp.where(exists, source[f * H + y].astype(F32), 0.0)
            put_window(windows, (f, y + 1), three_shifts(center, 0.0, 0.0))
            return 0

        for y in range(H):
            row_step(y, 0)


def own_second_kernel(own, second, weights, vectors, out, windows):
    bias = vectors[:, 3:4]
    second_windows(second, True, windows)

    def rows_step(n, _):
        acc = half_product(weights.at[1], windows, 1, 2 * n)
        for f in range(F):
            value = acc[f * C : (f + 1) * C] + bias
            for r in range(2):
                y = 2 * n + r
                out[f, y] = own[f, y].astype(F32) + value[:, r * W : (r + 1) * W]
        return 0

    for n in range(H // 2):
        rows_step(n, 0)


def inner_first_kernel(table, prev, partial, weights, vectors, _, _plan, out, windows):
    up, left = sides(table)
    bias, gain_one, gain_two = vectors[:, 0:1], vectors[:, 1:2], vectors[:, 2:3]
    write_record(prev, up, left, out, F * H)
    first_windows(prev, gain_one, table[1] > 0, windows)
    border_row, border_lane = jnp.where(up, 0, H - 1), jnp.where(left, 0, W - 1)
    lane = lanes(C)

    def rows_step(n, _):
        acc = partial[n] + half_product(weights.at[0], windows, 0, 2 * n)
        for f in range(F):
            value = norm_silu(acc[f * C : (f + 1) * C] + bias, gain_two)
            for r in range(2):
                y = 2 * n + r
                border = (lane == border_lane) | (y == border_row)
                out[f * H + y] = jnp.where(border, 0.0, value[:, r * W : (r + 1) * W]).astype(BF)
        return 0

    for n in range(H // 2):
        rows_step(n, 0)


def inner_second_kernel(table, partial, second_prev, weights, _, out, windows):
    second_windows(second_prev, table[1] > 0, windows)

    def rows_step(n, _):
        acc = half_product(weights.at[1], windows, 0, 2 * n)
        for f in range(F):
            for r in range(2):
                y = 2 * n + r
                out[f, y] = partial[f, y] + acc[f * C : (f + 1) * C, r * W : (r + 1) * W]
        return 0

    for n in range(H // 2):
        rows_step(n, 0)


def zero_ends(windows):
    for fr in range(F):
        for yy in (0, H + 1):
            windows[fr, yy] = jnp.zeros((3 * C, W), BF)


def band_parts(frames):
    parts = row_parts([(band, f) for band, _, f in frames], 0, 2)
    for n, (_, columns, f) in enumerate(frames):
        beside = [
            jnp.concatenate([columns[f, j + dx, dy] for dy in range(3) for dx in range(3)], axis=0)
            for j in range(2)
        ]
        parts[n] = jnp.concatenate([parts[n]] + beside, axis=1)
    return parts


def put_column(columns, fr, k, value):
    columns[fr, k, 0] = rotate(value, 1).astype(BF)
    columns[fr, k, 1] = value.astype(BF)
    columns[fr, k, 2] = rotate(value, W - 1).astype(BF)


def border_windows(table, vectors, record, base, halo, exists, band, columns):
    up, left = sides(table)
    gain = vectors[:, 1:2]
    src = lax.broadcasted_iota(jnp.int32, (W, 2 * W), 0)
    dst2 = lax.broadcasted_iota(jnp.int32, (W, 2 * W), 1)
    dst, col = dst2 % W, dst2 // W
    none = -1000
    body = jnp.where((dst >= 2) & (dst < H + 2), 2 * (dst - 2), none)
    above = jnp.where(dst < 2, 64 + 2 * (H - 2 + dst), none)
    below = jnp.where((dst >= H + 2) & (dst < H + 4), 64 + 2 * (dst - H - 2), none)
    corner = jnp.where(up, above, below)
    past = jnp.where(up, 0, H + 2)
    first_col = jnp.where(left, 0, W - 2)
    for f in range(F):
        pick = (src == jnp.maximum(body, corner) + f * 32 + col).astype(F32).astype(BF)
        theirs = jnp.dot(halo[4], pick, preferred_element_type=F32)
        theirs = norm_silu(jnp.where(exists, theirs, 0.0), gain)
        picks = [(src == body + f * 32 + col).astype(F32).astype(BF)]
        for r in range(2):
            picks.append(((src == first_col + col) & (dst == past + r)).astype(F32).astype(BF))
        mine = jnp.concatenate([record[base + 4], halo[2 * f], halo[2 * f + 1]], axis=1)
        ours = jnp.dot(mine, jnp.concatenate(picks, axis=0), preferred_element_type=F32)
        ours = norm_silu(jnp.where(exists, ours, 0.0), gain)
        low, high = jnp.where(left, theirs, ours), jnp.where(left, ours, theirs)
        for k in range(4):
            put_column(columns, f, k, (low if k < 2 else high)[:, (k % 2) * W : (k % 2 + 1) * W])
        near = jnp.where(left, theirs[:, W:], theirs[:, :W])
        for r in range(4):
            other, self = halo[2 * f + r % 2], record[base + 2 * f + r % 2]
            raw = jnp.where(up, other if r < 2 else self, self if r < 2 else other)
            at = jnp.where(up, r, H + r)
            moved = rotate(near, jnp.where(left, (W - at) % W, W - 1 - at))
            center = norm_silu(jnp.where(exists, raw.astype(F32), 0.0), gain)
            put_window(
                band, (f, r), three_shifts(center, jnp.where(left, moved, 0.0), jnp.where(left, 0.0, moved))
            )

def own_border_kernel(table, record, halo, vectors, _, band, columns):
    border_windows(table, vectors, record, 0, halo, True, band, columns)


def outer_kernel(
    table, inner, band0, columns0, second_own, second_prev, halo1, halo2, weights, vectors,
    out, band1, columns1, bandp, columnsp, band2, columns2
):
    up, left = sides(table)
    bias1, gain2 = vectors[:, 0:1], vectors[:, 2:3]
    lane = lanes(C)
    first_col = jnp.where(left, 0, W - 2)
    border_windows(table, vectors, second_own, F * H, halo1, table[1] >= 1, band1, columns1)
    border_windows(table, vectors, second_prev, F * H, halo2, table[1] >= 2, bandp, columnsp)
    frames = [(b, c, f) for b, c in ((bandp, columnsp), (band1, columns1), (band0, columns0)) for f in range(F)]

    inside = (lane >= jnp.where(up, 3, 2)) & (lane < jnp.where(up, H + 2, H + 1))
    row_at, col_at = jnp.where(up, 0, 2), jnp.where(left, 0, 2)
    for p in range(2):
        acc = product(weights.at[0], band_parts(frames[F * p : F * p + 2 * F]))
        for f in range(F):
            s = F * p + f
            value = norm_silu(acc[f * C : (f + 1) * C] + bias1, gain2)
            if p == 0:
                value = jnp.where(table[1] > 0, value, 0.0)
            beside = [value[:, 2 * W : 3 * W], value[:, 3 * W :]]
            near = jnp.where(left, beside[0], beside[1])
            for j in range(2):
                at = jnp.where(up, 1 + j, H + 1 + j)
                moved = rotate(near, jnp.where(left, W - at, W - 1 - at))
                center = value[:, j * W : (j + 1) * W]
                put_window(
                    band2,
                    (s, row_at + j),
                    three_shifts(center, jnp.where(left, moved, 0.0), jnp.where(left, 0.0, moved)),
                )
                band2[s, 2 - row_at + j] = jnp.zeros((3 * C, W), BF)
                put_column(columns2, s, col_at + j, jnp.where(inside, beside[j], 0.0))
                columns2[s, 2 - col_at + j] = jnp.zeros((3, C, W), BF)

    length = table[T_CLIP + table[T_LIST + table[0]] // TPC]
    start = table[1] * F
    acc = product(weights.at[1], band_parts([(band2, columns2, s) for s in range(2 * F)]))
    for f in range(F):
        value = acc[f * C : (f + 1) * C]
        for y in range(H):
            total = inner[f, y]
            for j in range(2):
                at = first_col + j
                moved = rotate(value[:, (2 + j) * W : (3 + j) * W], (at + W - 2 - y) % W)
                total = total + jnp.where(lane == at, moved, 0.0)
            if y < 2:
                total = total + jnp.where(up, value[:, y * W : (y + 1) * W], 0.0)
            if y >= H - 2:
                j = y - (H - 2)
                total = total + jnp.where(up, 0.0, value[:, j * W : (j + 1) * W])
            out[f, y] = jnp.where(start + f < length, total, 0.0).astype(BF)


def call(kernel, outs, kinds, scratch=(), mib=8, flops=0):
    single = not isinstance(outs, (list, tuple))
    return pl.pallas_call(
        kernel,
        out_shape=outs,
        in_specs=[{"s": SMEM, "v": VMEM, "-": ANY}[kind] for kind in kinds],
        out_specs=VMEM if single else [VMEM] * len(outs),
        scratch_shapes=list(scratch),
        compiler_params=params(mib),
        cost_estimate=pl.CostEstimate(flops=flops, bytes_accessed=2**20, transcendentals=0),
    )


def shape(*extent):
    return jax.ShapeDtypeStruct(extent, BF)


def place_of(z, y, c):
    return (z % NZ) * NY * NCORE + (y % NY) * NCORE + c


def pairs(move):
    return [
        (place_of(z, y, c), place_of(*move(z, y, c))) for z in range(NZ) for y in range(NY) for c in range(NCORE)
    ]


def send(array, move):
    return lax.ppermute(array, "tile", pairs(move))


def later(array, by=1):
    return lax.ppermute(array, "group", [(i, (i + by) % NX) for i in range(NX)])


def spread(record):
    along = lambda by: lambda z, y, c: (z + (by if c == 0 else -by), y, c)
    t0 = jnp.stack([record, send(record, swap)])
    t1 = send(t0, along(1))
    t2 = send(t0, along(2))
    t3 = send(jnp.concatenate([t2[:1], t1], axis=0), along(2))
    return t0, t1, t2, t3


def swap(z, y, c):
    return z, y, 1 - c


def deliver(table, plan, held, after):
    other = call(functools.partial(select_kernel, NY), shape(NY, REC, C, W), "svvvv-")(plan, *held, after)
    arrived = send(other, swap)
    mine = call(functools.partial(select_kernel, 0), shape(NY, REC, C, W), "svvvv-")(plan, *held, other)
    own, one, two, three = call(combine_kernel, [shape(REC, C, W)] * 4, "svv")(table, mine, arrived)
    total = own.astype(F32)
    for by, part in ((2, two), (1, one), (3, three)):
        total = total + send(part, lambda z, y, c, by=by: (z, y + by, c)).astype(F32)
    return total.astype(BF)


def per_device(
    features, tile_list, neighbours, clip_frames, gain_one, weight_one, bias_one, gain_two, weight_two, bias_two
):
    ids = jnp.stack([lax.axis_index("tile"), lax.axis_index("group")]).astype(jnp.int32)
    table = jnp.concatenate(
        [
            ids,
            tile_list,
            neighbours.reshape(-1),
            clip_frames,
        ]
    )
    vectors = jnp.stack([bias_one, gain_one, gain_two, bias_two], axis=1)
    own = features[0].transpose(0, 2, 1, 3)
    prev = later(own)
    record, packed = call(record_kernel, [shape(REC, C, W), shape(4 * F + 1, C // 2, W)], "sssv")(ids, tile_list, neighbours.T, own)
    held = spread(packed)
    weights = call(weights_kernel, shape(2, 2 * C, 4 * KF), "vv-", mib=16)(
        weight_one.reshape(3, 9 * C, C), weight_two.reshape(3, 9 * C, C), held[0]
    )
    plan = pl.pallas_call(
        plan_kernel,
        out_shape=jax.ShapeDtypeStruct((12 * NY,), jnp.int32),
        in_specs=[SMEM, ANY],
        out_specs=SMEM,
        scratch_shapes=[pltpu.SMEM((TILES,), jnp.int32)],
    )(table, held[0])
    scratch = [pltpu.VMEM((F, H + 2, 3 * C, W), BF)]
    own_one = call(
        own_first_kernel, jax.ShapeDtypeStruct((H // 2, 2 * C, 2 * W), F32), "vvv", scratch, 16, 3 * 10**9
    )(own, weights, vectors)
    second = call(
        inner_first_kernel, shape(F * H + REC, C, W), "svvvv-s", scratch, 16, 8 * 10**9
    )(table, prev, own_one, weights, vectors, held[1], plan)
    whole = jax.ShapeDtypeStruct((F, H, C, W), F32)
    own_two = call(own_second_kernel, whole, "vvvv", scratch, 16, 10**9)(own, second, weights, vectors)
    second_prev = later(second)
    halo = deliver(table, plan, held, second)
    halo1, halo2 = later(halo), later(halo, 2)
    inner = call(inner_second_kernel, whole, "svvv-", scratch, 16, 12 * 10**9)(
        table, own_two, second_prev, weights, halo
    )
    edges = [shape(F, 4, 3 * C, W), shape(F, 4, 3, C, W)]
    border0 = call(own_border_kernel, edges, "svvv-")(table, record, halo, vectors, inner)
    out = call(
        outer_kernel,
        shape(F, H, C, W),
        "s" + "v" * 9,
        [pltpu.VMEM(edge.shape, BF) for edge in edges] * 2
        + [pltpu.VMEM((2 * F, 4, 3 * C, W), BF), pltpu.VMEM((2 * F, 4, 3, C, W), BF)],
        24,
        4 * 10**9,
    )(table, inner, *border0, second, second_prev, halo1, halo2, weights, vectors)
    return out.transpose(0, 2, 1, 3)[None]


def solution(mesh):
    placed = (P("tile", "group", None, None, None), P(), P(), P(), P(), P(), P(), P(), P(), P())
    return jax.shard_map(
        per_device,
        mesh=mesh,
        in_specs=placed,
        out_specs=P("tile", "group", None, None, None),
        check_vma=False,
    )
```

```python
import functools

import jax
import jax.numpy as jnp
from jax import lax
from jax.experimental import pallas as pl
from jax.experimental.pallas import tpu as pltpu
from jax.sharding import PartitionSpec as P

NZ, NY, NCORE, NX = 8, 4, 2, 4
TILES = NZ * NY * NCORE
TPC = 4
C, H, W, F = 96, 16, 128, 2
REC = 5
KF = 9 * C + 32
T_LIST = 2
T_NEAR = T_LIST + TILES
T_CLIP = T_NEAR + TILES * 8
BF, F32 = jnp.bfloat16, jnp.float32

SMEM = pl.BlockSpec(memory_space=pltpu.SMEM)
VMEM = pl.BlockSpec(memory_space=pltpu.VMEM)
ANY = pl.BlockSpec(memory_space=pl.ANY)


def params(mib):
    return pltpu.CompilerParams(vmem_limit_bytes=mib * 1024 * 1024)


def sides(table):
    tile = table[T_LIST + table[0]]
    up = table[T_NEAR + tile * 8 + 1] >= 0
    left = table[T_NEAR + tile * 8 + 3] >= 0
    return up, left


def norm_silu(values, gain):
    inverse = lax.rsqrt(jnp.mean(values * values, axis=0, keepdims=True) + 1e-06)
    scaled = values * inverse * gain
    return scaled / (1.0 + jnp.exp(-scaled))


def rotate(values, by):
    return pltpu.roll(values, by, 1)


def lanes(rows):
    return lax.broadcasted_iota(jnp.int32, (rows, W), 1)


def write_record(features, up, left, out, base):
    row = jnp.where(up, 0, H - 2)
    for f in range(F):
        for r in range(2):
            out[base + 2 * f + r] = features[f, row + r]
    turn = jnp.where(left, 0, 2)
    lane = lanes(C)
    columns = jnp.zeros((C, W), F32)
    for f in range(F):
        for y in range(H):
            at = f * 32 + 2 * y
            moved = rotate(features[f, y].astype(F32), at + turn)
            columns = jnp.where(lane // 2 == at // 2, moved, columns)
    out[base + 4] = jnp.where(lane < 64, columns, rotate(columns, 64)).astype(BF)
    return columns


def record_kernel(ids, tiles, near, features, out, packed):
    tile = tiles[ids[0]]
    up, left = near[1, tile] >= 0, near[3, tile] >= 0
    columns = write_record(features, up, left, out, 0)
    for n in range(2 * F):
        packed[2 * n] = out[n, 0 : C // 2]
        packed[2 * n + 1] = out[n, C // 2 :]
    packed[4 * F] = jnp.where(lanes(C // 2) < 64, columns[: C // 2], rotate(columns[C // 2 :], 64)).astype(BF)


def weights_kernel(one, two, _, out):
    same = lax.broadcasted_iota(jnp.int32, (C, C), 0) == lax.broadcasted_iota(jnp.int32, (C, C), 1)
    same = same.astype(F32).astype(BF)
    for n, source in enumerate((one, two)):
        out[n, 0:C, 3 * KF :] = jnp.zeros((C, KF), BF)
        out[n, C:, 0:KF] = jnp.zeros((C, KF), BF)
        for t in range(3):
            flipped = lax.dot_general(same, source[t], (((1,), (1,)), ((), ())), preferred_element_type=F32)
            flipped = jnp.concatenate([flipped.astype(BF), jnp.zeros((C, KF - 9 * C), BF)], axis=1)
            out[n, 0:C, t * KF : (t + 1) * KF] = flipped
            out[n, C:, (t + 1) * KF : (t + 2) * KF] = flipped


def plan_kernel(table, _, out, inverse):
    me = table[0]
    z, y, c = me // (NY * NCORE), (me // NCORE) % NY, me % NCORE

    def invert(i, _):
        inverse[table[T_LIST + i]] = i
        return 0

    lax.fori_loop(0, TILES, invert, 0)

    def place(tile):
        slot = inverse[jnp.maximum(tile, 0)]
        zs, ys, cs = slot // (NY * NCORE), (slot // NCORE) % NY, slot % NCORE
        away = jnp.where(c == 0, z - zs, zs - z)
        away = jnp.where(away < 0, away + NZ, away)
        label = jnp.where(cs == c, 0, 1)
        fits = (tile >= 0) & (ys == y) & ((away >= 1) & (away <= 3) | (label == 0) & ((away == 0) | (away == 4)))
        return jnp.where(fits, jnp.minimum(away, 3), -1), jnp.where(away == 4, 0, jnp.where(away == 3, 1 + label, label))

    for n in range(2 * NY):
        core = c if n < NY else 1 - c
        near = T_NEAR + table[T_LIST + z * NY * NCORE + (n % NY) * NCORE + core] * 8
        vertical = jnp.maximum(table[near + 1], table[near + 6])
        horizontal = jnp.maximum(table[near + 3], table[near + 4])
        diagonal = jnp.maximum(
            jnp.maximum(table[near], table[near + 2]), jnp.maximum(table[near + 5], table[near + 7])
        )
        for k, tile in enumerate((vertical, horizontal, diagonal)):
            which, index = place(tile)
            out[6 * n + 2 * k] = which
            out[6 * n + 2 * k + 1] = index


def unpack_columns(block):
    values = block.astype(F32)
    turned, low = rotate(values, 64), lanes(C // 2) < 64
    both = [jnp.where(low, values, turned), jnp.where(low, turned, values)]
    return jnp.concatenate(both, axis=0).astype(BF)


def select_kernel(first, plan, t0, t1, t2, t3, _, out):
    held = (t0, t1, t2, t3)
    out[...] = jnp.zeros_like(out)
    low = lanes(C) < 64
    for yd in range(NY):
        n = first + yd
        for k, ref in enumerate(held):

            @pl.when(plan[6 * n] == k)
            def _():
                for b in range(2 * F):
                    out[yd, b, 0 : C // 2] = ref[plan[6 * n + 1], 2 * b]
                    out[yd, b, C // 2 :] = ref[plan[6 * n + 1], 2 * b + 1]

            @pl.when(plan[6 * n + 2] == k)
            def _():
                out[yd, 4] = jnp.where(low, unpack_columns(ref[plan[6 * n + 3], 4 * F]), out[yd, 4])

            @pl.when(plan[6 * n + 4] == k)
            def _():
                out[yd, 4] = jnp.where(low, out[yd, 4], unpack_columns(ref[plan[6 * n + 5], 4 * F]))


def combine_kernel(table, mine, arrived, own, one, two, three):
    y = (table[0] // NCORE) % NY
    for by, out in enumerate((own, one, two, three)):
        to = (y + by) % NY
        out[...] = (mine[to].astype(F32) + arrived[to].astype(F32)).astype(BF)


def three_shifts(center, at_left, at_right):
    lane = lanes(C)
    before = jnp.where(lane == 0, at_left, rotate(center, 1))
    after = jnp.where(lane == W - 1, at_right, rotate(center, W - 1))
    return before.astype(BF), center.astype(BF), after.astype(BF)


def put_window(windows, place, values):
    for k, value in enumerate(values):
        windows[(*place, slice(k * C, (k + 1) * C))] = value


def stack(parts):
    full = []
    for part in parts:
        full += [part, jnp.zeros((KF - 9 * C, part.shape[1]), BF)]
    return jnp.concatenate(full, axis=0)


def row_parts(frames, oy, count):
    return [
        jnp.concatenate([windows[f, pl.ds(oy + r, 3)].reshape(9 * C, W) for r in range(count)], axis=1)
        for windows, f in frames
    ]


def frames_of(*windows):
    return [(ref, f) for ref in windows for f in range(F)]


def product(weights, parts):
    return jnp.dot(weights[...], stack(parts), preferred_element_type=F32)


def half_product(weights, windows, half, oy):
    return product(weights.at[:, pl.ds(half * F * KF, F * KF)], row_parts(frames_of(windows), oy, 2))


def first_windows(source, gain, exists, windows):
    zero_ends(windows)
    for f in range(F):

        def row_step(y, _):
            center = jnp.where(exists, norm_silu(source[f, y].astype(F32), gain), 0.0)
            put_window(windows, (f, y + 1), three_shifts(center, 0.0, 0.0))
            return 0

        for y in range(H):
            row_step(y, 0)


def own_first_kernel(own, weights, vectors, out, windows):
    first_windows(own, vectors[:, 1:2], True, windows)

    def rows_step(n, _):
        out[n] = half_product(weights.at[0], windows, 1, 2 * n)
        return 0

    for n in range(H // 2):
        rows_step(n, 0)


def second_windows(source, exists, windows):
    zero_ends(windows)
    for f in range(F):

        def row_step(y, _):
            center = jnp.where(exists, source[f * H + y].astype(F32), 0.0)
            put_window(windows, (f, y + 1), three_shifts(center, 0.0, 0.0))
            return 0

        for y in range(H):
            row_step(y, 0)


def own_second_kernel(own, second, weights, vectors, out, windows):
    bias = vectors[:, 3:4]
    second_windows(second, True, windows)

    def rows_step(n, _):
        acc = half_product(weights.at[1], windows, 1, 2 * n)
        for f in range(F):
            value = acc[f * C : (f + 1) * C] + bias
            for r in range(2):
                y = 2 * n + r
                out[f, y] = own[f, y].astype(F32) + value[:, r * W : (r + 1) * W]
        return 0

    for n in range(H // 2):
        rows_step(n, 0)


def inner_first_kernel(table, prev, partial, weights, vectors, _, _plan, out, windows):
    up, left = sides(table)
    bias, gain_one, gain_two = vectors[:, 0:1], vectors[:, 1:2], vectors[:, 2:3]
    write_record(prev, up, left, out, F * H)
    first_windows(prev, gain_one, table[1] > 0, windows)
    border_row, border_lane = jnp.where(up, 0, H - 1), jnp.where(left, 0, W - 1)
    lane = lanes(C)

    def rows_step(n, _):
        acc = partial[n] + half_product(weights.at[0], windows, 0, 2 * n)
        for f in range(F):
            value = norm_silu(acc[f * C : (f + 1) * C] + bias, gain_two)
            for r in range(2):
                y = 2 * n + r
                border = (lane == border_lane) | (y == border_row)
                out[f * H + y] = jnp.where(border, 0.0, value[:, r * W : (r + 1) * W]).astype(BF)
        return 0

    for n in range(H // 2):
        rows_step(n, 0)


def inner_second_kernel(table, partial, second_prev, weights, _, out, windows):
    second_windows(second_prev, table[1] > 0, windows)

    def rows_step(n, _):
        acc = half_product(weights.at[1], windows, 0, 2 * n)
        for f in range(F):
            for r in range(2):
                y = 2 * n + r
                out[f, y] = partial[f, y] + acc[f * C : (f + 1) * C, r * W : (r + 1) * W]
        return 0

    for n in range(H // 2):
        rows_step(n, 0)


def zero_ends(windows):
    for fr in range(F):
        for yy in (0, H + 1):
            windows[fr, yy] = jnp.zeros((3 * C, W), BF)


def band_parts(frames):
    parts = row_parts([(band, f) for band, _, f in frames], 0, 2)
    for n, (_, columns, f) in enumerate(frames):
        beside = [
            jnp.concatenate([columns[f, j + dx, dy] for dy in range(3) for dx in range(3)], axis=0)
            for j in range(2)
        ]
        parts[n] = jnp.concatenate([parts[n]] + beside, axis=1)
    return parts


def put_column(columns, fr, k, value):
    columns[fr, k, 0] = rotate(value, 1).astype(BF)
    columns[fr, k, 1] = value.astype(BF)
    columns[fr, k, 2] = rotate(value, W - 1).astype(BF)


def border_windows(table, vectors, record, base, halo, exists, band, columns):
    up, left = sides(table)
    gain = vectors[:, 1:2]
    src = lax.broadcasted_iota(jnp.int32, (W, 2 * W), 0)
    dst2 = lax.broadcasted_iota(jnp.int32, (W, 2 * W), 1)
    dst, col = dst2 % W, dst2 // W
    none = -1000
    body = jnp.where((dst >= 2) & (dst < H + 2), 2 * (dst - 2), none)
    above = jnp.where(dst < 2, 64 + 2 * (H - 2 + dst), none)
    below = jnp.where((dst >= H + 2) & (dst < H + 4), 64 + 2 * (dst - H - 2), none)
    corner = jnp.where(up, above, below)
    past = jnp.where(up, 0, H + 2)
    first_col = jnp.where(left, 0, W - 2)
    for f in range(F):
        pick = (src == jnp.maximum(body, corner) + f * 32 + col).astype(F32).astype(BF)
        theirs = jnp.dot(halo[4], pick, preferred_element_type=F32)
        theirs = norm_silu(jnp.where(exists, theirs, 0.0), gain)
        picks = [(src == body + f * 32 + col).astype(F32).astype(BF)]
        for r in range(2):
            picks.append(((src == first_col + col) & (dst == past + r)).astype(F32).astype(BF))
        mine = jnp.concatenate([record[base + 4], halo[2 * f], halo[2 * f + 1]], axis=1)
        ours = jnp.dot(mine, jnp.concatenate(picks, axis=0), preferred_element_type=F32)
        ours = norm_silu(jnp.where(exists, ours, 0.0), gain)
        low, high = jnp.where(left, theirs, ours), jnp.where(left, ours, theirs)
        for k in range(4):
            put_column(columns, f, k, (low if k < 2 else high)[:, (k % 2) * W : (k % 2 + 1) * W])
        near = jnp.where(left, theirs[:, W:], theirs[:, :W])
        for r in range(4):
            other, self = halo[2 * f + r % 2], record[base + 2 * f + r % 2]
            raw = jnp.where(up, other if r < 2 else self, self if r < 2 else other)
            at = jnp.where(up, r, H + r)
            moved = rotate(near, jnp.where(left, (W - at) % W, W - 1 - at))
            center = norm_silu(jnp.where(exists, raw.astype(F32), 0.0), gain)
            put_window(
                band, (f, r), three_shifts(center, jnp.where(left, moved, 0.0), jnp.where(left, 0.0, moved))
            )

def own_border_kernel(table, record, halo, vectors, _, band, columns):
    border_windows(table, vectors, record, 0, halo, True, band, columns)


def outer_kernel(
    table, inner, band0, columns0, second_own, second_prev, halo2, halo1, weights, vectors,
    out, band1, columns1, bandp, columnsp, band2, columns2
):
    up, left = sides(table)
    bias1, gain2 = vectors[:, 0:1], vectors[:, 2:3]
    lane = lanes(C)
    first_col = jnp.where(left, 0, W - 2)
    border_windows(table, vectors, second_own, F * H, halo1, table[1] >= 1, band1, columns1)
    border_windows(table, vectors, second_prev, F * H, halo2, table[1] >= 2, bandp, columnsp)
    frames = [(b, c, f) for b, c in ((bandp, columnsp), (band1, columns1), (band0, columns0)) for f in range(F)]

    inside = (lane >= jnp.where(up, 3, 2)) & (lane < jnp.where(up, H + 2, H + 1))
    row_at, col_at = jnp.where(up, 0, 2), jnp.where(left, 0, 2)
    for p in range(2):
        acc = product(weights.at[0], band_parts(frames[F * p : F * p + 2 * F]))
        for f in range(F):
            s = F * p + f
            value = norm_silu(acc[f * C : (f + 1) * C] + bias1, gain2)
            if p == 0:
                value = jnp.where(table[1] > 0, value, 0.0)
            beside = [value[:, 2 * W : 3 * W], value[:, 3 * W :]]
            near = jnp.where(left, beside[0], beside[1])
            for j in range(2):
                at = jnp.where(up, 1 + j, H + 1 + j)
                moved = rotate(near, jnp.where(left, W - at, W - 1 - at))
                center = value[:, j * W : (j + 1) * W]
                put_window(
                    band2,
                    (s, row_at + j),
                    three_shifts(center, jnp.where(left, moved, 0.0), jnp.where(left, 0.0, moved)),
                )
                band2[s, 2 - row_at + j] = jnp.zeros((3 * C, W), BF)
                put_column(columns2, s, col_at + j, jnp.where(inside, beside[j], 0.0))
                columns2[s, 2 - col_at + j] = jnp.zeros((3, C, W), BF)

    length = table[T_CLIP + table[T_LIST + table[0]] // TPC]
    start = table[1] * F
    acc = product(weights.at[1], band_parts([(band2, columns2, s) for s in range(2 * F)]))
    for f in range(F):
        value = acc[f * C : (f + 1) * C]
        for y in range(H):
            total = inner[f, y]
            for j in range(2):
                at = first_col + j
                moved = rotate(value[:, (2 + j) * W : (3 + j) * W], (at + W - 2 - y) % W)
                total = total + jnp.where(lane == at, moved, 0.0)
            if y < 2:
                total = total + jnp.where(up, value[:, y * W : (y + 1) * W], 0.0)
            if y >= H - 2:
                j = y - (H - 2)
                total = total + jnp.where(up, 0.0, value[:, j * W : (j + 1) * W])
            out[f, y] = jnp.where(start + f < length, total, 0.0).astype(BF)


def call(kernel, outs, kinds, scratch=(), mib=8, flops=0):
    single = not isinstance(outs, (list, tuple))
    return pl.pallas_call(
        kernel,
        out_shape=outs,
        in_specs=[{"s": SMEM, "v": VMEM, "-": ANY}[kind] for kind in kinds],
        out_specs=VMEM if single else [VMEM] * len(outs),
        scratch_shapes=list(scratch),
        compiler_params=params(mib),
        cost_estimate=pl.CostEstimate(flops=flops, bytes_accessed=2**20, transcendentals=0),
    )


def shape(*extent):
    return jax.ShapeDtypeStruct(extent, BF)


def place_of(z, y, c):
    return (z % NZ) * NY * NCORE + (y % NY) * NCORE + c


def pairs(move):
    return [
        (place_of(z, y, c), place_of(*move(z, y, c))) for z in range(NZ) for y in range(NY) for c in range(NCORE)
    ]


def send(array, move):
    return lax.ppermute(array, "tile", pairs(move))


def later(array, by=1):
    return lax.ppermute(array, "group", [(i, (i + by) % NX) for i in range(NX)])


def spread(record):
    along = lambda by: lambda z, y, c: (z + (by if c == 0 else -by), y, c)
    t0 = jnp.stack([record, send(record, swap)])
    t1 = send(t0, along(1))
    t2 = send(t0, along(2))
    t3 = send(jnp.concatenate([t2[:1], t1], axis=0), along(2))
    return t0, t1, t2, t3


def swap(z, y, c):
    return z, y, 1 - c


def deliver(table, plan, held, after):
    other = call(functools.partial(select_kernel, NY), shape(NY, REC, C, W), "svvvv-")(plan, *held, after)
    arrived = send(other, swap)
    mine = call(functools.partial(select_kernel, 0), shape(NY, REC, C, W), "svvvv-")(plan, *held, other)
    own, one, two, three = call(combine_kernel, [shape(REC, C, W)] * 4, "svv")(table, mine, arrived)
    total = own.astype(F32)
    for by, part in ((2, two), (1, one), (3, three)):
        total = total + send(part, lambda z, y, c, by=by: (z, y + by, c)).astype(F32)
    return total.astype(BF)


def per_device(
    features, tile_list, neighbours, clip_frames, gain_one, weight_one, bias_one, gain_two, weight_two, bias_two
):
    ids = jnp.stack([lax.axis_index("tile"), lax.axis_index("group")]).astype(jnp.int32)
    table = jnp.concatenate(
        [
            ids,
            tile_list,
            neighbours.reshape(-1),
            clip_frames,
        ]
    )
    vectors = jnp.stack([bias_one, gain_one, gain_two, bias_two], axis=1)
    own = features[0].transpose(0, 2, 1, 3)
    prev = later(own)
    record, packed = call(record_kernel, [shape(REC, C, W), shape(4 * F + 1, C // 2, W)], "sssv")(ids, tile_list, neighbours.T, own)
    held = spread(packed)
    weights = call(weights_kernel, shape(2, 2 * C, 4 * KF), "vv-", mib=16)(
        weight_one.reshape(3, 9 * C, C), weight_two.reshape(3, 9 * C, C), held[0]
    )
    plan = pl.pallas_call(
        plan_kernel,
        out_shape=jax.ShapeDtypeStruct((12 * NY,), jnp.int32),
        in_specs=[SMEM, ANY],
        out_specs=SMEM,
        scratch_shapes=[pltpu.SMEM((TILES,), jnp.int32)],
    )(table, held[0])
    scratch = [pltpu.VMEM((F, H + 2, 3 * C, W), BF)]
    own_one = call(
        own_first_kernel, jax.ShapeDtypeStruct((H // 2, 2 * C, 2 * W), F32), "vvv", scratch, 16, 3 * 10**9
    )(own, weights, vectors)
    second = call(
        inner_first_kernel, shape(F * H + REC, C, W), "svvvv-s", scratch, 16, 8 * 10**9
    )(table, prev, own_one, weights, vectors, held[1], plan)
    whole = jax.ShapeDtypeStruct((F, H, C, W), F32)
    own_two = call(own_second_kernel, whole, "vvvv", scratch, 16, 10**9)(own, second, weights, vectors)
    second_prev = later(second)
    halo = deliver(table, plan, held, second)
    halo1, halo2 = later(halo), later(halo, 2)
    inner = call(inner_second_kernel, whole, "svvv-", scratch, 16, 12 * 10**9)(
        table, own_two, second_prev, weights, halo
    )
    edges = [shape(F, 4, 3 * C, W), shape(F, 4, 3, C, W)]
    border0 = call(own_border_kernel, edges, "svvv-")(table, record, halo, vectors, inner)
    out = call(
        outer_kernel,
        shape(F, H, C, W),
        "s" + "v" * 9,
        [pltpu.VMEM(edge.shape, BF) for edge in edges] * 2
        + [pltpu.VMEM((2 * F, 4, 3 * C, W), BF), pltpu.VMEM((2 * F, 4, 3, C, W), BF)],
        24,
        4 * 10**9,
    )(table, inner, *border0, second, second_prev, halo2, halo1, weights, vectors)
    return out.transpose(0, 2, 1, 3)[None]


def solution(mesh):
    placed = (P("tile", "group", None, None, None), P(), P(), P(), P(), P(), P(), P(), P(), P())
    return jax.shard_map(
        per_device,
        mesh=mesh,
        in_specs=placed,
        out_specs=P("tile", "group", None, None, None),
        check_vma=False,
    )
```
